768 devices in a mesh: win: 96 (over y, x, z_hi), head: 8 (over z_lo, core).
Axes of the slice: x: 4, y: 8, z: 12 (z_hi: 3, z_lo: 4; z = z_hi * 4 + z_lo), core: 2. Of those that a mesh axis runs over, the one named last changes fastest.
Arguments:
- block_input: bfloat16 [55296, 512], P('win'), may hold values from -40 to 40
- stream: bfloat16 [55296, 512], P('win'), may hold values from -6 to 6
- grad_out: bfloat16 [55296, 512], P('win'), may hold values from -6 to 6
- regions: int32 [55296], P('win'), may hold values from 0 to 2
- qkv_weight: bfloat16 [3, 512, 512], P(None, None, 'head'), may hold values from -12 to 12
- out_weight: bfloat16 [512, 512], P('head'), may hold values from -0.25 to 0.25
- up_weight: bfloat16 [512, 2048], P(None, 'head'), may hold values from -0.25 to 0.25
- down_weight: bfloat16 [2048, 512], P('head'), may hold values from -0.125 to 0.125
Outputs:
- grad_input: bfloat16 [55296, 512], P(('win', 'head'))
- weight_grads: float32 [8, 393216], P('head', 'win')
The draws below stay inside these ranges and needn't reach their ends.
All inputs are finite; a program needn't handle non-finite values.
Results may differ from the reference program's by a relative error of at most 0.018.
The reference program's roundings to bfloat16 on the way (of `act`, `pre_grad`, `grad_mid`, `attended_grad` and `score_grad`) count: a program that leaves them out, or rounds other values in their place, can miss the bound.
Values may be sent and summed in bfloat16 or wider, within the bound.
No kernel may reach another device: no remote copies, remote signals or barrier semaphores. Data moves between devices by JAX's collectives and lax.ppermute only.
A program may use at most 32 MiB of HBM per device.

```python
from functools import partial
import jax
import jax.numpy as jnp
from jax import lax

D = 512
HEADS = 8
HS = 64
FF = 2048
WIN = 144
HALF = 72
TOKENS = 55296
N_HEAD = 8


def draw_block_input(key, part):
    key = jax.random.fold_in(key, 11)
    first = jax.random.fold_in(key, 0)
    third = jax.random.fold_in(key, 2)
    base = jnp.clip(jax.random.normal(first, (TOKENS, D), jnp.float32), -5.0, 5.0)
    scales = jnp.exp(jax.random.uniform(third, (TOKENS, 1), jnp.float32, jnp.log(0.5), jnp.log(2.0)))
    return (base * scales).astype(jnp.bfloat16)


def draw_qkv_weight(key, part):
    key = jax.random.fold_in(key, 12)
    first = jax.random.fold_in(key, 0)
    base = jnp.clip(jax.random.normal(first, (3, D, HEADS * HS), jnp.float32), -4.0, 4.0) * D ** (-0.5)
    return base.astype(jnp.bfloat16)


def with_ends(drawn, own_key, smallest, top_value):
    longest = drawn.shape.index(max(drawn.shape))
    spots = []
    for shift in (0, 1):
        where = [jax.random.randint(jax.random.fold_in(own_key, axis), (), 0, length) for axis, length in enumerate(drawn.shape)]
        where[longest] = (where[longest] + shift) % drawn.shape[longest]
        spots.append(tuple(where))
    return drawn.at[spots[0]].set(smallest).at[spots[1]].set(top_value)


def levels(rng, dims, cuts, least, high):
    level, own = 1.0, jax.random.fold_in(rng, 6)
    for dim, blocks in cuts:
        steps = jnp.exp(jax.random.uniform(jax.random.fold_in(own, dim), (blocks,), jnp.float32, least / len(cuts), high / len(cuts)))
        level = level * jnp.repeat(steps, dims[dim] // blocks).reshape([-1 if axis == dim else 1 for axis in range(len(dims))])
    return level


def scatter_about(stream_key, extent, deviation, bound, pieces=(), dtype=jnp.bfloat16):
    entries = deviation * jax.random.normal(stream_key, extent, jnp.float32)
    if pieces:
        entries = entries * levels(stream_key, extent, pieces, -0.22, 0.18)
    return jnp.clip(entries, -bound, bound).astype(dtype)


def setup_inputs(seed: int = 0) -> dict:
    splits = jax.random.split(jax.random.key(seed), 9)
    return {
        "block_input": draw_block_input(jax.random.fold_in(splits[8], 71), 0),
        "stream": scatter_about(splits[1], (TOKENS, D), 1.0, 6.0, ((0, 96),)),
        "grad_out": scatter_about(splits[2], (TOKENS, D), 1.0, 6.0, ((0, 96),)),
        "regions": with_ends(jax.random.randint(splits[3], (TOKENS,), 0, 3), jax.random.fold_in(splits[3], 1), 0, 2).astype(jnp.int32),
        "qkv_weight": draw_qkv_weight(jax.random.fold_in(splits[8], 71), 0),
        "out_weight": scatter_about(splits[5], (HEADS * HS, D), (HEADS * HS) ** -0.5, 0.25, ((0, 8),)),
        "up_weight": scatter_about(splits[6], (D, FF), D ** -0.5, 0.25, ((1, 8),)),
        "down_weight": scatter_about(splits[7], (FF, D), FF ** -0.5, 0.125, ((0, 8),)),
    }


epsilon = 1e-05

def normalize(values):
    data_f = values.astype(jnp.float32)
    centred = data_f - lax.optimization_barrier(jnp.mean(data_f, axis=-1, keepdims=True))
    factor = lax.rsqrt(lax.optimization_barrier(jnp.mean(centred * centred, axis=-1, keepdims=True)) + epsilon)
    return (centred * factor, factor)

def norm_back(normed, factor, upper):
    inner = upper - lax.optimization_barrier(jnp.mean(upper, axis=-1, keepdims=True))
    return factor * (inner - normed * lax.optimization_barrier(jnp.mean(upper * normed, axis=-1, keepdims=True)))

def contract_rows(left, right):
    return lax.dot_general(left, right, (((0,), (0,)), ((), ())), preferred_element_type=jnp.float32)

def contract_cols(left, right):
    return lax.dot_general(left, right, (((1,), (1,)), ((), ())), preferred_element_type=jnp.float32)

def mlp_back(stream, grad_out, up_weight, down_weight):
    normed, factor = normalize(stream)
    unit = normed.astype(jnp.bfloat16)
    pre = jnp.dot(unit, up_weight, preferred_element_type=jnp.float32)
    act, pull = jax.vjp(partial(jax.nn.gelu, approximate=True), pre)
    act_b = act.astype(jnp.bfloat16)
    upper = contract_cols(grad_out, down_weight)
    pre_grad = pull(upper)[0].astype(jnp.bfloat16)
    down_grad = contract_rows(act_b, grad_out)
    up_grad = contract_rows(unit, pre_grad)
    unit_grad = contract_cols(pre_grad, up_weight)
    return (normed, factor, up_grad, down_grad, unit_grad)

def attend_back(shifted_in, shifted_grad, regions, qkv_weight, out_weight, width, head_size):
    row_count = shifted_in.shape[0]
    windows = row_count // width
    columns = qkv_weight.shape[2]
    heads = columns // head_size
    scaling = head_size ** (-0.5)
    proj = jnp.einsum('td,idc->itc', shifted_in.astype(jnp.float32), qkv_weight.astype(jnp.float32)).astype(jnp.bfloat16)
    proj = proj.reshape(3, windows, width, heads, head_size)
    query, keys, value = (proj[0], proj[1], proj[2])
    scores = jnp.einsum('wqhe,wkhe->whqk', query.astype(jnp.float32), keys.astype(jnp.float32)) * scaling
    labels = regions.reshape(windows, width)
    same = labels[:, None, :, None] == labels[:, None, None, :]
    kept = jnp.where(same, scores, -jnp.inf)
    highest = lax.optimization_barrier(jnp.max(kept, axis=-1, keepdims=True))
    raised = jnp.exp(kept - highest)
    probs = raised / lax.optimization_barrier(jnp.sum(raised, axis=-1, keepdims=True))
    probs_b = probs.astype(jnp.bfloat16)
    attended = jnp.einsum('whqk,wkhe->wqhe', probs_b.astype(jnp.float32), value.astype(jnp.float32)).astype(jnp.bfloat16)
    out_grad = contract_rows(attended.reshape(row_count, columns), shifted_grad)
    attended_grad = contract_cols(shifted_grad, out_weight).astype(jnp.bfloat16).reshape(windows, width, heads, head_size)
    prob_grad = jnp.einsum('wqhe,wkhe->whqk', attended_grad.astype(jnp.float32), value.astype(jnp.float32))
    score_grad = (probs * (prob_grad - lax.optimization_barrier(jnp.sum(prob_grad * probs, axis=-1, keepdims=True))) * scaling).astype(jnp.bfloat16)
    value_grad = jnp.einsum('whqk,wqhe->wkhe', probs_b.astype(jnp.float32), attended_grad.astype(jnp.float32)).astype(jnp.bfloat16)
    query_grad = jnp.einsum('whqk,wkhe->wqhe', score_grad.astype(jnp.float32), keys.astype(jnp.float32)).astype(jnp.bfloat16)
    key_grad = jnp.einsum('whqk,wqhe->wkhe', score_grad.astype(jnp.float32), query.astype(jnp.float32)).astype(jnp.bfloat16)
    stacked = jnp.stack([query_grad, key_grad, value_grad]).reshape(3, row_count, columns)
    qkv_grad = jnp.einsum('td,itc->idc', shifted_in.astype(jnp.float32), stacked.astype(jnp.float32))
    in_grad = jnp.einsum('itc,idc->td', stacked.astype(jnp.float32), qkv_weight.astype(jnp.float32))
    return (qkv_grad, out_grad, in_grad)

def reference(block_input, stream, grad_out, regions, qkv_weight, out_weight, up_weight, down_weight):
    normed_in, factor_in = normalize(block_input)
    hidden = normed_in.astype(jnp.bfloat16)
    normed_mid, factor_mid, up_grad, down_grad, unit_grad = mlp_back(stream, grad_out, up_weight, down_weight)
    middle = grad_out.astype(jnp.float32) + norm_back(normed_mid, factor_mid, unit_grad)
    grad_mid = middle.astype(jnp.bfloat16)
    shifted_in = jnp.roll(hidden, -HALF, axis=0)
    shifted_grad = jnp.roll(grad_mid, -HALF, axis=0)
    qkv_grad, out_grad, in_grad = attend_back(shifted_in, shifted_grad, regions, qkv_weight, out_weight, WIN, HS)
    hidden_grad = jnp.roll(in_grad, HALF, axis=0)
    grad_input = (middle + norm_back(normed_in, factor_in, hidden_grad)).astype(jnp.bfloat16)
    per_head = HEADS // N_HEAD * HS
    per_unit = FF // N_HEAD
    flat_rows = []
    for head_slot in range(N_HEAD):
        flat_rows.append(jnp.concatenate([qkv_grad[:, :, head_slot * per_head:(head_slot + 1) * per_head].reshape(-1), out_grad[head_slot * per_head:(head_slot + 1) * per_head].reshape(-1), up_grad[:, head_slot * per_unit:(head_slot + 1) * per_unit].reshape(-1), down_grad[head_slot * per_unit:(head_slot + 1) * per_unit].reshape(-1)]))
    return (grad_input, jnp.stack(flat_rows))
```

```python
from functools import partial

import jax
import jax.numpy as jnp
from jax import lax
from jax.sharding import Mesh, PartitionSpec as P

HS = 64
WIN = 144
HALF = 72


epsilon = 1e-05


WIN_AXES = ("y", "x", "zh")
HEAD_AXES = ("zl", "core")


def shifted(block, axis, distance):
    devices = range(lax.axis_size(axis))
    route = [((i - distance) % len(devices), i) for i in devices]
    return lax.ppermute(block, axis, route)


def exchange(pieces, axis):
    received = lax.all_to_all(pieces.astype(jnp.bfloat16), axis, 0, 0)
    return jnp.sum(received.astype(jnp.float32), axis=0)


def normalize(values):
    data_f = values.astype(jnp.float32)
    centred = data_f - jnp.mean(data_f, axis=-1, keepdims=True)
    factor = lax.rsqrt(jnp.mean(centred * centred, axis=-1, keepdims=True) + epsilon)
    return (centred * factor, factor)


def norm_back(normed, factor, upper):
    inner = upper - jnp.mean(upper, axis=-1, keepdims=True)
    return factor * (inner - normed * jnp.mean(upper * normed, axis=-1, keepdims=True))


def contract_rows(left, right):
    return lax.dot_general(
        left, right, (((0,), (0,)), ((), ())), preferred_element_type=jnp.float32
    )


def contract_cols(left, right):
    return lax.dot_general(
        left, right, (((1,), (1,)), ((), ())), preferred_element_type=jnp.float32
    )


def mlp_back(stream, grad_out, up_weight, down_weight):
    normed, factor = normalize(stream)
    unit = normed.astype(jnp.bfloat16)
    pre = jnp.dot(unit, up_weight, preferred_element_type=jnp.float32)
    act, pull = jax.vjp(partial(jax.nn.gelu, approximate=True), pre)
    act_b = act.astype(jnp.bfloat16)
    upper = contract_cols(grad_out, down_weight)
    pre_grad = pull(upper)[0].astype(jnp.bfloat16)
    down_grad = contract_rows(act_b, grad_out)
    up_grad = contract_rows(unit, pre_grad)
    unit_grad = contract_cols(pre_grad, up_weight)
    return (normed, factor, up_grad, down_grad, unit_grad)


def attend_back(shifted_in, shifted_grad, regions, qkv_weight, out_weight, width, head_size):
    row_count = shifted_in.shape[0]
    windows = row_count // width
    columns = qkv_weight.shape[2]
    heads = columns // head_size
    scaling = head_size ** (-0.5)
    proj = jnp.einsum(
        "td,idc->itc", shifted_in, qkv_weight, preferred_element_type=jnp.float32
    ).astype(jnp.bfloat16)
    proj = proj.reshape(3, windows, width, heads, head_size)
    query, keys, value = (proj[0], proj[1], proj[2])
    scores = (
        jnp.einsum("wqhe,wkhe->whqk", query, keys, preferred_element_type=jnp.float32) * scaling
    )
    labels = regions.reshape(windows, width)
    same = labels[:, None, :, None] == labels[:, None, None, :]
    kept = jnp.where(same, scores, -jnp.inf)
    highest = jnp.max(kept, axis=-1, keepdims=True)
    raised = jnp.exp(kept - highest)
    probs = raised / jnp.sum(raised, axis=-1, keepdims=True)
    probs_b = probs.astype(jnp.bfloat16)
    attended = jnp.einsum(
        "whqk,wkhe->wqhe", probs_b, value, preferred_element_type=jnp.float32
    ).astype(jnp.bfloat16)
    out_grad = contract_rows(attended.reshape(row_count, columns), shifted_grad)
    attended_grad = (
        contract_cols(shifted_grad, out_weight)
        .astype(jnp.bfloat16)
        .reshape(windows, width, heads, head_size)
    )
    prob_grad = jnp.einsum(
        "wqhe,wkhe->whqk", attended_grad, value, preferred_element_type=jnp.float32
    )
    score_grad = (
        probs * (prob_grad - jnp.sum(prob_grad * probs, axis=-1, keepdims=True)) * scaling
    ).astype(jnp.bfloat16)
    value_grad = jnp.einsum(
        "whqk,wqhe->wkhe", probs_b, attended_grad, preferred_element_type=jnp.float32
    ).astype(jnp.bfloat16)
    query_grad = jnp.einsum(
        "whqk,wkhe->wqhe", score_grad, keys, preferred_element_type=jnp.float32
    ).astype(jnp.bfloat16)
    key_grad = jnp.einsum(
        "whqk,wqhe->wkhe", score_grad, query, preferred_element_type=jnp.float32
    ).astype(jnp.bfloat16)
    stacked = jnp.stack([query_grad, key_grad, value_grad]).reshape(3, row_count, columns)
    qkv_grad = jnp.einsum("td,itc->idc", shifted_in, stacked, preferred_element_type=jnp.float32)
    in_grad = jnp.einsum("itc,idc->td", stacked, qkv_weight, preferred_element_type=jnp.float32)
    return (qkv_grad, out_grad, in_grad)


def shards(block_input, stream, grad_out, regions, qkv_weight, out_weight, up_weight, down_weight):
    row_count = block_input.shape[0]
    width = block_input.shape[1]
    y_count, x_count, z_count = [lax.axis_size(axis) for axis in WIN_AXES]
    head_count = lax.axis_size(HEAD_AXES)
    share_rows = row_count // head_count
    share_start = lax.axis_index(HEAD_AXES) * share_rows

    def share(values):
        return lax.dynamic_slice_in_dim(values, share_start, share_rows, 0)

    normed_in, factor_in = normalize(block_input)
    hidden = normed_in.astype(jnp.bfloat16)
    far_hidden = shifted(hidden[:HALF], WIN_AXES, -1)
    normed_mid, factor_mid, up_grad, down_grad, unit_grad = mlp_back(
        stream, grad_out, up_weight, down_weight
    )
    summed = exchange(unit_grad.reshape(head_count, share_rows, width), HEAD_AXES)
    own_mid, own_mid_factor = normalize(share(stream))
    mid_share = share(grad_out).astype(jnp.float32) + norm_back(own_mid, own_mid_factor, summed)
    grad_mid = lax.all_gather(mid_share.astype(jnp.bfloat16), HEAD_AXES, axis=0, tiled=True)
    far_grad = shifted(grad_mid[:HALF], WIN_AXES, -1)
    shifted_in = jnp.concatenate([hidden[HALF:], far_hidden], 0)
    shifted_grad = jnp.concatenate([grad_mid[HALF:], far_grad], 0)
    qkv_grad, out_grad, in_grad = attend_back(
        shifted_in, shifted_grad, regions, qkv_weight, out_weight, WIN, HS
    )
    in_grad = in_grad.astype(jnp.bfloat16)
    returned = shifted(in_grad[row_count - HALF :], WIN_AXES, 1)
    flattened = jnp.concatenate(
        [qkv_grad.reshape(-1), out_grad.reshape(-1), up_grad.reshape(-1), down_grad.reshape(-1)]
    ).astype(jnp.bfloat16)
    pieces = flattened.reshape(y_count, x_count, z_count, -1, 128).transpose(1, 0, 2, 3, 4)
    partial_sum = exchange(pieces, "x")
    owned = exchange(partial_sum.reshape(y_count * z_count, -1, 128), ("y", "zh"))
    plain_grad = jnp.concatenate([returned, in_grad[: row_count - HALF]], 0)
    own_grad = exchange(plain_grad.reshape(head_count, share_rows, width), HEAD_AXES)
    own_in, own_in_factor = normalize(share(block_input))
    grad_input = (mid_share + norm_back(own_in, own_in_factor, own_grad)).astype(jnp.bfloat16)
    return (grad_input, owned.reshape(1, -1))


def solution(mesh):
    fine = Mesh(mesh.devices.reshape(8, 4, 3, 4, 2), WIN_AXES + HEAD_AXES)
    return jax.shard_map(
        shards,
        mesh=fine,
        in_specs=(
            P(WIN_AXES, None),
            P(WIN_AXES, None),
            P(WIN_AXES, None),
            P(WIN_AXES),
            P(None, None, HEAD_AXES),
            P(HEAD_AXES, None),
            P(None, HEAD_AXES),
            P(HEAD_AXES, None),
        ),
        out_specs=(P(WIN_AXES + HEAD_AXES, None), P(HEAD_AXES, WIN_AXES)),
        check_vma=False,
    )
```

```python
import jax
import jax.numpy as jnp
from jax import lax
from jax.experimental import pallas as pl
from jax.experimental.pallas import tpu as pltpu
from jax.sharding import Mesh, PartitionSpec as P

HS = 64
WIN = 144
HALF = 72
WIN_AXES = ("y", "x", "zh")
HEAD_AXES = ("zl", "core")
BLOCK = (32, 128)
EPSILON = 1e-05
BF = jnp.bfloat16
F32 = jnp.float32


def normalize(values):
    data_f = values.astype(F32)
    centred = data_f - jnp.mean(data_f, axis=-1, keepdims=True)
    factor = lax.rsqrt(jnp.mean(centred * centred, axis=-1, keepdims=True) + EPSILON)
    return (centred * factor, factor)


def norm_back(normed, factor, upper):
    inner = upper - jnp.mean(upper, axis=-1, keepdims=True)
    return factor * (inner - normed * jnp.mean(upper * normed, axis=-1, keepdims=True))


def dot(left, right):
    return lax.dot_general(left, right, (((1,), (0,)), ((), ())), preferred_element_type=F32)


def contract_rows(left, right):
    return lax.dot_general(left, right, (((0,), (0,)), ((), ())), preferred_element_type=F32)


def contract_cols(left, right):
    return lax.dot_general(left, right, (((1,), (1,)), ((), ())), preferred_element_type=F32)


def call(kernel, outs, args, scratch=(), flops=10**8, scalars=0):
    vmem = pl.BlockSpec(memory_space=pltpu.VMEM)
    smem = pl.BlockSpec(memory_space=pltpu.SMEM)
    size = sum(a.size * a.dtype.itemsize for a in args)
    return pl.pallas_call(
        kernel,
        out_shape=[jax.ShapeDtypeStruct(shape, dtype) for shape, dtype in outs],
        in_specs=[smem] * scalars + [vmem] * (len(args) - scalars),
        out_specs=[vmem] * len(outs),
        scratch_shapes=list(scratch),
        compiler_params=pltpu.CompilerParams(vmem_limit_bytes=40 * 2**20),
        cost_estimate=pl.CostEstimate(flops=flops, bytes_accessed=2 * size, transcendentals=0),
    )(*args)


def mlp_kernel(stream, grad_out, up_weight, down_weight, unit_grad, unit_out, act_out, pre_out):
    rows = stream.shape[0]
    for start in range(0, rows, WIN):
        part = pl.ds(start, WIN)
        unit = normalize(stream[part, :])[0].astype(BF)
        pre = dot(unit, up_weight[...])
        upper = contract_cols(grad_out[part, :], down_weight[...])
        scale = 0.7978845608028654
        square = pre * pre
        bent = jnp.tanh(scale * (pre + 0.044715 * (square * pre)))
        act = 0.5 * pre * (1.0 + bent)
        slope = 0.5 * (1.0 + bent) + 0.5 * pre * (1.0 - bent * bent) * (
            scale * (1.0 + 3 * 0.044715 * square)
        )
        pre_grad = (upper * slope).astype(BF)
        unit_out[part, :] = unit
        act_out[part, :] = act.astype(BF)
        pre_out[part, :] = pre_grad
        grad = contract_cols(pre_grad, up_weight[...])
        first = start // HALF
        unit_grad[first] = grad[:HALF].astype(BF)
        unit_grad[first + 1] = grad[HALF:].astype(BF)


def forward_kernel(
    block_input, far_input, labels_col, labels_row, qkv_weight, unit, act, pre_grad, grad_out,
    shifted_in, query_out, key_out, value_out, probs_out, attended_out, early, late, rows_f32,
):
    near = normalize(block_input[...])[0]
    far = normalize(far_input[...])[0]
    windows = block_input.shape[0] // WIN
    for index in range(windows):
        start = HALF + WIN * index
        if index < windows - 1:
            piece = near[start : start + WIN]
        else:
            piece = jnp.concatenate([near[start:], far], axis=0)
        inputs = piece.astype(BF)
        shifted_in[index] = inputs
        query, key, value = [dot(inputs, qkv_weight[i]).astype(BF) for i in range(3)]
        query_out[index] = query
        key_out[index] = key
        value_out[index] = value
        scores = contract_cols(query, key) * HS**-0.5
        kept = jnp.where(labels_col[index] == labels_row[index], scores, -jnp.inf)
        raised = jnp.exp(kept - jnp.max(kept, axis=-1, keepdims=True))
        probs = raised / jnp.sum(raised, axis=-1, keepdims=True)
        probs_out[index] = probs
        attended_out[index] = dot(probs.astype(BF), value).astype(BF)
    up_grad = contract_rows(unit[...], pre_grad[...])
    ups, wide = up_grad.shape[0], up_grad.shape[1] // 128
    for column in range(wide):
        rows_f32[pl.ds(column, ups, stride=wide), :] = up_grad[:, 128 * column : 128 * column + 128]
    down_grad = contract_rows(act[...], grad_out[...])
    downs, wide = down_grad.shape[0], down_grad.shape[1] // 128
    base = ups * up_grad.shape[1] // 128
    for column in range(wide):
        rows_f32[pl.ds(base + column, downs, stride=wide), :] = down_grad[
            :, 128 * column : 128 * column + 128
        ]
    for owner in range(32, 96):
        block = rows_f32[32 * (owner - 32) : 32 * (owner - 31), :].astype(BF)
        if owner < 36:
            early[owner - 32] = block
        else:
            late[owner % 12 // 3, owner // 12 * 3 + owner % 3 - 9] = block


def middle_kernel(parts, stream, grad_out, mid, grad_mid):
    summed = jnp.sum(parts[...].astype(F32), axis=0)
    normed, factor = normalize(stream[...])
    middle = grad_out[...].astype(F32) + norm_back(normed, factor, summed)
    mid[...] = middle
    grad_mid[...] = middle.astype(BF)


def backward_kernel(
    place, mine, theirs, shifted_in, query_in, key_in, value_in, probs_in, attended,
    qkv_weight, out_weight, early, keep, give, pieces, grads, outs,
):
    chip, core = place[0], place[1]
    windows = shifted_in.shape[0]

    def where(chunk):
        head = (chunk + 1) % 8
        return lax.rem(head // 2 - chip + 4, 4), head % 2

    def load(chunk):
        slot, owner = where(chunk)
        return jnp.where(core == owner, mine[slot].astype(F32), theirs[slot].astype(F32))

    def store(chunk, value):
        slot, owner = where(chunk)

        @pl.when(core == owner)
        def _():
            keep[slot] = value

        @pl.when(core != owner)
        def _():
            give[slot] = value

    totals = [0.0, 0.0, 0.0]
    out_grad = 0.0
    for index in range(windows):
        upper = jnp.concatenate([load(2 * index), load(2 * index + 1)], axis=0).astype(BF)
        query, key, value = query_in[index], key_in[index], value_in[index]
        probs = probs_in[index]
        attended_grad = contract_cols(upper, out_weight[...]).astype(BF)
        out_grad = out_grad + contract_rows(attended[index], upper)
        prob_grad = contract_cols(attended_grad, value)
        inner = prob_grad - jnp.sum(prob_grad * probs, axis=-1, keepdims=True)
        score_grad = (probs * inner * HS**-0.5).astype(BF)
        grads_b = [
            dot(score_grad, key).astype(BF),
            contract_rows(score_grad, query).astype(BF),
            contract_rows(probs.astype(BF), attended_grad).astype(BF),
        ]
        in_grad = sum(contract_cols(grads_b[i], qkv_weight[i]) for i in range(3)).astype(F32)
        store(2 * index, in_grad[:HALF].astype(BF))
        store(2 * index + 1, in_grad[HALF:].astype(BF))
        for i in range(3):
            totals[i] = totals[i] + contract_rows(shifted_in[index], grads_b[i])
    half = grads.shape[1] // 2
    for i in range(3):
        grads[i] = totals[i]
    for column in range(out_grad.shape[1] // 128):
        outs[pl.ds(column, HS, stride=4), :] = out_grad[:, 128 * column : 128 * column + 128]
    for owner in range(36):
        if owner < 24:
            kind, first = owner // 8, owner % 8 * 64
            even = grads[kind, pl.ds(first, 32, stride=2), :]
            odd = grads[kind, pl.ds(first + 1, 32, stride=2), :]
            block = jnp.concatenate([even, odd], axis=1).astype(BF)
        elif owner < 32:
            block = outs[32 * (owner - 24) : 32 * (owner - 23), :].astype(BF)
        else:
            block = early[owner - 32]
        pieces[owner % 12 // 3, owner // 12 * 3 + owner % 3] = block


def final_kernel(first, second, third, fourth, mid, block_input, grad_input):
    total = (first[...].astype(F32) + second[...].astype(F32)) + (
        third[...].astype(F32) + fourth[...].astype(F32)
    )
    normed, factor = normalize(block_input[...])
    grad_input[...] = (mid[...] + norm_back(normed, factor, total)).astype(BF)


def exchange(pieces, axis):
    received = lax.all_to_all(pieces, axis, 0, 0)
    return jnp.sum(received.astype(F32), axis=0)


def routes(step, back):
    pairs = []
    for win in range(96):
        for chip in range(4):
            for core in range(2):
                goal = (chip + step) % 4
                far = core == 0 and (goal if back else chip) == 0
                if step == 0 and not far:
                    continue
                other = (win + ((1 if back else -1) if far else 0)) % 96
                pairs.append((win * 8 + chip * 2 + core, other * 8 + goal * 2 + core))
    return pairs


def send(value, step, back):
    return lax.ppermute(value, WIN_AXES + HEAD_AXES, routes(step, back))


def shards(block_input, stream, grad_out, regions, qkv_weight, out_weight, up_weight, down_weight):
    rows, width = block_input.shape
    windows = rows // WIN
    head_count = lax.axis_size(HEAD_AXES)
    share_rows = rows // head_count
    share_start = lax.axis_index(HEAD_AXES) * share_rows
    chip, core = lax.axis_index("zl"), lax.axis_index("core")
    at_start = (chip == 0) & (core == 0)
    columns = qkv_weight.shape[2]
    units = up_weight.shape[1]

    def share(values):
        return lax.dynamic_slice_in_dim(values, share_start, share_rows, 0)

    count = lax.axis_size(WIN_AXES)
    far_input = lax.ppermute(
        block_input[:HALF], WIN_AXES, [((i + 1) % count, i) for i in range(count)]
    )
    unit_grad, unit, act, pre_grad = call(
        mlp_kernel,
        [((head_count, share_rows, width), BF), ((rows, width), BF)] + [((rows, units), BF)] * 2,
        (stream, grad_out, up_weight, down_weight),
    )
    parts = lax.all_to_all(unit_grad, HEAD_AXES, 0, 0)
    labels = regions.reshape(windows, WIN)
    per_window = (windows, WIN, columns)
    shifted_in, query, key, value, probs, attended, early, late = call(
        forward_kernel,
        [
            ((windows, WIN, width), BF),
            (per_window, BF),
            (per_window, BF),
            (per_window, BF),
            ((windows, WIN, WIN), F32),
            (per_window, BF),
            ((4,) + BLOCK, BF),
            ((4, 15) + BLOCK, BF),
        ],
        (
            block_input, far_input, labels[:, :, None], labels[:, None, :], qkv_weight,
            unit, act, pre_grad, grad_out,
        ),
        scratch=[pltpu.VMEM((64 * 32, 128), F32)],
    )
    mid, grad_mid = call(
        middle_kernel,
        [((share_rows, width), F32), ((share_rows, width), BF)],
        (parts, share(stream), share(grad_out)),
    )
    late_sum = exchange(late, "x")
    arrived = [send(grad_mid, step, False) for step in range(4)]
    mine = jnp.stack([jnp.where(at_start, arrived[0], grad_mid)] + arrived[:0:-1])
    theirs = lax.ppermute(mine, "core", [(0, 1), (1, 0)])
    keep, give, pieces = call(
        backward_kernel,
        [((4, HALF, width), BF), ((4, HALF, width), BF), ((4, 9) + BLOCK, BF)],
        (
            jnp.stack([chip, core]).astype(jnp.int32), mine, theirs, shifted_in, query, key, value,
            probs, attended, qkv_weight, out_weight, early,
        ),
        scratch=[pltpu.VMEM((3, width, columns), F32), pltpu.VMEM((8 * 32, 128), F32)],
        scalars=1,
    )
    early_sum = exchange(pieces, "x")
    received = lax.ppermute(give, "core", [(0, 1), (1, 0)])
    pair = [(keep[k].astype(F32) + received[k].astype(F32)).astype(BF) for k in range(4)]
    back = [send(pair[step], step, True) for step in range(4)]
    (grad_input,) = call(
        final_kernel,
        [((share_rows, width), BF)],
        (jnp.where(at_start, back[0], pair[0]), *back[1:], mid, share(block_input)),
    )
    partial_sum = jnp.concatenate([early_sum, late_sum], 0).astype(BF)
    owned = exchange(partial_sum, ("y", "zh"))
    return (grad_input, owned.reshape(1, -1))


def solution(mesh):
    fine = Mesh(mesh.devices.reshape(8, 4, 3, 4, 2), WIN_AXES + HEAD_AXES)
    return jax.shard_map(
        shards,
        mesh=fine,
        in_specs=(
            P(WIN_AXES, None),
            P(WIN_AXES, None),
            P(WIN_AXES, None),
            P(WIN_AXES),
            P(None, None, HEAD_AXES),
            P(HEAD_AXES, None),
            P(None, HEAD_AXES),
            P(HEAD_AXES, None),
        ),
        out_specs=(P(WIN_AXES + HEAD_AXES, None), P(HEAD_AXES, WIN_AXES)),
        check_vma=False,
    )
```

```python
import jax
import jax.numpy as jnp
from jax import lax
from jax.experimental import pallas as pl
from jax.experimental.pallas import tpu as pltpu
from jax.sharding import Mesh, PartitionSpec as P

HS = 64
WIN = 144
HALF = 72
WIN_AXES = ("y", "x", "zh")
HEAD_AXES = ("zl", "core")
BLOCK = (32, 128)
EPSILON = 1e-05
BF = jnp.bfloat16
F32 = jnp.float32


def normalize(values):
    data_f = values.astype(F32)
    centred = data_f - jnp.mean(data_f, axis=-1, keepdims=True)
    factor = lax.rsqrt(jnp.mean(centred * centred, axis=-1, keepdims=True) + EPSILON)
    return (centred * factor, factor)


def norm_back(normed, factor, upper):
    inner = upper - jnp.mean(upper, axis=-1, keepdims=True)
    return factor * (inner - normed * jnp.mean(upper * normed, axis=-1, keepdims=True))


def dot(left, right):
    return lax.dot_general(left, right, (((1,), (0,)), ((), ())), preferred_element_type=F32)


def contract_rows(left, right):
    return lax.dot_general(left, right, (((0,), (0,)), ((), ())), preferred_element_type=F32)


def contract_cols(left, right):
    return lax.dot_general(left, right, (((1,), (1,)), ((), ())), preferred_element_type=F32)


def call(kernel, outs, args, scratch=(), flops=10**8, scalars=0, after=()):
    vmem = pl.BlockSpec(memory_space=pltpu.VMEM)
    smem = pl.BlockSpec(memory_space=pltpu.SMEM)
    size = sum(a.size * a.dtype.itemsize for a in args)
    return pl.pallas_call(
        kernel,
        out_shape=[jax.ShapeDtypeStruct(shape, dtype) for shape, dtype in outs],
        in_specs=[smem] * scalars
        + [vmem] * (len(args) - scalars)
        + [pl.BlockSpec(memory_space=pl.ANY)] * len(after),
        out_specs=[vmem] * len(outs),
        scratch_shapes=list(scratch),
        compiler_params=pltpu.CompilerParams(vmem_limit_bytes=40 * 2**20),
        cost_estimate=pl.CostEstimate(flops=flops, bytes_accessed=2 * size, transcendentals=0),
    )(*args, *after)


def mlp_kernel(stream, grad_out, up_weight, down_weight, unit_grad, unit_out, act_out, pre_out):
    unit = normalize(stream[...])[0].astype(BF)
    pre = dot(unit, up_weight[...])
    upper = contract_cols(grad_out[...], down_weight[...])
    scale = 0.7978845608028654
    square = pre * pre
    bent = jnp.tanh(scale * (pre + 0.044715 * (square * pre)))
    slope = 0.5 * (1.0 + bent) + 0.5 * pre * (1.0 - bent * bent) * (
        scale * (1.0 + 3 * 0.044715 * square)
    )
    pre_grad = (upper * slope).astype(BF)
    unit_out[...] = unit
    act_out[...] = (0.5 * pre * (1.0 + bent)).astype(BF)
    pre_out[...] = pre_grad
    grad = contract_cols(pre_grad, up_weight[...])
    unit_grad[0] = grad[:HALF].astype(BF)
    unit_grad[1] = grad[HALF:].astype(BF)


def mlp(stream, grad_out, up_weight, down_weight):
    rows, width = stream.shape
    units = up_weight.shape[1]
    whole = lambda array: pl.BlockSpec(array.shape, lambda i: (0, 0))
    part = lambda columns: pl.BlockSpec((WIN, columns), lambda i: (i, 0))
    return pl.pallas_call(
        mlp_kernel,
        grid=(rows // WIN,),
        out_shape=[
            jax.ShapeDtypeStruct((rows // HALF, HALF, width), BF),
            jax.ShapeDtypeStruct((rows, width), BF),
            jax.ShapeDtypeStruct((rows, units), BF),
            jax.ShapeDtypeStruct((rows, units), BF),
        ],
        in_specs=[part(width), part(width), whole(up_weight), whole(down_weight)],
        out_specs=[
            pl.BlockSpec((2, HALF, width), lambda i: (i, 0, 0)),
            part(width),
            part(units),
            part(units),
        ],
        compiler_params=pltpu.CompilerParams(vmem_limit_bytes=56 * 2**20),
        cost_estimate=pl.CostEstimate(
            flops=6 * rows * width * units, bytes_accessed=3 * 2**20, transcendentals=0
        ),
    )(stream, grad_out, up_weight, down_weight)


def forward_kernel(
    block_input, far_input, labels_col, labels_row, qkv_weight, out_weight, unit, act, pre_grad,
    grad_out,
    turned_in, query_out, key_out, turned_value, probs_out, turned_probs, turned_attended,
    turned_qkv, turned_out, ffn, rows_f32,
):
    near = normalize(block_input[...])[0]
    far = normalize(far_input[...])[0]
    windows = block_input.shape[0] // WIN
    for i in range(3):
        turned_qkv[HS * i : HS * i + HS, :] = qkv_weight[i].astype(F32).T.astype(BF)
    turned_out[...] = out_weight[...].astype(F32).T.astype(BF)
    for index in range(windows):
        start = HALF + WIN * index
        if index < windows - 1:
            piece = near[start : start + WIN]
        else:
            piece = jnp.concatenate([near[start:], far], axis=0)
        inputs = piece.astype(BF)
        turned_in[index] = piece.T.astype(BF)
        query, key, value = [dot(inputs, qkv_weight[i]) for i in range(3)]
        query, key = query.astype(BF), key.astype(BF)
        query_out[index] = query
        key_out[index] = key
        turned_value[index] = value.T.astype(BF)
        scores = contract_cols(query, key) * HS**-0.5
        kept = jnp.where(labels_col[index] == labels_row[index], scores, -jnp.inf)
        raised = jnp.exp(kept - jnp.max(kept, axis=-1, keepdims=True))
        probs = raised / jnp.sum(raised, axis=-1, keepdims=True)
        probs_out[index] = probs
        turned_probs[index] = probs.T.astype(BF)
        turned_attended[index] = dot(probs.astype(BF), value.astype(BF)).T.astype(BF)
    up_grad = contract_rows(unit[...], pre_grad[...])
    ups, wide = up_grad.shape[0], up_grad.shape[1] // 128
    for column in range(wide):
        rows_f32[pl.ds(column, ups, stride=wide), :] = up_grad[:, 128 * column : 128 * column + 128]
    down_grad = contract_rows(act[...], grad_out[...])
    downs, wide = down_grad.shape[0], down_grad.shape[1] // 128
    base = ups * up_grad.shape[1] // 128
    for column in range(wide):
        rows_f32[pl.ds(base + column, downs, stride=wide), :] = down_grad[
            :, 128 * column : 128 * column + 128
        ]
    for owner in range(32, 96):
        block = rows_f32[32 * (owner - 32) : 32 * (owner - 31), :].astype(BF)
        ffn[owner - 32] = block


def middle_kernel(parts, stream, grad_out, _, mid, grad_mid):
    summed = jnp.sum(parts[...].astype(F32), axis=0)
    normed, factor = normalize(stream[...])
    middle = grad_out[...].astype(F32) + norm_back(normed, factor, summed)
    mid[...] = middle
    grad_mid[...] = middle.astype(BF)


def window_back(
    upper, index, query, key, turned_value, probs_in, turned_probs, turned_attended, turned_in,
    turned_qkv, turned_out,
):
    probs = probs_in[index]
    attended_grad = dot(upper, turned_out[...]).astype(BF)
    out_grad = dot(turned_attended[index], upper)
    prob_grad = dot(attended_grad, turned_value[index])
    inner = prob_grad - jnp.sum(prob_grad * probs, axis=-1, keepdims=True)
    score_grad = (probs * inner * HS**-0.5).astype(BF)
    grads = jnp.concatenate(
        [
            dot(score_grad, key[index]),
            contract_rows(score_grad, query[index]),
            dot(turned_probs[index], attended_grad),
        ],
        axis=1,
    ).astype(BF)
    return dot(grads, turned_qkv[...]), dot(turned_in[index], grads), out_grad


def near_kernel(grad_mid, *refs):
    saved, (in_grad, qkv_total, out_total) = refs[:9], refs[9:]
    qkv_sum, out_sum = 0.0, 0.0
    grads = grad_mid[...].astype(F32)
    for index in range(grad_mid.shape[0] // WIN - 1):
        upper = grads[HALF + WIN * index : HALF + WIN * index + WIN].astype(BF)
        rows, qkv_grad, out_grad = window_back(upper, index, *saved)
        qkv_sum, out_sum = qkv_sum + qkv_grad, out_sum + out_grad
        in_grad[2 * index] = rows[:HALF].astype(BF)
        in_grad[2 * index + 1] = rows[HALF:].astype(BF)
    qkv_total[...] = qkv_sum
    out_total[...] = out_sum


def far_kernel(place, own, far, *refs):
    saved, (in_near, qkv_total, out_total, ffn) = refs[:9], refs[9:13]
    in_grad, first, second, third, fourth, grads, outs, pieces = refs[13:]
    upper = jnp.concatenate([own[...].astype(F32), far[...].astype(F32)], axis=0).astype(BF)
    rows, qkv_grad, out_grad = window_back(upper, saved[0].shape[0] - 1, *saved)
    count = in_grad.shape[0]
    in_grad[count - 1] = rows[:HALF].astype(BF)
    in_grad[0] = rows[HALF:].astype(BF)
    for chunk in range(count - 2):
        in_grad[chunk + 1] = in_near[chunk]
    qkv_grad = qkv_total[...] + qkv_grad
    out_grad = out_total[...] + out_grad
    for i in range(3):
        grads[i] = qkv_grad[:, HS * i : HS * i + HS]
    for column in range(out_grad.shape[1] // 128):
        outs[pl.ds(column, HS, stride=4), :] = out_grad[:, 128 * column : 128 * column + 128]
    slots = [lax.rem(x - place[0] + 4, 4) for x in range(4)]
    for owner in range(96):
        if owner < 24:
            kind, start = owner // 8, owner % 8 * 64
            even = grads[kind, pl.ds(start, 32, stride=2), :]
            odd = grads[kind, pl.ds(start + 1, 32, stride=2), :]
            block = jnp.concatenate([even, odd], axis=1).astype(BF)
        elif owner < 32:
            block = outs[32 * (owner - 24) : 32 * (owner - 23), :].astype(BF)
        else:
            block = ffn[owner - 32]
        pieces[slots[owner % 12 // 3], owner // 12 * 3 + owner % 3] = block
    for slot, out in enumerate((first, second, third, fourth)):
        out[...] = pieces[slot]


def sum_kernel(parts, total, total_b):
    total[...] = jnp.sum(parts[...].astype(F32), axis=0)
    total_b[...] = total[...].astype(BF)


def final_kernel(place, summed, arrived, mid, block_input, grad_input):
    total = jnp.where(place[0] == 0, arrived[...].astype(F32), summed[...])
    normed, factor = normalize(block_input[...])
    grad_input[...] = (mid[...] + norm_back(normed, factor, total)).astype(BF)


def exchange(pieces, axis):
    received = lax.all_to_all(pieces, axis, 0, 0)
    return jnp.sum(received.astype(F32), axis=0)


def shards(block_input, stream, grad_out, regions, qkv_weight, out_weight, up_weight, down_weight):
    rows, width = block_input.shape
    windows = rows // WIN
    head_count = lax.axis_size(HEAD_AXES)
    share_rows = rows // head_count
    head = lax.axis_index(HEAD_AXES)
    columns = qkv_weight.shape[2]
    count = lax.axis_size(WIN_AXES)

    def share(values):
        return lax.dynamic_slice_in_dim(values, head * share_rows, share_rows, 0)

    def from_next(values):
        return lax.ppermute(values, WIN_AXES, [((i + 1) % count, i) for i in range(count)])

    far_input = from_next(block_input[:HALF])
    unit_grad, unit, act, pre_grad = mlp(stream, grad_out, up_weight, down_weight)
    parts = lax.all_to_all(unit_grad, HEAD_AXES, 0, 0)
    labels = regions.reshape(windows, WIN)
    per_window = (windows, WIN, columns)
    turned_in, query, key, value, probs, turned_probs, attended, qkv_t, out_t, ffn = call(
        forward_kernel,
        [
            ((windows, width, WIN), BF),
            (per_window, BF),
            (per_window, BF),
            ((windows, columns, WIN), BF),
            ((windows, WIN, WIN), F32),
            ((windows, WIN, WIN), BF),
            ((windows, columns, WIN), BF),
            ((3 * columns, width), BF),
            ((width, columns), BF),
            ((64,) + BLOCK, BF),
        ],
        (
            block_input, far_input, labels[:, :, None], labels[:, None, :], qkv_weight, out_weight,
            unit, act, pre_grad, grad_out,
        ),
        scratch=[pltpu.VMEM((64 * 32, 128), F32)],
    )
    mid, own_grad_mid = call(
        middle_kernel,
        [((share_rows, width), F32), ((share_rows, width), BF)],
        (parts, share(stream), share(grad_out)),
        after=(query,),
    )
    grad_mid = lax.all_gather(own_grad_mid, HEAD_AXES, axis=0, tiled=True)
    far_grad = from_next(grad_mid[:HALF])
    saved = (query, key, value, probs, turned_probs, attended, turned_in, qkv_t, out_t)
    in_near, qkv_total, out_total = call(
        near_kernel,
        [((head_count - 2, HALF, width), BF), ((width, 3 * columns), F32), ((columns, width), F32)],
        (grad_mid, *saved),
    )
    in_grad, *pieces = call(
        far_kernel,
        [((head_count, HALF, width), BF)] + [((24,) + BLOCK, BF)] * 4,
        (
            lax.axis_index("x").astype(jnp.int32).reshape(1), grad_mid[rows - HALF :], far_grad,
            *saved, in_near, qkv_total, out_total, ffn,
        ),
        scratch=[
            pltpu.VMEM((3, width, columns), F32),
            pltpu.VMEM((8 * 32, 128), F32),
            pltpu.VMEM((4, 24) + BLOCK, BF),
        ],
        scalars=1,
    )
    in_parts = lax.all_to_all(in_grad, HEAD_AXES, 0, 0)
    moved = [
        lax.ppermute(pieces[k], "x", [(i, (i + k) % 4) for i in range(4)]) for k in range(1, 4)
    ]
    partial_sum = sum(piece.astype(F32) for piece in [pieces[0]] + moved).astype(BF)
    summed, summed_b = call(
        sum_kernel, [((share_rows, width), F32), ((share_rows, width), BF)], (in_parts,)
    )
    size = lax.axis_size(HEAD_AXES)
    arrived = lax.ppermute(
        summed_b,
        WIN_AXES + HEAD_AXES,
        [(i * size, (i + 1) % count * size) for i in range(count)],
    )
    owned = exchange(partial_sum, ("y", "zh"))
    (grad_input,) = call(
        final_kernel,
        [((share_rows, width), BF)],
        (head.astype(jnp.int32).reshape(1), summed, arrived, mid, share(block_input)),
        scalars=1,
    )
    return (grad_input, owned.reshape(1, -1))


def solution(mesh):
    fine = Mesh(mesh.devices.reshape(8, 4, 3, 4, 2), WIN_AXES + HEAD_AXES)
    return jax.shard_map(
        shards,
        mesh=fine,
        in_specs=(
            P(WIN_AXES, None),
            P(WIN_AXES, None),
            P(WIN_AXES, None),
            P(WIN_AXES),
            P(None, None, HEAD_AXES),
            P(HEAD_AXES, None),
            P(None, HEAD_AXES),
            P(HEAD_AXES, None),
        ),
        out_specs=(P(WIN_AXES + HEAD_AXES, None), P(HEAD_AXES, WIN_AXES)),
        check_vma=False,
    )
```

```python
import jax
import jax.numpy as jnp
from jax import lax
from jax.experimental import pallas as pl
from jax.experimental.pallas import tpu as pltpu
from jax.sharding import Mesh, PartitionSpec as P

HS = 64
WIN = 144
HALF = 72
WIN_AXES = ("y", "x", "zh")
HEAD_AXES = ("zl", "core")
BLOCK = (32, 128)
EPSILON = 1e-05
BF = jnp.bfloat16
F32 = jnp.float32


def normalize(values):
    data_f = values.astype(F32)
    centred = data_f - jnp.mean(data_f, axis=-1, keepdims=True)
    factor = lax.rsqrt(jnp.mean(centred * centred, axis=-1, keepdims=True) + EPSILON)
    return (centred * factor, factor)


def norm_back(normed, factor, upper):
    inner = upper - jnp.mean(upper, axis=-1, keepdims=True)
    return factor * (inner - normed * jnp.mean(upper * normed, axis=-1, keepdims=True))


def dot(left, right):
    return lax.dot_general(left, right, (((1,), (0,)), ((), ())), preferred_element_type=F32)


def contract_rows(left, right):
    return lax.dot_general(left, right, (((0,), (0,)), ((), ())), preferred_element_type=F32)


def contract_cols(left, right):
    return lax.dot_general(left, right, (((1,), (1,)), ((), ())), preferred_element_type=F32)


VMEM = pl.BlockSpec(memory_space=pltpu.VMEM)
SMEM = pl.BlockSpec(memory_space=pltpu.SMEM)
ANY = pl.BlockSpec(memory_space=pl.ANY)


def call(kernel, grid, ins, outs, args, scratch=(), chosen=None, flops=10**8):
    spec = pltpu.PrefetchScalarGridSpec(
        num_scalar_prefetch=0 if chosen is None else 1,
        grid=grid,
        in_specs=ins,
        out_specs=[out[2] for out in outs],
        scratch_shapes=list(scratch),
    )
    first = () if chosen is None else (chosen,)
    return pl.pallas_call(
        kernel,
        grid_spec=spec,
        out_shape=[jax.ShapeDtypeStruct(out[0], out[1]) for out in outs],
        compiler_params=pltpu.CompilerParams(vmem_limit_bytes=24 * 2**20),
        cost_estimate=pl.CostEstimate(flops=flops, bytes_accessed=2 * 2**20, transcendentals=0),
    )(*first, *args)


def whole(array):
    zeros = (0,) * len(array.shape)
    return pl.BlockSpec(array.shape, lambda *_: zeros)


def mlp_kernel(
    place, stream, grad_out, up_weight, down_weight, unit_grad, first, second, third, fourth, early,
    up_sum, down_sum, rows_f32, pieces,
):
    step = pl.program_id(0)
    unit = normalize(stream[...])[0].astype(BF)
    pre = dot(unit, up_weight[...])
    upper = contract_cols(grad_out[...], down_weight[...])
    scale = 0.7978845608028654
    square = pre * pre
    bent = jnp.tanh(scale * (pre + 0.044715 * (square * pre)))
    slope = 0.5 * (1.0 + bent) + 0.5 * pre * (1.0 - bent * bent) * (
        scale * (1.0 + 3 * 0.044715 * square)
    )
    pre_grad = (upper * slope).astype(BF)
    act = (0.5 * pre * (1.0 + bent)).astype(BF)
    grad = contract_cols(pre_grad, up_weight[...])
    unit_grad[0] = grad[:HALF].astype(BF)
    unit_grad[1] = grad[HALF:].astype(BF)
    up_part = contract_rows(unit, pre_grad)
    down_part = contract_rows(act, grad_out[...])

    @pl.when(step == 0)
    def _():
        up_sum[...] = up_part
        down_sum[...] = down_part

    @pl.when(step > 0)
    def _():
        up_sum[...] += up_part
        down_sum[...] += down_part

    @pl.when(step == pl.num_programs(0) - 1)
    def _():
        base = 0
        for total in (up_sum, down_sum):
            rows, wide = total.shape[0], total.shape[1] // 128
            for column in range(wide):
                rows_f32[pl.ds(base + column, rows, stride=wide), :] = total[
                    :, 128 * column : 128 * column + 128
                ]
            base += rows * wide
        slots = [lax.rem(x - place[0] + 4, 4) for x in range(4)]
        for owner in range(32, 96):
            block = rows_f32[32 * (owner - 32) : 32 * (owner - 31), :].astype(BF)
            if owner < 36:
                early[owner - 32] = block
            else:
                pieces[slots[owner % 12 // 3], owner // 12 * 3 + owner % 3 - 9] = block
        for slot, out in enumerate((first, second, third, fourth)):
            out[...] = pieces[slot]


def mlp(x_place, stream, grad_out, up_weight, down_weight):
    rows, width = stream.shape
    units = up_weight.shape[1]
    part = lambda columns: pl.BlockSpec((WIN, columns), lambda i, s: (i, 0))
    late = jax.ShapeDtypeStruct((15,) + BLOCK, BF)
    early = jax.ShapeDtypeStruct((4,) + BLOCK, BF)
    return call(
        mlp_kernel,
        (rows // WIN,),
        [part(width), part(width), whole(up_weight), whole(down_weight)],
        [((rows // HALF, HALF, width), BF, pl.BlockSpec((2, HALF, width), lambda i, s: (i, 0, 0)))]
        + [(late.shape, BF, whole(late))] * 4
        + [(early.shape, BF, whole(early))],
        (stream, grad_out, up_weight, down_weight),
        scratch=[
            pltpu.VMEM((width, units), F32),
            pltpu.VMEM((units, width), F32),
            pltpu.VMEM((64 * 32, 128), F32),
            pltpu.VMEM((4, 15) + BLOCK, BF),
        ],
        chosen=x_place,
        flops=10 * rows * width * units,
    )


def forward_kernel(lead, trail, far, labels, turned_qkv, hidden, packed, probs_out):
    step = pl.program_id(0)
    tail = jnp.where(step == pl.num_programs(0) - 1, far[...].astype(F32), trail[0].astype(F32))
    piece = jnp.concatenate([normalize(lead[0])[0], normalize(tail)[0]], axis=0)
    inputs = piece.astype(BF)
    hidden[0] = inputs
    query, key, value = [contract_cols(inputs, turned_qkv[i]).astype(BF) for i in range(3)]
    row = labels[pl.ds(step, 1), :].astype(F32)
    column = jnp.broadcast_to(row, (8, WIN)).T[:, :1]
    scores = contract_cols(query, key) * HS**-0.5
    kept = jnp.where(column == row, scores, -jnp.inf)
    raised = jnp.exp(kept - jnp.max(kept, axis=-1, keepdims=True))
    probs = raised / jnp.sum(raised, axis=-1, keepdims=True)
    probs_out[0] = probs
    attended = dot(probs.astype(BF), value).astype(BF)
    packed[0] = jnp.concatenate([query, key, value, attended], axis=1)


def middle_kernel(place, parts, stream, grad_out, _, mid, grad_mid):
    summed = jnp.sum(parts[...].astype(F32), axis=0)
    normed, factor = normalize(stream[0])
    middle = grad_out[0].astype(F32) + norm_back(normed, factor, summed)
    mid[...] = middle
    grad_mid[...] = middle.astype(BF)


def window_back(upper, hidden, packed, probs_in, turned_qkv, out_weight):
    probs = probs_in[0]
    query, key, value, attended = [packed[0][:, HS * i : HS * i + HS] for i in range(4)]
    attended_grad = contract_cols(upper, out_weight[...]).astype(BF)
    out_grad = contract_rows(attended, upper)
    prob_grad = contract_cols(attended_grad, value)
    inner = prob_grad - jnp.sum(prob_grad * probs, axis=-1, keepdims=True)
    score_grad = (probs * inner * HS**-0.5).astype(BF)
    grads = jnp.concatenate(
        [
            dot(score_grad, key),
            contract_rows(score_grad, query),
            contract_rows(probs.astype(BF), attended_grad),
        ],
        axis=1,
    ).astype(BF)
    return dot(grads, turned_qkv[...]), contract_rows(hidden[0], grads), out_grad


def near_kernel(lead, trail, *refs):
    saved, (in_grad, qkv_total, out_total) = refs[:5], refs[5:]
    step = pl.program_id(0)
    upper = jnp.concatenate([lead[0].astype(F32), trail[0].astype(F32)], axis=0).astype(BF)
    rows, qkv_grad, out_grad = window_back(upper, *saved)
    in_grad[2 * step] = rows[:HALF].astype(BF)
    in_grad[2 * step + 1] = rows[HALF:].astype(BF)

    @pl.when(step == 0)
    def _():
        qkv_total[...] = qkv_grad
        out_total[...] = out_grad

    @pl.when(step > 0)
    def _():
        qkv_total[...] += qkv_grad
        out_total[...] += out_grad


def far_kernel(place, own, far, *refs):
    saved, (in_near, qkv_total, out_total, early) = refs[:5], refs[5:9]
    in_grad, first, second, third, fourth, grads, outs, pieces = refs[9:]
    upper = jnp.concatenate([own[0].astype(F32), far[...].astype(F32)], axis=0).astype(BF)
    rows, qkv_grad, out_grad = window_back(upper, *saved)
    in_grad[in_grad.shape[0] - 1] = rows[:HALF].astype(BF)
    in_grad[0] = rows[HALF:].astype(BF)
    for chunk in range(in_near.shape[0]):
        in_grad[chunk + 1] = in_near[chunk]
    qkv_grad = qkv_total[...] + qkv_grad
    out_grad = out_total[...] + out_grad
    for i in range(3):
        grads[i] = qkv_grad[:, HS * i : HS * i + HS]
    for column in range(out_grad.shape[1] // 128):
        outs[pl.ds(column, HS, stride=4), :] = out_grad[:, 128 * column : 128 * column + 128]
    slots = [lax.rem(x - place[0] + 4, 4) for x in range(4)]
    for owner in range(36):
        if owner < 24:
            kind, start = owner // 8, owner % 8 * 64
            even = grads[kind, pl.ds(start, 32, stride=2), :]
            odd = grads[kind, pl.ds(start + 1, 32, stride=2), :]
            block = jnp.concatenate([even, odd], axis=1).astype(BF)
        elif owner < 32:
            block = outs[32 * (owner - 24) : 32 * (owner - 23), :].astype(BF)
        else:
            block = early[owner - 32]
        pieces[slots[owner % 12 // 3], owner // 12 * 3 + owner % 3] = block
    for slot, out in enumerate((first, second, third, fourth)):
        out[...] = pieces[slot]


def sum_kernel(parts, total, total_b):
    total[...] = jnp.sum(parts[...].astype(F32), axis=0)
    total_b[...] = total[...].astype(BF)


def final_kernel(place, summed, arrived, mid, block_input, grad_input):
    total = jnp.where(place[0] == 0, arrived[...].astype(F32), summed[...])
    normed, factor = normalize(block_input[0])
    grad_input[...] = (mid[...] + norm_back(normed, factor, total)).astype(BF)


def exchange(pieces, axis):
    received = lax.all_to_all(pieces, axis, 0, 0)
    return jnp.sum(received.astype(F32), axis=0)


def shards(block_input, stream, grad_out, regions, qkv_weight, out_weight, up_weight, down_weight):
    rows, width = block_input.shape
    windows = rows // WIN
    head_count = lax.axis_size(HEAD_AXES)
    share_rows = rows // head_count
    head = lax.axis_index(HEAD_AXES)
    columns = qkv_weight.shape[2]
    count = lax.axis_size(WIN_AXES)
    head_place = head.astype(jnp.int32).reshape(1)
    x_place = lax.axis_index("x").astype(jnp.int32).reshape(1)
    chunk = (1, HALF, width)
    chunked = [array.reshape(-1, HALF, width) for array in (block_input, stream, grad_out)]
    chunks_in, chunks_mid, chunks_out = chunked
    turned_qkv = jnp.swapaxes(qkv_weight, 1, 2)

    def from_next(values):
        return lax.ppermute(values, WIN_AXES, [((i + 1) % count, i) for i in range(count)])

    def along_x(pieces):
        moved = [
            lax.ppermute(pieces[k], "x", [(i, (i + k) % 4) for i in range(4)]) for k in range(1, 4)
        ]
        return sum(piece.astype(F32) for piece in [pieces[0]] + moved).astype(BF)

    far_input = from_next(block_input[:HALF])
    unit_grad, *late, early = mlp(x_place, stream, grad_out, up_weight, down_weight)
    parts = lax.all_to_all(unit_grad, HEAD_AXES, 0, 0)
    late_sum = along_x(late)
    labels = regions.reshape(windows, WIN)
    window = lambda columns, offset=0: pl.BlockSpec(
        (1, WIN, columns), lambda i, *_: (i + offset, 0, 0)
    )
    hidden, packed, probs = call(
        forward_kernel,
        (windows,),
        [
            pl.BlockSpec(chunk, lambda i: (2 * i + 1, 0, 0)),
            pl.BlockSpec(chunk, lambda i: (jnp.minimum(2 * i + 2, 2 * windows - 1), 0, 0)),
            whole(far_input),
            whole(labels),
            whole(turned_qkv),
        ],
        [
            ((windows, WIN, width), BF, window(width)),
            ((windows, WIN, 4 * columns), BF, window(4 * columns)),
            ((windows, WIN, WIN), F32, window(WIN)),
        ],
        (chunks_in, chunks_in, far_input, labels, turned_qkv),
    )
    mine = pl.BlockSpec(chunk, lambda i, place: (place[0], 0, 0))
    row_part = jax.ShapeDtypeStruct((share_rows, width), BF)
    mid, own_grad_mid = call(
        middle_kernel,
        (1,),
        [whole(parts), mine, mine, ANY],
        [(row_part.shape, F32, whole(row_part)), (row_part.shape, BF, whole(row_part))],
        (parts, chunks_mid, chunks_out, probs),
        chosen=head_place,
    )
    grad_mid = lax.all_gather(own_grad_mid, HEAD_AXES, axis=0)
    far_grad = from_next(grad_mid[0])
    weights = (turned_qkv.reshape(-1, width), out_weight)
    in_near, qkv_total, out_total = call(
        near_kernel,
        (windows - 1,),
        [
            pl.BlockSpec(chunk, lambda i: (2 * i + 1, 0, 0)),
            pl.BlockSpec(chunk, lambda i: (2 * i + 2, 0, 0)),
            window(width),
            window(4 * columns),
            window(WIN),
            *[whole(weight) for weight in weights],
        ],
        [
            ((head_count - 2, HALF, width), BF, VMEM),
            ((width, 3 * columns), F32, VMEM),
            ((columns, width), F32, VMEM),
        ],
        (grad_mid, grad_mid, hidden, packed, probs, *weights),
    )
    last = windows - 1
    piece = jax.ShapeDtypeStruct((9,) + BLOCK, BF)
    in_grad, *pieces = call(
        far_kernel,
        (1,),
        [
            pl.BlockSpec(chunk, lambda i, s: (head_count - 1, 0, 0)),
            whole(far_grad),
            window(width, last),
            window(4 * columns, last),
            window(WIN, last),
            *[whole(weight) for weight in weights],
            VMEM,
            VMEM,
            VMEM,
            whole(early),
        ],
        [((head_count, HALF, width), BF, VMEM)] + [(piece.shape, BF, whole(piece))] * 4,
        (
            grad_mid, far_grad, hidden, packed, probs, *weights, in_near, qkv_total, out_total,
            early,
        ),
        scratch=[
            pltpu.VMEM((3, width, columns), F32),
            pltpu.VMEM((8 * 32, 128), F32),
            pltpu.VMEM((4, 9) + BLOCK, BF),
        ],
        chosen=x_place,
    )
    in_parts = lax.all_to_all(in_grad, HEAD_AXES, 0, 0)
    early_sum = along_x(pieces)
    summed, summed_b = call(
        sum_kernel,
        (1,),
        [whole(in_parts)],
        [(row_part.shape, F32, whole(row_part)), (row_part.shape, BF, whole(row_part))],
        (in_parts,),
    )
    arrived = lax.ppermute(
        summed_b,
        WIN_AXES + HEAD_AXES,
        [(i * head_count, (i + 1) % count * head_count) for i in range(count)],
    )
    owned = exchange(jnp.concatenate([early_sum, late_sum], 0), ("y", "zh"))
    (grad_input,) = call(
        final_kernel,
        (1,),
        [whole(summed), whole(arrived), whole(mid), mine],
        [(row_part.shape, BF, whole(row_part))],
        (summed, arrived, mid, chunks_in),
        chosen=head_place,
    )
    return (grad_input, owned.reshape(1, -1))


def solution(mesh):
    fine = Mesh(mesh.devices.reshape(8, 4, 3, 4, 2), WIN_AXES + HEAD_AXES)
    return jax.shard_map(
        shards,
        mesh=fine,
        in_specs=(
            P(WIN_AXES, None),
            P(WIN_AXES, None),
            P(WIN_AXES, None),
            P(WIN_AXES),
            P(None, None, HEAD_AXES),
            P(HEAD_AXES, None),
            P(None, HEAD_AXES),
            P(HEAD_AXES, None),
        ),
        out_specs=(P(WIN_AXES + HEAD_AXES, None), P(HEAD_AXES, WIN_AXES)),
        check_vma=False,
    )
```

```python
import jax
import jax.numpy as jnp
from jax import lax
from jax.experimental import pallas as pl
from jax.experimental.pallas import tpu as pltpu
from jax.sharding import Mesh, PartitionSpec as P

HS = 64
WIN = 144
HALF = 72
WIN_AXES = ("y", "x", "zh")
HEAD_AXES = ("zl", "core")
BLOCK = (32, 128)
EPSILON = 1e-05
BF = jnp.bfloat16
F32 = jnp.float32


def normalize(values):
    data_f = values.astype(F32)
    centred = data_f - jnp.mean(data_f, axis=-1, keepdims=True)
    factor = lax.rsqrt(jnp.mean(centred * centred, axis=-1, keepdims=True) + EPSILON)
    return (centred * factor, factor)


def norm_back(normed, factor, upper):
    inner = upper - jnp.mean(upper, axis=-1, keepdims=True)
    return factor * (inner - normed * jnp.mean(upper * normed, axis=-1, keepdims=True))


def dot(left, right):
    return lax.dot_general(left, right, (((1,), (0,)), ((), ())), preferred_element_type=F32)


def contract_rows(left, right):
    return lax.dot_general(left, right, (((0,), (0,)), ((), ())), preferred_element_type=F32)


def contract_cols(left, right):
    return lax.dot_general(left, right, (((1,), (1,)), ((), ())), preferred_element_type=F32)


VMEM = pl.BlockSpec(memory_space=pltpu.VMEM)
SMEM = pl.BlockSpec(memory_space=pltpu.SMEM)
ANY = pl.BlockSpec(memory_space=pl.ANY)


def call(kernel, grid, ins, outs, args, scratch=(), chosen=None, flops=10**8, vmem=60):
    spec = pltpu.PrefetchScalarGridSpec(
        num_scalar_prefetch=0 if chosen is None else 1,
        grid=grid,
        in_specs=ins,
        out_specs=[out[2] for out in outs],
        scratch_shapes=list(scratch),
    )
    first = () if chosen is None else (chosen,)
    return pl.pallas_call(
        kernel,
        grid_spec=spec,
        out_shape=[jax.ShapeDtypeStruct(out[0], out[1]) for out in outs],
        compiler_params=pltpu.CompilerParams(vmem_limit_bytes=vmem * 2**20),
        cost_estimate=pl.CostEstimate(flops=flops, bytes_accessed=2 * 2**20, transcendentals=0),
    )(*first, *args)


def whole(array):
    zeros = (0,) * len(array.shape)
    return pl.BlockSpec(array.shape, lambda *_: zeros)


def mlp_kernel(
    place, stream, grad_out, up_weight, down_weight, unit_grad, first, second, third, fourth, early,
    up_sum, down_sum, rows_f32, pieces,
):
    step = pl.program_id(0)
    unit = normalize(stream[...])[0].astype(BF)
    pre = dot(unit, up_weight[...])
    upper = contract_cols(grad_out[...], down_weight[...])
    scale = 0.7978845608028654
    square = pre * pre
    bent = jnp.tanh(scale * (pre + 0.044715 * (square * pre)))
    slope = 0.5 * (1.0 + bent) + 0.5 * pre * (1.0 - bent * bent) * (
        scale * (1.0 + 3 * 0.044715 * square)
    )
    pre_grad = (upper * slope).astype(BF)
    act = (0.5 * pre * (1.0 + bent)).astype(BF)
    grad = contract_cols(pre_grad, up_weight[...])
    unit_grad[0] = grad[:HALF].astype(BF)
    unit_grad[1] = grad[HALF:].astype(BF)
    up_part = contract_rows(unit, pre_grad)
    down_part = contract_rows(act, grad_out[...])

    @pl.when(step == 0)
    def _():
        up_sum[...] = up_part
        down_sum[...] = down_part

    @pl.when(step > 0)
    def _():
        up_sum[...] += up_part
        down_sum[...] += down_part

    @pl.when(step == pl.num_programs(0) - 1)
    def _():
        base = 0
        for total in (up_sum, down_sum):
            rows, wide = total.shape[0], total.shape[1] // 128
            for column in range(wide):
                rows_f32[pl.ds(base + column, rows, stride=wide), :] = total[
                    :, 128 * column : 128 * column + 128
                ]
            base += rows * wide
        slots = [lax.rem(x - place[0] + 4, 4) for x in range(4)]
        for owner in range(32, 96):
            block = rows_f32[32 * (owner - 32) : 32 * (owner - 31), :].astype(BF)
            if owner < 36:
                early[owner - 32] = block
            else:
                pieces[slots[owner % 12 // 3], owner // 12 * 3 + owner % 3 - 9] = block
        for slot, out in enumerate((first, second, third, fourth)):
            out[...] = pieces[slot]


def mlp(x_place, stream, grad_out, up_weight, down_weight):
    rows, width = stream.shape
    units = up_weight.shape[1]
    part = lambda columns: pl.BlockSpec((WIN, columns), lambda i, s: (i, 0))
    late = jax.ShapeDtypeStruct((15,) + BLOCK, BF)
    early = jax.ShapeDtypeStruct((4,) + BLOCK, BF)
    return call(
        mlp_kernel,
        (rows // WIN,),
        [part(width), part(width), whole(up_weight), whole(down_weight)],
        [((rows // HALF, HALF, width), BF, pl.BlockSpec((2, HALF, width), lambda i, s: (i, 0, 0)))]
        + [(late.shape, BF, whole(late))] * 4
        + [(early.shape, BF, whole(early))],
        (stream, grad_out, up_weight, down_weight),
        scratch=[
            pltpu.VMEM((width, units), F32),
            pltpu.VMEM((units, width), F32),
            pltpu.VMEM((64 * 32, 128), F32),
            pltpu.VMEM((4, 15) + BLOCK, BF),
        ],
        chosen=x_place,
        flops=10 * rows * width * units,
    )


def window_forward(lead, tail, row, turned_qkv):
    piece = jnp.concatenate([normalize(lead)[0], normalize(tail)[0]], axis=0)
    inputs = piece.astype(BF)
    query, key, value = [
        contract_cols(inputs, turned_qkv[HS * i : HS * i + HS, :]).astype(BF) for i in range(3)
    ]
    row = row.astype(F32)
    column = jnp.broadcast_to(row, (8, WIN)).T[:, :1]
    scores = contract_cols(query, key) * HS**-0.5
    kept = jnp.where(column == row, scores, -jnp.inf)
    raised = jnp.exp(kept - jnp.max(kept, axis=-1, keepdims=True))
    probs = raised / jnp.sum(raised, axis=-1, keepdims=True)
    attended = dot(probs.astype(BF), value).astype(BF)
    return inputs, (query, key, value, attended), probs


def forward_kernel(lead, tail, labels, turned_qkv, hidden, packed, probs_out):
    row = labels[pl.ds(pl.program_id(0), 1), :]
    hidden[0], parts, probs_out[0] = window_forward(lead[0], tail[0], row, turned_qkv)
    packed[0] = jnp.concatenate(parts, axis=1)


def middle_kernel(place, parts, stream, grad_out, _, __, mid, grad_mid):
    summed = jnp.sum(parts[...].astype(F32), axis=0)
    normed, factor = normalize(stream[0])
    middle = grad_out[0].astype(F32) + norm_back(normed, factor, summed)
    mid[...] = middle
    grad_mid[...] = middle.astype(BF)


def window_back(upper, hidden, parts, probs, turned_qkv, out_weight):
    query, key, value, attended = parts
    attended_grad = contract_cols(upper, out_weight[...]).astype(BF)
    out_grad = contract_rows(attended, upper)
    prob_grad = contract_cols(attended_grad, value)
    inner = prob_grad - jnp.sum(prob_grad * probs, axis=-1, keepdims=True)
    score_grad = (probs * inner * HS**-0.5).astype(BF)
    grads = jnp.concatenate(
        [
            dot(score_grad, key),
            contract_rows(score_grad, query),
            contract_rows(probs.astype(BF), attended_grad),
        ],
        axis=1,
    ).astype(BF)
    return dot(grads, turned_qkv[...]), contract_rows(hidden, grads), out_grad


def near_kernel(lead, trail, *refs):
    hidden, packed, probs, turned_qkv, out_weight, in_grad, qkv_total, out_total = refs
    parts = [packed[0][:, HS * i : HS * i + HS] for i in range(4)]
    step = pl.program_id(0)
    upper = jnp.concatenate([lead[0].astype(F32), trail[0].astype(F32)], axis=0).astype(BF)
    rows, qkv_grad, out_grad = window_back(
        upper, hidden[0], parts, probs[0], turned_qkv, out_weight
    )
    in_grad[2 * step] = rows[:HALF].astype(BF)
    in_grad[2 * step + 1] = rows[HALF:].astype(BF)

    @pl.when(step == 0)
    def _():
        qkv_total[...] = qkv_grad
        out_total[...] = out_grad

    @pl.when(step > 0)
    def _():
        qkv_total[...] += qkv_grad
        out_total[...] += out_grad


def far_kernel(
    place, own, far, lead, tail, labels, turned_qkv, out_weight, in_near, qkv_total, out_total,
    early, in_grad, first, second, third, fourth, grads, outs, pieces,
):
    saved = window_forward(lead[0], tail[...], labels[labels.shape[0] - 1 :, :], turned_qkv)
    upper = jnp.concatenate([own[0].astype(F32), far[...].astype(F32)], axis=0).astype(BF)
    rows, qkv_grad, out_grad = window_back(upper, *saved, turned_qkv, out_weight)
    in_grad[in_grad.shape[0] - 1] = rows[:HALF].astype(BF)
    in_grad[0] = rows[HALF:].astype(BF)
    for chunk in range(in_near.shape[0]):
        in_grad[chunk + 1] = in_near[chunk]
    qkv_grad = qkv_total[...] + qkv_grad
    out_grad = out_total[...] + out_grad
    for i in range(3):
        grads[i] = qkv_grad[:, HS * i : HS * i + HS]
    for column in range(out_grad.shape[1] // 128):
        outs[pl.ds(column, HS, stride=4), :] = out_grad[:, 128 * column : 128 * column + 128]
    slots = [lax.rem(x - place[0] + 4, 4) for x in range(4)]
    for owner in range(36):
        if owner < 24:
            kind, start = owner // 8, owner % 8 * 64
            even = grads[kind, pl.ds(start, 32, stride=2), :]
            odd = grads[kind, pl.ds(start + 1, 32, stride=2), :]
            block = jnp.concatenate([even, odd], axis=1).astype(BF)
        elif owner < 32:
            block = outs[32 * (owner - 24) : 32 * (owner - 23), :].astype(BF)
        else:
            block = early[owner - 32]
        pieces[slots[owner % 12 // 3], owner // 12 * 3 + owner % 3] = block
    for slot, out in enumerate((first, second, third, fourth)):
        out[...] = pieces[slot]


def sum_kernel(parts, total, total_b):
    total[...] = jnp.sum(parts[...].astype(F32), axis=0)
    total_b[...] = total[...].astype(BF)


def final_kernel(place, summed, arrived, mid, block_input, grad_input):
    total = jnp.where(place[0] == 0, arrived[...].astype(F32), summed[...])
    normed, factor = normalize(block_input[0])
    grad_input[...] = (mid[...] + norm_back(normed, factor, total)).astype(BF)


def exchange(pieces, axis):
    received = lax.all_to_all(pieces, axis, 0, 0)
    return jnp.sum(received.astype(F32), axis=0)


def shards(block_input, stream, grad_out, regions, qkv_weight, out_weight, up_weight, down_weight):
    rows, width = block_input.shape
    windows = rows // WIN
    head_count = lax.axis_size(HEAD_AXES)
    share_rows = rows // head_count
    head = lax.axis_index(HEAD_AXES)
    columns = qkv_weight.shape[2]
    count = lax.axis_size(WIN_AXES)
    head_place = head.astype(jnp.int32).reshape(1)
    x_place = lax.axis_index("x").astype(jnp.int32).reshape(1)
    chunk = (1, HALF, width)
    chunked = [array.reshape(-1, HALF, width) for array in (block_input, stream, grad_out)]
    chunks_in, chunks_mid, chunks_out = chunked
    turned_qkv = jnp.swapaxes(qkv_weight, 1, 2)

    def from_next(values):
        return lax.ppermute(values, WIN_AXES, [((i + 1) % count, i) for i in range(count)])

    def along_x(pieces):
        moved = [
            lax.ppermute(pieces[k], "x", [(i, (i + k) % 4) for i in range(4)]) for k in range(1, 4)
        ]
        return sum(piece.astype(F32) for piece in [pieces[0]] + moved).astype(BF)

    far_input = from_next(block_input[:HALF])
    unit_grad, *late, early = mlp(x_place, stream, grad_out, up_weight, down_weight)
    parts = lax.all_to_all(unit_grad, HEAD_AXES, 0, 0)
    late_sum = along_x(late)
    labels = regions.reshape(windows, WIN)
    window = lambda columns: pl.BlockSpec((1, WIN, columns), lambda i: (i, 0, 0))
    weights = (turned_qkv.reshape(-1, width), out_weight)
    near = windows - 1
    hidden, packed, probs = call(
        forward_kernel,
        (near,),
        [
            pl.BlockSpec(chunk, lambda i: (2 * i + 1, 0, 0)),
            pl.BlockSpec(chunk, lambda i: (2 * i + 2, 0, 0)),
            whole(labels),
            whole(weights[0]),
        ],
        [
            ((near, WIN, width), BF, window(width)),
            ((near, WIN, 4 * columns), BF, window(4 * columns)),
            ((near, WIN, WIN), F32, window(WIN)),
        ],
        (chunks_in, chunks_in, labels, weights[0]),
    )
    mine = pl.BlockSpec(chunk, lambda i, place: (place[0], 0, 0))
    row_part = jax.ShapeDtypeStruct((share_rows, width), BF)
    mid, own_grad_mid = call(
        middle_kernel,
        (1,),
        [whole(parts), mine, mine, ANY, ANY],
        [(row_part.shape, F32, whole(row_part)), (row_part.shape, BF, whole(row_part))],
        (parts, chunks_mid, chunks_out, probs, late_sum),
        chosen=head_place,
        vmem=16,
    )
    grad_mid = lax.all_gather(own_grad_mid, HEAD_AXES, axis=0)
    far_grad = from_next(grad_mid[0])
    in_near, qkv_total, out_total = call(
        near_kernel,
        (near,),
        [
            pl.BlockSpec(chunk, lambda i: (2 * i + 1, 0, 0)),
            pl.BlockSpec(chunk, lambda i: (2 * i + 2, 0, 0)),
            window(width),
            window(4 * columns),
            window(WIN),
            *[whole(weight) for weight in weights],
        ],
        [
            ((head_count - 2, HALF, width), BF, VMEM),
            ((width, 3 * columns), F32, VMEM),
            ((columns, width), F32, VMEM),
        ],
        (grad_mid, grad_mid, hidden, packed, probs, *weights),
        vmem=56,
    )
    piece = jax.ShapeDtypeStruct((9,) + BLOCK, BF)
    in_grad, *pieces = call(
        far_kernel,
        (1,),
        [
            pl.BlockSpec(chunk, lambda i, s: (head_count - 1, 0, 0)),
            whole(far_grad),
            pl.BlockSpec(chunk, lambda i, s: (head_count - 1, 0, 0)),
            whole(far_input),
            whole(labels),
            *[whole(weight) for weight in weights],
            VMEM,
            VMEM,
            VMEM,
            whole(early),
        ],
        [((head_count, HALF, width), BF, VMEM)] + [(piece.shape, BF, whole(piece))] * 4,
        (
            grad_mid, far_grad, chunks_in, far_input, labels, *weights, in_near, qkv_total,
            out_total, early,
        ),
        scratch=[
            pltpu.VMEM((3, width, columns), F32),
            pltpu.VMEM((8 * 32, 128), F32),
            pltpu.VMEM((4, 9) + BLOCK, BF),
        ],
        chosen=x_place,
        vmem=56,
    )
    in_parts = lax.all_to_all(in_grad, HEAD_AXES, 0, 0)
    early_sum = along_x(pieces)
    summed, summed_b = call(
        sum_kernel,
        (1,),
        [whole(in_parts)],
        [(row_part.shape, F32, whole(row_part)), (row_part.shape, BF, whole(row_part))],
        (in_parts,),
        vmem=16,
    )
    arrived = lax.ppermute(
        summed_b,
        WIN_AXES + HEAD_AXES,
        [(i * head_count, (i + 1) % count * head_count) for i in range(count)],
    )
    owned = exchange(jnp.concatenate([early_sum, late_sum], 0), ("y", "zh"))
    (grad_input,) = call(
        final_kernel,
        (1,),
        [whole(summed), whole(arrived), whole(mid), mine],
        [(row_part.shape, BF, whole(row_part))],
        (summed, arrived, mid, chunks_in),
        chosen=head_place,
        vmem=16,
    )
    return (grad_input, owned.reshape(1, -1))


def solution(mesh):
    fine = Mesh(mesh.devices.reshape(8, 4, 3, 4, 2), WIN_AXES + HEAD_AXES)
    return jax.shard_map(
        shards,
        mesh=fine,
        in_specs=(
            P(WIN_AXES, None),
            P(WIN_AXES, None),
            P(WIN_AXES, None),
            P(WIN_AXES),
            P(None, None, HEAD_AXES),
            P(HEAD_AXES, None),
            P(None, HEAD_AXES),
            P(HEAD_AXES, None),
        ),
        out_specs=(P(WIN_AXES + HEAD_AXES, None), P(HEAD_AXES, WIN_AXES)),
        check_vma=False,
    )
```

```python
import jax
import jax.numpy as jnp
from jax import lax
from jax.experimental import pallas as pl
from jax.experimental.pallas import tpu as pltpu
from jax.sharding import Mesh, PartitionSpec as P

HS = 64
WIN = 144
HALF = 72
WIN_AXES = ("y", "x", "zh")
HEAD_AXES = ("zl", "core")
BLOCK = (32, 128)
EPSILON = 1e-05
BF = jnp.bfloat16
F32 = jnp.float32


def normalize(values):
    data_f = values.astype(F32)
    centred = data_f - jnp.mean(data_f, axis=-1, keepdims=True)
    factor = lax.rsqrt(jnp.mean(centred * centred, axis=-1, keepdims=True) + EPSILON)
    return (centred * factor, factor)


def norm_back(normed, factor, upper):
    inner = upper - jnp.mean(upper, axis=-1, keepdims=True)
    return factor * (inner - normed * jnp.mean(upper * normed, axis=-1, keepdims=True))


def dot(left, right):
    return lax.dot_general(left, right, (((1,), (0,)), ((), ())), preferred_element_type=F32)


def contract_rows(left, right):
    return lax.dot_general(left, right, (((0,), (0,)), ((), ())), preferred_element_type=F32)


def contract_cols(left, right):
    return lax.dot_general(left, right, (((1,), (1,)), ((), ())), preferred_element_type=F32)


VMEM = pl.BlockSpec(memory_space=pltpu.VMEM)
SMEM = pl.BlockSpec(memory_space=pltpu.SMEM)
ANY = pl.BlockSpec(memory_space=pl.ANY)


def call(kernel, grid, ins, outs, args, scratch=(), chosen=None, flops=10**8, vmem=60, aliases=None):
    spec = pltpu.PrefetchScalarGridSpec(
        num_scalar_prefetch=0 if chosen is None else 1,
        grid=grid,
        in_specs=ins,
        out_specs=[out[2] for out in outs],
        scratch_shapes=list(scratch),
    )
    first = () if chosen is None else (chosen,)
    return pl.pallas_call(
        kernel,
        grid_spec=spec,
        out_shape=[jax.ShapeDtypeStruct(out[0], out[1]) for out in outs],
        input_output_aliases=aliases or {},
        compiler_params=pltpu.CompilerParams(vmem_limit_bytes=int(vmem * 2**20)),
        cost_estimate=pl.CostEstimate(flops=flops, bytes_accessed=2 * 2**20, transcendentals=0),
    )(*first, *args)


def whole(array):
    zeros = (0,) * len(array.shape)
    return pl.BlockSpec(array.shape, lambda *_: zeros)


def mlp_kernel(
    stream, grad_out, up_weight, down_weight, unit_grad, late, early, up_sum, down_sum, rows_f32
):
    step = pl.program_id(0)
    unit = normalize(stream[...])[0].astype(BF)
    pre = dot(unit, up_weight[...])
    upper = contract_cols(grad_out[...], down_weight[...])
    scale = 0.7978845608028654
    square = pre * pre
    bent = jnp.tanh(scale * (pre + 0.044715 * (square * pre)))
    slope = 0.5 * (1.0 + bent) + 0.5 * pre * (1.0 - bent * bent) * (
        scale * (1.0 + 3 * 0.044715 * square)
    )
    pre_grad = (upper * slope).astype(BF)
    act = (0.5 * pre * (1.0 + bent)).astype(BF)
    grad = contract_cols(pre_grad, up_weight[...])
    unit_grad[0] = grad[:HALF].astype(BF)
    unit_grad[1] = grad[HALF:].astype(BF)
    up_part = contract_rows(unit, pre_grad)
    down_part = contract_rows(act, grad_out[...])

    @pl.when(step == 0)
    def _():
        up_sum[...] = up_part
        down_sum[...] = down_part

    @pl.when(step > 0)
    def _():
        up_sum[...] += up_part
        down_sum[...] += down_part

    @pl.when(step == pl.num_programs(0) - 1)
    def _():
        base = 0
        for total in (up_sum, down_sum):
            rows, wide = total.shape[0], total.shape[1] // 128
            for column in range(wide):
                rows_f32[pl.ds(base + column, rows, stride=wide), :] = total[
                    :, 128 * column : 128 * column + 128
                ]
            base += rows * wide
        for owner in range(32, 96):
            block = rows_f32[32 * (owner - 32) : 32 * (owner - 31), :].astype(BF)
            if owner < 36:
                early[owner - 32] = block
            else:
                late[owner % 12 // 3, owner // 12 * 3 + owner % 3 - 9] = block


def mlp(stream, grad_out, up_weight, down_weight):
    rows, width = stream.shape
    units = up_weight.shape[1]
    part = lambda columns: pl.BlockSpec((WIN, columns), lambda i: (i, 0))
    late = jax.ShapeDtypeStruct((4, 15) + BLOCK, BF)
    early = jax.ShapeDtypeStruct((4,) + BLOCK, BF)
    return call(
        mlp_kernel,
        (rows // WIN,),
        [part(width), part(width), whole(up_weight), whole(down_weight)],
        [((rows // HALF, HALF, width), BF, pl.BlockSpec((2, HALF, width), lambda i: (i, 0, 0)))]
        + [(late.shape, BF, whole(late)), (early.shape, BF, whole(early))],
        (stream, grad_out, up_weight, down_weight),
        scratch=[
            pltpu.VMEM((width, units), F32),
            pltpu.VMEM((units, width), F32),
            pltpu.VMEM((64 * 32, 128), F32),
        ],
        flops=69 * 10**8,
    )


def window_forward(lead, tail, row, turned_qkv):
    piece = jnp.concatenate([normalize(lead)[0], normalize(tail)[0]], axis=0)
    inputs = piece.astype(BF)
    query, key, value = [
        contract_cols(inputs, turned_qkv[HS * i : HS * i + HS, :]).astype(BF) for i in range(3)
    ]
    row = row.astype(F32)
    column = jnp.broadcast_to(row, (8, WIN)).T[:, :1]
    scores = contract_cols(query, key) * HS**-0.5
    kept = jnp.where(column == row, scores, -jnp.inf)
    raised = jnp.exp(kept - jnp.max(kept, axis=-1, keepdims=True))
    probs = raised / jnp.sum(raised, axis=-1, keepdims=True)
    attended = dot(probs.astype(BF), value).astype(BF)
    return inputs, (query, key, value, attended), probs


def forward_kernel(
    place, lead, tail, labels, turned_qkv, stream, grad_out, hidden, packed, probs_out, own
):
    row = labels[pl.ds(pl.program_id(0), 1), :]
    hidden[0], parts, probs_out[0] = window_forward(lead[0], tail[0], row, turned_qkv)
    packed[0] = jnp.concatenate(parts, axis=1)
    own[0] = stream[0]
    own[1] = grad_out[0]


def middle_kernel(parts, own, _, mid, grad_mid, __):
    summed = jnp.sum(parts[...].astype(F32), axis=0)
    normed, factor = normalize(own[0])
    middle = own[1].astype(F32) + norm_back(normed, factor, summed)
    mid[...] = middle
    grad_mid[...] = middle.astype(BF)


def window_back(upper, hidden, parts, probs, turned_qkv, out_weight):
    query, key, value, attended = parts
    attended_grad = contract_cols(upper, out_weight[...]).astype(BF)
    out_grad = contract_rows(attended, upper)
    prob_grad = contract_cols(attended_grad, value)
    inner = prob_grad - jnp.sum(prob_grad * probs, axis=-1, keepdims=True)
    score_grad = (probs * inner * HS**-0.5).astype(BF)
    grads = jnp.concatenate(
        [
            dot(score_grad, key),
            contract_rows(score_grad, query),
            contract_rows(probs.astype(BF), attended_grad),
        ],
        axis=1,
    ).astype(BF)
    return dot(grads, turned_qkv[...]), contract_rows(hidden, grads), out_grad


def near_kernel(lead, trail, *refs):
    hidden, packed, probs, turned_qkv, out_weight, in_grad, qkv_total, out_total = refs
    parts = [packed[0][:, HS * i : HS * i + HS] for i in range(4)]
    step = pl.program_id(0)
    upper = jnp.concatenate([lead[0].astype(F32), trail[0].astype(F32)], axis=0).astype(BF)
    rows, qkv_grad, out_grad = window_back(
        upper, hidden[0], parts, probs[0], turned_qkv, out_weight
    )
    in_grad[2 * step] = rows[:HALF].astype(BF)
    in_grad[2 * step + 1] = rows[HALF:].astype(BF)

    @pl.when(step == 0)
    def _():
        qkv_total[...] = qkv_grad
        out_total[...] = out_grad

    @pl.when(step > 0)
    def _():
        qkv_total[...] += qkv_grad
        out_total[...] += out_grad


def far_kernel(
    place, own, far, lead, tail, labels, turned_qkv, out_weight, in_near, qkv_total, out_total,
    early, in_grad, first, second, third, fourth, grads, outs, pieces,
):
    saved = window_forward(lead[0], tail[...], labels[labels.shape[0] - 1 :, :], turned_qkv)
    upper = jnp.concatenate([own[0].astype(F32), far[...].astype(F32)], axis=0).astype(BF)
    rows, qkv_grad, out_grad = window_back(upper, *saved, turned_qkv, out_weight)
    in_grad[in_grad.shape[0] - 1] = rows[:HALF].astype(BF)
    in_grad[0] = rows[HALF:].astype(BF)
    for chunk in range(in_near.shape[0]):
        in_grad[chunk + 1] = in_near[chunk]
    qkv_grad = qkv_total[...] + qkv_grad
    out_grad = out_total[...] + out_grad
    for i in range(3):
        grads[i] = qkv_grad[:, HS * i : HS * i + HS]
    for column in range(out_grad.shape[1] // 128):
        outs[pl.ds(column, HS, stride=4), :] = out_grad[:, 128 * column : 128 * column + 128]
    slots = [lax.rem(x - place[0] + 4, 4) for x in range(4)]
    for owner in range(36):
        if owner < 24:
            kind, start = owner // 8, owner % 8 * 64
            even = grads[kind, pl.ds(start, 32, stride=2), :]
            odd = grads[kind, pl.ds(start + 1, 32, stride=2), :]
            block = jnp.concatenate([even, odd], axis=1).astype(BF)
        elif owner < 32:
            block = outs[32 * (owner - 24) : 32 * (owner - 23), :].astype(BF)
        else:
            block = early[owner - 32]
        pieces[slots[owner % 12 // 3], owner // 12 * 3 + owner % 3] = block
    for slot, out in enumerate((first, second, third, fourth)):
        out[...] = pieces[slot]


def sum_kernel(parts, total, total_b):
    total[...] = jnp.sum(parts[...].astype(F32), axis=0)
    total_b[...] = total[...].astype(BF)


def final_kernel(place, summed, arrived, mid, block_input, grad_input, token):
    total = jnp.where(place[0] == 0, arrived[...].astype(F32), summed[...])
    normed, factor = normalize(block_input[0])
    grad_input[...] = (mid[...] + norm_back(normed, factor, total)).astype(BF)
    token[...] = jnp.zeros_like(token)


def join_kernel(first, second, third, fourth, late, joined):
    count = first.shape[0]
    near = (first[...].astype(F32) + second[...].astype(F32)) + (
        third[...].astype(F32) + fourth[...].astype(F32)
    )
    joined[:count] = near.astype(BF)
    joined[count:] = jnp.sum(late[...].astype(F32), axis=0).astype(BF)


def total_kernel(received, _, owned):
    owned[...] = jnp.sum(received[...].astype(F32), axis=0)


def shards(block_input, stream, grad_out, regions, qkv_weight, out_weight, up_weight, down_weight):
    rows, width = block_input.shape
    windows = rows // WIN
    head_count = lax.axis_size(HEAD_AXES)
    share_rows = rows // head_count
    head = lax.axis_index(HEAD_AXES)
    columns = qkv_weight.shape[2]
    count = lax.axis_size(WIN_AXES)
    head_place = head.astype(jnp.int32).reshape(1)
    x_place = lax.axis_index("x").astype(jnp.int32).reshape(1)
    chunk = (1, HALF, width)
    chunked = [array.reshape(-1, HALF, width) for array in (block_input, stream, grad_out)]
    chunks_in, chunks_mid, chunks_out = chunked
    turned_qkv = jnp.swapaxes(qkv_weight, 1, 2)

    def from_next(values):
        return lax.ppermute(values, WIN_AXES, [((i + 1) % count, i) for i in range(count)])

    far_input = from_next(block_input[:HALF])
    unit_grad, late, early = mlp(stream, grad_out, up_weight, down_weight)
    parts = lax.all_to_all(unit_grad, HEAD_AXES, 0, 0)
    labels = regions.reshape(windows, WIN)
    window = lambda columns: pl.BlockSpec((1, WIN, columns), lambda i, *_: (i, 0, 0))
    weights = (turned_qkv.reshape(-1, width), out_weight)
    near = windows - 1
    token = jax.ShapeDtypeStruct((8, 128), F32)
    row_part = jax.ShapeDtypeStruct((share_rows, width), BF)
    mine = pl.BlockSpec(chunk, lambda i, place: (place[0], 0, 0))
    own_rows = jax.ShapeDtypeStruct((2, share_rows, width), BF)
    hidden, packed, probs, own = call(
        forward_kernel,
        (near,),
        [
            pl.BlockSpec(chunk, lambda i, _: (2 * i + 1, 0, 0)),
            pl.BlockSpec(chunk, lambda i, _: (2 * i + 2, 0, 0)),
            whole(labels),
            whole(weights[0]),
            mine,
            mine,
        ],
        [
            ((near, WIN, width), BF, window(width)),
            ((near, WIN, 4 * columns), BF, window(4 * columns)),
            ((near, WIN, WIN), F32, window(WIN)),
            (own_rows.shape, BF, whole(own_rows)),
        ],
        (chunks_in, chunks_in, labels, weights[0], chunks_mid, chunks_out),
        chosen=head_place,
        flops=53 * 10**8,
    )
    mid, own_grad_mid, late = call(
        middle_kernel,
        (1,),
        [whole(parts), whole(own), ANY],
        [
            (row_part.shape, F32, whole(row_part)),
            (row_part.shape, BF, whole(row_part)),
            (late.shape, BF, ANY),
        ],
        (parts, own, late),
        aliases={2: 2},
        vmem=16,
    )
    grad_mid = lax.all_gather(own_grad_mid, HEAD_AXES, axis=0)
    far_grad = from_next(grad_mid[0])
    in_near, qkv_total, out_total = call(
        near_kernel,
        (near,),
        [
            pl.BlockSpec(chunk, lambda i: (2 * i + 1, 0, 0)),
            pl.BlockSpec(chunk, lambda i: (2 * i + 2, 0, 0)),
            window(width),
            window(4 * columns),
            window(WIN),
            *[whole(weight) for weight in weights],
        ],
        [
            ((head_count - 2, HALF, width), BF, VMEM),
            ((width, 3 * columns), F32, VMEM),
            ((columns, width), F32, VMEM),
        ],
        (grad_mid, grad_mid, hidden, packed, probs, *weights),
        flops=37 * 10**8,
        vmem=24,
    )
    late_parts = lax.all_to_all(late, "x", 0, 0)
    piece = jax.ShapeDtypeStruct((9,) + BLOCK, BF)
    in_grad, *pieces = call(
        far_kernel,
        (1,),
        [
            pl.BlockSpec(chunk, lambda i, s: (head_count - 1, 0, 0)),
            whole(far_grad),
            pl.BlockSpec(chunk, lambda i, s: (head_count - 1, 0, 0)),
            whole(far_input),
            whole(labels),
            *[whole(weight) for weight in weights],
            VMEM,
            VMEM,
            VMEM,
            whole(early),
        ],
        [((head_count, HALF, width), BF, VMEM)] + [(piece.shape, BF, whole(piece))] * 4,
        (
            grad_mid, far_grad, chunks_in, far_input, labels, *weights, in_near, qkv_total,
            out_total, early,
        ),
        scratch=[
            pltpu.VMEM((3, width, columns), F32),
            pltpu.VMEM((8 * 32, 128), F32),
            pltpu.VMEM((4, 9) + BLOCK, BF),
        ],
        chosen=x_place,
        vmem=56,
        flops=46 * 10**8,
    )
    in_parts = lax.all_to_all(in_grad, HEAD_AXES, 0, 0)
    moved = [
        lax.ppermute(pieces[k], "x", [(i, (i + k) % 4) for i in range(4)]) for k in range(1, 4)
    ]
    joined = jax.ShapeDtypeStruct((24,) + BLOCK, BF)
    (partial_sum,) = call(
        join_kernel,
        (1,),
        [whole(piece)] * 4 + [whole(late_parts)],
        [(joined.shape, BF, whole(joined))],
        (pieces[0], *moved, late_parts),
        vmem=16,
    )
    summed, summed_b = call(
        sum_kernel,
        (1,),
        [whole(in_parts)],
        [(row_part.shape, F32, whole(row_part)), (row_part.shape, BF, whole(row_part))],
        (in_parts,),
        vmem=16,
    )
    arrived = lax.ppermute(
        summed_b,
        WIN_AXES + HEAD_AXES,
        [(i * head_count, (i + 1) % count * head_count) for i in range(count)],
    )
    received = lax.all_to_all(partial_sum, ("y", "zh"), 0, 0)
    grad_input, ready = call(
        final_kernel,
        (1,),
        [whole(summed), whole(arrived), whole(mid), mine],
        [(row_part.shape, BF, whole(row_part)), (token.shape, F32, whole(token))],
        (summed, arrived, mid, chunks_in),
        chosen=head_place,
        vmem=16,
    )
    owner_block = jax.ShapeDtypeStruct(BLOCK, F32)
    (owned,) = call(
        total_kernel,
        (1,),
        [whole(received), ANY],
        [(BLOCK, F32, whole(owner_block))],
        (received, ready),
        vmem=16,
    )
    return (grad_input, owned.reshape(1, -1))


def solution(mesh):
    fine = Mesh(mesh.devices.reshape(8, 4, 3, 4, 2), WIN_AXES + HEAD_AXES)
    return jax.shard_map(
        shards,
        mesh=fine,
        in_specs=(
            P(WIN_AXES, None),
            P(WIN_AXES, None),
            P(WIN_AXES, None),
            P(WIN_AXES),
            P(None, None, HEAD_AXES),
            P(HEAD_AXES, None),
            P(None, HEAD_AXES),
            P(HEAD_AXES, None),
        ),
        out_specs=(P(WIN_AXES + HEAD_AXES, None), P(HEAD_AXES, WIN_AXES)),
        check_vma=False,
    )
```

```python
import jax
import jax.numpy as jnp
from jax import lax
from jax.experimental import pallas as pl
from jax.experimental.pallas import tpu as pltpu
from jax.sharding import Mesh, PartitionSpec as P

HS = 64
WIN = 144
HALF = 72
WIN_AXES = ("y", "x", "zh")
HEAD_AXES = ("zl", "core")
BLOCK = (32, 128)
EPSILON = 1e-05
BF = jnp.bfloat16
F32 = jnp.float32


def normalize(values):
    data_f = values.astype(F32)
    centred = data_f - jnp.mean(data_f, axis=-1, keepdims=True)
    factor = lax.rsqrt(jnp.mean(centred * centred, axis=-1, keepdims=True) + EPSILON)
    return (centred * factor, factor)


def norm_back(normed, factor, upper):
    inner = upper - jnp.mean(upper, axis=-1, keepdims=True)
    return factor * (inner - normed * jnp.mean(upper * normed, axis=-1, keepdims=True))


def dot(left, right):
    return lax.dot_general(left, right, (((1,), (0,)), ((), ())), preferred_element_type=F32)


def contract_rows(left, right):
    return lax.dot_general(left, right, (((0,), (0,)), ((), ())), preferred_element_type=F32)


def contract_cols(left, right):
    return lax.dot_general(left, right, (((1,), (1,)), ((), ())), preferred_element_type=F32)


VMEM = pl.BlockSpec(memory_space=pltpu.VMEM)
SMEM = pl.BlockSpec(memory_space=pltpu.SMEM)
ANY = pl.BlockSpec(memory_space=pl.ANY)


def call(kernel, grid, ins, outs, args, scratch=(), chosen=None, flops=10**8, vmem=60, aliases=None):
    spec = pltpu.PrefetchScalarGridSpec(
        num_scalar_prefetch=0 if chosen is None else 1,
        grid=grid,
        in_specs=ins,
        out_specs=[out[2] for out in outs],
        scratch_shapes=list(scratch),
    )
    first = () if chosen is None else (chosen,)
    return pl.pallas_call(
        kernel,
        grid_spec=spec,
        out_shape=[jax.ShapeDtypeStruct(out[0], out[1]) for out in outs],
        input_output_aliases=aliases or {},
        compiler_params=pltpu.CompilerParams(vmem_limit_bytes=int(vmem * 2**20)),
        cost_estimate=pl.CostEstimate(flops=flops, bytes_accessed=2 * 2**20, transcendentals=0),
    )(*first, *args)


def whole(array):
    zeros = (0,) * len(array.shape)
    return pl.BlockSpec(array.shape, lambda *_: zeros)


def mlp_kernel(
    stream, grad_out, up_weight, down_weight, unit_grad, late, early, up_sum, down_sum, rows_f32
):
    step = pl.program_id(0)
    unit = normalize(stream[...])[0].astype(BF)
    pre = dot(unit, up_weight[...])
    upper = contract_cols(grad_out[...], down_weight[...])
    scale = 0.7978845608028654
    square = pre * pre
    bent = jnp.tanh(scale * (pre + 0.044715 * (square * pre)))
    slope = 0.5 * (1.0 + bent) + 0.5 * pre * (1.0 - bent * bent) * (
        scale * (1.0 + 3 * 0.044715 * square)
    )
    pre_grad = (upper * slope).astype(BF)
    act = (0.5 * pre * (1.0 + bent)).astype(BF)
    grad = contract_cols(pre_grad, up_weight[...])
    unit_grad[0] = grad[:HALF].astype(BF)
    unit_grad[1] = grad[HALF:].astype(BF)
    up_part = contract_rows(unit, pre_grad)
    down_part = contract_rows(act, grad_out[...])

    @pl.when(step == 0)
    def _():
        up_sum[...] = up_part
        down_sum[...] = down_part

    @pl.when(step > 0)
    def _():
        up_sum[...] += up_part
        down_sum[...] += down_part

    @pl.when(step == pl.num_programs(0) - 1)
    def _():
        base = 0
        for total in (up_sum, down_sum):
            rows, wide = total.shape[0], total.shape[1] // 128
            for column in range(wide):
                rows_f32[pl.ds(base + column, rows, stride=wide), :] = total[
                    :, 128 * column : 128 * column + 128
                ]
            base += rows * wide
        for owner in range(32, 96):
            block = rows_f32[32 * (owner - 32) : 32 * (owner - 31), :].astype(BF)
            if owner < 36:
                early[owner - 32] = block
            else:
                late[owner % 12 // 3, owner // 12 * 3 + owner % 3 - 9] = block


def mlp(stream, grad_out, up_weight, down_weight):
    rows, width = stream.shape
    units = up_weight.shape[1]
    part = lambda columns: pl.BlockSpec((WIN, columns), lambda i: (i, 0))
    late = jax.ShapeDtypeStruct((4, 15) + BLOCK, BF)
    early = jax.ShapeDtypeStruct((4,) + BLOCK, BF)
    return call(
        mlp_kernel,
        (rows // WIN,),
        [part(width), part(width), whole(up_weight), whole(down_weight)],
        [((rows // HALF, HALF, width), BF, pl.BlockSpec((2, HALF, width), lambda i: (i, 0, 0)))]
        + [(late.shape, BF, whole(late)), (early.shape, BF, whole(early))],
        (stream, grad_out, up_weight, down_weight),
        scratch=[
            pltpu.VMEM((width, units), F32),
            pltpu.VMEM((units, width), F32),
            pltpu.VMEM((64 * 32, 128), F32),
        ],
        flops=69 * 10**8,
    )


def window_forward(lead, tail, row, turned_qkv):
    piece = jnp.concatenate([normalize(lead)[0], normalize(tail)[0]], axis=0)
    inputs = piece.astype(BF)
    query, key, value = [
        contract_cols(inputs, turned_qkv[HS * i : HS * i + HS, :]).astype(BF) for i in range(3)
    ]
    row = row.astype(F32)
    column = jnp.broadcast_to(row, (8, WIN)).T[:, :1]
    scores = contract_cols(query, key) * HS**-0.5
    kept = jnp.where(column == row, scores, -jnp.inf)
    raised = jnp.exp(kept - jnp.max(kept, axis=-1, keepdims=True))
    probs = raised / jnp.sum(raised, axis=-1, keepdims=True)
    attended = dot(probs.astype(BF), value).astype(BF)
    return inputs, (query, key, value, attended), probs


def forward_kernel(
    place, lead, tail, labels, turned_qkv, stream, grad_out, hidden, packed, probs_out, own
):
    row = labels[pl.ds(pl.program_id(0), 1), :]
    hidden[0], parts, probs_out[0] = window_forward(lead[0], tail[0], row, turned_qkv)
    packed[0] = jnp.concatenate(parts, axis=1)
    own[0] = stream[0]
    own[1] = grad_out[0]


def last_forward_kernel(
    lead, tail, labels, turned_qkv, _, __, ___, hidden, packed, probs_out, token
):
    row = labels[labels.shape[0] - 1 :, :]
    hidden[0], parts, probs_out[0] = window_forward(lead[0], tail[...], row, turned_qkv)
    packed[0] = jnp.concatenate(parts, axis=1)
    token[...] = jnp.zeros_like(token)


def give_kernel(place, own, far, _, given):
    given[...] = jnp.where(place[0] == 0, far[...].astype(F32), own[...].astype(F32)).astype(BF)


def middle_kernel(parts, own, _, mid, grad_mid, __):
    summed = jnp.sum(parts[...].astype(F32), axis=0)
    normed, factor = normalize(own[0])
    middle = own[1].astype(F32) + norm_back(normed, factor, summed)
    mid[...] = middle
    grad_mid[...] = middle.astype(BF)


def window_back(upper, hidden, parts, probs, turned_qkv, out_weight):
    query, key, value, attended = parts
    attended_grad = contract_cols(upper, out_weight[...]).astype(BF)
    out_grad = contract_rows(attended, upper)
    prob_grad = contract_cols(attended_grad, value)
    inner = prob_grad - jnp.sum(prob_grad * probs, axis=-1, keepdims=True)
    score_grad = (probs * inner * HS**-0.5).astype(BF)
    grads = jnp.concatenate(
        [
            dot(score_grad, key),
            contract_rows(score_grad, query),
            contract_rows(probs.astype(BF), attended_grad),
        ],
        axis=1,
    ).astype(BF)
    return dot(grads, turned_qkv[...]), contract_rows(hidden, grads), out_grad


def backward_kernel(
    place, lead, trail, hidden, packed, probs, turned_qkv, out_weight, early, in_grad, first, second,
    third, fourth, qkv_sum, out_sum, grads, outs, pieces,
):
    step = pl.program_id(0)
    parts = [packed[0][:, HS * i : HS * i + HS] for i in range(4)]
    upper = jnp.concatenate([lead[0].astype(F32), trail[0].astype(F32)], axis=0).astype(BF)
    rows, qkv_part, out_part = window_back(
        upper, hidden[0], parts, probs[0], turned_qkv, out_weight
    )
    in_grad[2 * step + 1] = rows[:HALF].astype(BF)
    in_grad[lax.rem(2 * step + 2, in_grad.shape[0])] = rows[HALF:].astype(BF)

    @pl.when(step == 0)
    def _():
        qkv_sum[...] = qkv_part
        out_sum[...] = out_part

    @pl.when(step > 0)
    def _():
        qkv_sum[...] += qkv_part
        out_sum[...] += out_part

    @pl.when(step == pl.num_programs(0) - 1)
    def _():
        for i in range(3):
            grads[i] = qkv_sum[:, HS * i : HS * i + HS]
        for column in range(out_sum.shape[1] // 128):
            outs[pl.ds(column, HS, stride=4), :] = out_sum[:, 128 * column : 128 * column + 128]
        slots = [lax.rem(x - place[0] + 4, 4) for x in range(4)]
        for owner in range(36):
            if owner < 24:
                kind, start = owner // 8, owner % 8 * 64
                even = grads[kind, pl.ds(start, 32, stride=2), :]
                odd = grads[kind, pl.ds(start + 1, 32, stride=2), :]
                block = jnp.concatenate([even, odd], axis=1).astype(BF)
            elif owner < 32:
                block = outs[32 * (owner - 24) : 32 * (owner - 23), :].astype(BF)
            else:
                block = early[owner - 32]
            pieces[slots[owner % 12 // 3], owner // 12 * 3 + owner % 3] = block
        for slot, out in enumerate((first, second, third, fourth)):
            out[...] = pieces[slot]


def sum_kernel(parts, total, total_b):
    total[...] = jnp.sum(parts[...].astype(F32), axis=0)
    total_b[...] = total[...].astype(BF)


def final_kernel(place, summed, arrived, mid, block_input, grad_input, token):
    total = jnp.where(place[0] == 0, arrived[...].astype(F32), summed[...])
    normed, factor = normalize(block_input[0])
    grad_input[...] = (mid[...] + norm_back(normed, factor, total)).astype(BF)
    token[...] = jnp.zeros_like(token)


def join_kernel(first, second, third, fourth, late, joined):
    count = first.shape[0]
    near = (first[...].astype(F32) + second[...].astype(F32)) + (
        third[...].astype(F32) + fourth[...].astype(F32)
    )
    joined[:count] = near.astype(BF)
    joined[count:] = jnp.sum(late[...].astype(F32), axis=0).astype(BF)


def total_kernel(received, _, owned):
    owned[...] = jnp.sum(received[...].astype(F32), axis=0)


def shards(block_input, stream, grad_out, regions, qkv_weight, out_weight, up_weight, down_weight):
    rows, width = block_input.shape
    windows = rows // WIN
    head_count = lax.axis_size(HEAD_AXES)
    share_rows = rows // head_count
    head = lax.axis_index(HEAD_AXES)
    columns = qkv_weight.shape[2]
    count = lax.axis_size(WIN_AXES)
    head_place = head.astype(jnp.int32).reshape(1)
    x_place = lax.axis_index("x").astype(jnp.int32).reshape(1)
    chunk = (1, HALF, width)
    chunked = [array.reshape(-1, HALF, width) for array in (block_input, stream, grad_out)]
    chunks_in, chunks_mid, chunks_out = chunked
    turned_qkv = jnp.swapaxes(qkv_weight, 1, 2)

    def from_next(values):
        return lax.ppermute(values, WIN_AXES, [((i + 1) % count, i) for i in range(count)])

    far_input = from_next(block_input[:HALF])
    unit_grad, late, early = mlp(stream, grad_out, up_weight, down_weight)
    parts = lax.all_to_all(unit_grad, HEAD_AXES, 0, 0)
    labels = regions.reshape(windows, WIN)
    window = lambda columns: pl.BlockSpec((1, WIN, columns), lambda i, *_: (i, 0, 0))
    weights = (turned_qkv.reshape(-1, width), out_weight)
    token = jax.ShapeDtypeStruct((8, 128), F32)
    row_part = jax.ShapeDtypeStruct((share_rows, width), BF)
    mine = pl.BlockSpec(chunk, lambda i, place: (place[0], 0, 0))
    own_rows = jax.ShapeDtypeStruct((2, share_rows, width), BF)
    hidden, packed, probs, own = call(
        forward_kernel,
        (windows - 1,),
        [
            pl.BlockSpec(chunk, lambda i, _: (2 * i + 1, 0, 0)),
            pl.BlockSpec(chunk, lambda i, _: (2 * i + 2, 0, 0)),
            whole(labels),
            whole(weights[0]),
            mine,
            mine,
        ],
        [
            ((windows, WIN, width), BF, window(width)),
            ((windows, WIN, 4 * columns), BF, window(4 * columns)),
            ((windows, WIN, WIN), F32, window(WIN)),
            (own_rows.shape, BF, whole(own_rows)),
        ],
        (chunks_in, chunks_in, labels, weights[0], chunks_mid, chunks_out),
        chosen=head_place,
        flops=53 * 10**8,
    )
    mid, own_grad_mid, late = call(
        middle_kernel,
        (1,),
        [whole(parts), whole(own), ANY],
        [
            (row_part.shape, F32, whole(row_part)),
            (row_part.shape, BF, whole(row_part)),
            (late.shape, BF, ANY),
        ],
        (parts, own, late),
        aliases={2: 2},
        vmem=16,
    )
    far_grad = lax.ppermute(
        own_grad_mid,
        WIN_AXES + HEAD_AXES,
        [((i + 1) % count * head_count, i * head_count) for i in range(count)],
    )
    late_parts = lax.all_to_all(late, "x", 0, 0)
    final = lambda columns: pl.BlockSpec((1, WIN, columns), lambda i: (windows - 1, 0, 0))
    hidden, packed, probs, done = call(
        last_forward_kernel,
        (1,),
        [
            pl.BlockSpec(chunk, lambda i: (head_count - 1, 0, 0)),
            whole(far_input),
            whole(labels),
            whole(weights[0]),
            ANY,
            ANY,
            ANY,
        ],
        [
            (hidden.shape, BF, final(width)),
            (packed.shape, BF, final(4 * columns)),
            (probs.shape, F32, final(WIN)),
            (token.shape, F32, whole(token)),
        ],
        (chunks_in, far_input, labels, weights[0], hidden, packed, probs),
        aliases={4: 0, 5: 1, 6: 2},
        flops=20 * 10**8,
    )
    (given,) = call(
        give_kernel,
        (1,),
        [whole(own_grad_mid), whole(far_grad), ANY],
        [(row_part.shape, BF, whole(row_part))],
        (own_grad_mid, far_grad, done),
        chosen=head_place,
        vmem=16,
    )
    grad_mid = lax.all_gather(given, HEAD_AXES, axis=0)
    piece = jax.ShapeDtypeStruct((9,) + BLOCK, BF)
    in_rows = jax.ShapeDtypeStruct((head_count, HALF, width), BF)
    in_grad, *pieces = call(
        backward_kernel,
        (windows,),
        [
            pl.BlockSpec(chunk, lambda i, _: (2 * i + 1, 0, 0)),
            pl.BlockSpec(chunk, lambda i, _: (lax.rem(2 * i + 2, head_count), 0, 0)),
            window(width),
            window(4 * columns),
            window(WIN),
            *[whole(weight) for weight in weights],
            whole(early),
        ],
        [(in_rows.shape, BF, whole(in_rows))] + [(piece.shape, BF, whole(piece))] * 4,
        (grad_mid, grad_mid, hidden, packed, probs, *weights, early),
        scratch=[
            pltpu.VMEM((width, 3 * columns), F32),
            pltpu.VMEM((columns, width), F32),
            pltpu.VMEM((3, width, columns), F32),
            pltpu.VMEM((8 * 32, 128), F32),
            pltpu.VMEM((4, 9) + BLOCK, BF),
        ],
        chosen=x_place,
        vmem=24,
        flops=70 * 10**8,
    )
    in_parts = lax.all_to_all(in_grad, HEAD_AXES, 0, 0)
    moved = [
        lax.ppermute(pieces[k], "x", [(i, (i + k) % 4) for i in range(4)]) for k in range(1, 4)
    ]
    joined = jax.ShapeDtypeStruct((24,) + BLOCK, BF)
    (partial_sum,) = call(
        join_kernel,
        (1,),
        [whole(piece)] * 4 + [whole(late_parts)],
        [(joined.shape, BF, whole(joined))],
        (pieces[0], *moved, late_parts),
        vmem=16,
    )
    summed, summed_b = call(
        sum_kernel,
        (1,),
        [whole(in_parts)],
        [(row_part.shape, F32, whole(row_part)), (row_part.shape, BF, whole(row_part))],
        (in_parts,),
        vmem=16,
    )
    arrived = lax.ppermute(
        summed_b,
        WIN_AXES + HEAD_AXES,
        [(i * head_count, (i + 1) % count * head_count) for i in range(count)],
    )
    received = lax.all_to_all(partial_sum, ("y", "zh"), 0, 0)
    grad_input, ready = call(
        final_kernel,
        (1,),
        [whole(summed), whole(arrived), whole(mid), mine],
        [(row_part.shape, BF, whole(row_part)), (token.shape, F32, whole(token))],
        (summed, arrived, mid, chunks_in),
        chosen=head_place,
        vmem=16,
    )
    owner_block = jax.ShapeDtypeStruct(BLOCK, F32)
    (owned,) = call(
        total_kernel,
        (1,),
        [whole(received), ANY],
        [(BLOCK, F32, whole(owner_block))],
        (received, ready),
        vmem=16,
    )
    return (grad_input, owned.reshape(1, -1))


def solution(mesh):
    fine = Mesh(mesh.devices.reshape(8, 4, 3, 4, 2), WIN_AXES + HEAD_AXES)
    return jax.shard_map(
        shards,
        mesh=fine,
        in_specs=(
            P(WIN_AXES, None),
            P(WIN_AXES, None),
            P(WIN_AXES, None),
            P(WIN_AXES),
            P(None, None, HEAD_AXES),
            P(HEAD_AXES, None),
            P(None, HEAD_AXES),
            P(HEAD_AXES, None),
        ),
        out_specs=(P(WIN_AXES + HEAD_AXES, None), P(HEAD_AXES, WIN_AXES)),
        check_vma=False,
    )
```

```python
import jax
import jax.numpy as jnp
from jax import lax
from jax.experimental import pallas as pl
from jax.experimental.pallas import tpu as pltpu
from jax.sharding import Mesh, PartitionSpec as P

HS = 64
WIN = 144
HALF = 72
WIN_AXES = ("y", "x", "zh")
HEAD_AXES = ("zl", "core")
BLOCK = (32, 128)
EPSILON = 1e-05
BF = jnp.bfloat16
F32 = jnp.float32


def normalize(values):
    data_f = values.astype(F32)
    centred = data_f - jnp.mean(data_f, axis=-1, keepdims=True)
    factor = lax.rsqrt(jnp.mean(centred * centred, axis=-1, keepdims=True) + EPSILON)
    return (centred * factor, factor)


def norm_back(normed, factor, upper):
    inner = upper - jnp.mean(upper, axis=-1, keepdims=True)
    return factor * (inner - normed * jnp.mean(upper * normed, axis=-1, keepdims=True))


def dot(left, right):
    return lax.dot_general(left, right, (((1,), (0,)), ((), ())), preferred_element_type=F32)


def contract_rows(left, right):
    return lax.dot_general(left, right, (((0,), (0,)), ((), ())), preferred_element_type=F32)


def contract_cols(left, right):
    return lax.dot_general(left, right, (((1,), (1,)), ((), ())), preferred_element_type=F32)


VMEM = pl.BlockSpec(memory_space=pltpu.VMEM)
SMEM = pl.BlockSpec(memory_space=pltpu.SMEM)
ANY = pl.BlockSpec(memory_space=pl.ANY)


def call(kernel, grid, ins, outs, args, scratch=(), chosen=None, flops=10**8, vmem=60, aliases=None):
    spec = pltpu.PrefetchScalarGridSpec(
        num_scalar_prefetch=0 if chosen is None else 1,
        grid=grid,
        in_specs=ins,
        out_specs=[out[2] for out in outs],
        scratch_shapes=list(scratch),
    )
    first = () if chosen is None else (chosen,)
    return pl.pallas_call(
        kernel,
        grid_spec=spec,
        out_shape=[jax.ShapeDtypeStruct(out[0], out[1]) for out in outs],
        input_output_aliases=aliases or {},
        compiler_params=pltpu.CompilerParams(vmem_limit_bytes=int(vmem * 2**20)),
        cost_estimate=pl.CostEstimate(flops=flops, bytes_accessed=2 * 2**20, transcendentals=0),
    )(*first, *args)


def whole(array):
    zeros = (0,) * len(array.shape)
    return pl.BlockSpec(array.shape, lambda *_: zeros)


def mlp_kernel(
    stream, grad_out, up_weight, down_weight, unit_grad, late, early, up_sum, down_sum, rows_f32
):
    step = pl.program_id(0)
    unit = normalize(stream[...])[0].astype(BF)
    pre = dot(unit, up_weight[...])
    upper = contract_cols(grad_out[...], down_weight[...])
    scale = 0.7978845608028654
    square = pre * pre
    bent = jnp.tanh(scale * (pre + 0.044715 * (square * pre)))
    slope = 0.5 * (1.0 + bent) + 0.5 * pre * (1.0 - bent * bent) * (
        scale * (1.0 + 3 * 0.044715 * square)
    )
    pre_grad = (upper * slope).astype(BF)
    act = (0.5 * pre * (1.0 + bent)).astype(BF)
    grad = contract_cols(pre_grad, up_weight[...])
    unit_grad[0] = grad[:HALF].astype(BF)
    unit_grad[1] = grad[HALF:].astype(BF)
    up_part = contract_rows(unit, pre_grad)
    down_part = contract_rows(act, grad_out[...])

    @pl.when(step == 0)
    def _():
        up_sum[...] = up_part
        down_sum[...] = down_part

    @pl.when(step > 0)
    def _():
        up_sum[...] += up_part
        down_sum[...] += down_part

    @pl.when(step == pl.num_programs(0) - 1)
    def _():
        base = 0
        for total in (up_sum, down_sum):
            rows, wide = total.shape[0], total.shape[1] // 128
            for column in range(wide):
                rows_f32[pl.ds(base + column, rows, stride=wide), :] = total[
                    :, 128 * column : 128 * column + 128
                ]
            base += rows * wide
        for owner in range(32, 96):
            block = rows_f32[32 * (owner - 32) : 32 * (owner - 31), :].astype(BF)
            if owner < 36:
                early[owner - 32] = block
            else:
                late[owner % 12 // 3, owner // 12 * 3 + owner % 3 - 9] = block


def mlp(stream, grad_out, up_weight, down_weight):
    rows, width = stream.shape
    units = up_weight.shape[1]
    part = lambda columns: pl.BlockSpec((WIN, columns), lambda i: (i, 0))
    late = jax.ShapeDtypeStruct((4, 15) + BLOCK, BF)
    early = jax.ShapeDtypeStruct((4,) + BLOCK, BF)
    return call(
        mlp_kernel,
        (rows // WIN,),
        [part(width), part(width), whole(up_weight), whole(down_weight)],
        [((rows // HALF, HALF, width), BF, pl.BlockSpec((2, HALF, width), lambda i: (i, 0, 0)))]
        + [(late.shape, BF, whole(late)), (early.shape, BF, whole(early))],
        (stream, grad_out, up_weight, down_weight),
        scratch=[
            pltpu.VMEM((width, units), F32),
            pltpu.VMEM((units, width), F32),
            pltpu.VMEM((64 * 32, 128), F32),
        ],
        flops=69 * 10**8,
    )


def window_forward(lead, tail, row, turned_qkv):
    piece = jnp.concatenate([normalize(lead)[0], normalize(tail)[0]], axis=0)
    inputs = piece.astype(BF)
    query, key, value = [
        contract_cols(inputs, turned_qkv[HS * i : HS * i + HS, :]).astype(BF) for i in range(3)
    ]
    row = row.astype(F32)
    column = jnp.broadcast_to(row, (8, WIN)).T[:, :1]
    scores = contract_cols(query, key) * HS**-0.5
    kept = jnp.where(column == row, scores, -jnp.inf)
    raised = jnp.exp(kept - jnp.max(kept, axis=-1, keepdims=True))
    probs = raised / jnp.sum(raised, axis=-1, keepdims=True)
    attended = dot(probs.astype(BF), value).astype(BF)
    return inputs, (query, key, value, attended), probs


def forward_kernel(
    place, lead, trail, far, labels, turned_qkv, stream, grad_out, hidden, packed, probs_out, own
):
    step = pl.program_id(0)
    tail = jnp.where(step == pl.num_programs(0) - 1, far[...].astype(F32), trail[0].astype(F32))
    row = labels[pl.ds(step, 1), :]
    hidden[0], parts, probs_out[0] = window_forward(lead[0], tail, row, turned_qkv)
    packed[0] = jnp.concatenate(parts, axis=1)
    own[0] = stream[0]
    own[1] = grad_out[0]


def give_kernel(place, own, far, given):
    given[...] = jnp.where(place[0] == 0, far[...].astype(F32), own[...].astype(F32)).astype(BF)


def gate_kernel(_, __, ___):
    pass


def middle_kernel(parts, own, mid, grad_mid):
    summed = jnp.sum(parts[...].astype(F32), axis=0)
    normed, factor = normalize(own[0])
    middle = own[1].astype(F32) + norm_back(normed, factor, summed)
    mid[...] = middle
    grad_mid[...] = middle.astype(BF)


def window_back(upper, hidden, parts, probs, turned_qkv, out_weight):
    query, key, value, attended = parts
    attended_grad = contract_cols(upper, out_weight[...]).astype(BF)
    out_grad = contract_rows(attended, upper)
    prob_grad = contract_cols(attended_grad, value)
    inner = prob_grad - jnp.sum(prob_grad * probs, axis=-1, keepdims=True)
    score_grad = (probs * inner * HS**-0.5).astype(BF)
    grads = jnp.concatenate(
        [
            dot(score_grad, key),
            contract_rows(score_grad, query),
            contract_rows(probs.astype(BF), attended_grad),
        ],
        axis=1,
    ).astype(BF)
    return dot(grads, turned_qkv[...]), contract_rows(hidden, grads), out_grad


def backward_kernel(
    place, lead, trail, hidden, packed, probs, turned_qkv, out_weight, early, late, in_grad, first,
    second, third, fourth, qkv_sum, out_sum, grads, outs, pieces,
):
    step = pl.program_id(0)
    parts = [packed[0][:, HS * i : HS * i + HS] for i in range(4)]
    upper = jnp.concatenate([lead[0].astype(F32), trail[0].astype(F32)], axis=0).astype(BF)
    rows, qkv_part, out_part = window_back(
        upper, hidden[0], parts, probs[0], turned_qkv, out_weight
    )
    in_grad[2 * step + 1] = rows[:HALF].astype(BF)
    in_grad[lax.rem(2 * step + 2, in_grad.shape[0])] = rows[HALF:].astype(BF)

    @pl.when(step == 0)
    def _():
        qkv_sum[...] = qkv_part
        out_sum[...] = out_part

    @pl.when(step > 0)
    def _():
        qkv_sum[...] += qkv_part
        out_sum[...] += out_part

    @pl.when(step == pl.num_programs(0) - 1)
    def _():
        for i in range(3):
            grads[i] = qkv_sum[:, HS * i : HS * i + HS]
        for column in range(out_sum.shape[1] // 128):
            outs[pl.ds(column, HS, stride=4), :] = out_sum[:, 128 * column : 128 * column + 128]
        slots = [lax.rem(x - place[0] + 4, 4) for x in range(4)]
        for owner in range(36):
            if owner < 24:
                kind, start = owner // 8, owner % 8 * 64
                even = grads[kind, pl.ds(start, 32, stride=2), :]
                odd = grads[kind, pl.ds(start + 1, 32, stride=2), :]
                block = jnp.concatenate([even, odd], axis=1).astype(BF)
            elif owner < 32:
                block = outs[32 * (owner - 24) : 32 * (owner - 23), :].astype(BF)
            else:
                block = early[owner - 32]
            pieces[slots[owner % 12 // 3], owner // 12 * 3 + owner % 3] = block
        for x in range(4):
            for index in range(late.shape[1]):
                pieces[slots[x], 9 + index] = late[x, index]
        for slot, out in enumerate((first, second, third, fourth)):
            out[...] = pieces[slot]


def sum_kernel(parts, total, total_b):
    total[...] = jnp.sum(parts[...].astype(F32), axis=0)
    total_b[...] = total[...].astype(BF)


def final_kernel(place, summed, arrived, mid, block_input, grad_input, token):
    total = jnp.where(place[0] == 0, arrived[...].astype(F32), summed[...])
    normed, factor = normalize(block_input[0])
    grad_input[...] = (mid[...] + norm_back(normed, factor, total)).astype(BF)
    token[...] = jnp.zeros_like(token)


def join_kernel(first, second, third, fourth, joined):
    total = (first[...].astype(F32) + second[...].astype(F32)) + (
        third[...].astype(F32) + fourth[...].astype(F32)
    )
    joined[...] = total.astype(BF)


def total_kernel(received, _, owned):
    owned[...] = jnp.sum(received[...].astype(F32), axis=0)


def shards(block_input, stream, grad_out, regions, qkv_weight, out_weight, up_weight, down_weight):
    rows, width = block_input.shape
    windows = rows // WIN
    head_count = lax.axis_size(HEAD_AXES)
    share_rows = rows // head_count
    head = lax.axis_index(HEAD_AXES)
    columns = qkv_weight.shape[2]
    count = lax.axis_size(WIN_AXES)
    head_place = head.astype(jnp.int32).reshape(1)
    x_place = lax.axis_index("x").astype(jnp.int32).reshape(1)
    chunk = (1, HALF, width)
    chunked = [array.reshape(-1, HALF, width) for array in (block_input, stream, grad_out)]
    chunks_in, chunks_mid, chunks_out = chunked
    turned_qkv = jnp.swapaxes(qkv_weight, 1, 2)

    def from_next(values):
        return lax.ppermute(values, WIN_AXES, [((i + 1) % count, i) for i in range(count)])

    far_input = from_next(block_input[:HALF])
    unit_grad, late, early = mlp(stream, grad_out, up_weight, down_weight)
    (unit_grad,) = call(
        gate_kernel,
        (1,),
        [ANY, ANY],
        [(unit_grad.shape, BF, ANY)],
        (unit_grad, far_input),
        aliases={0: 0},
        vmem=60,
    )
    parts = lax.all_to_all(unit_grad, HEAD_AXES, 0, 0)
    labels = regions.reshape(windows, WIN)
    window = lambda columns: pl.BlockSpec((1, WIN, columns), lambda i, *_: (i, 0, 0))
    weights = (turned_qkv.reshape(-1, width), out_weight)
    token = jax.ShapeDtypeStruct((8, 128), F32)
    row_part = jax.ShapeDtypeStruct((share_rows, width), BF)
    mine = pl.BlockSpec(chunk, lambda i, place: (place[0], 0, 0))
    own_rows = jax.ShapeDtypeStruct((2, share_rows, width), BF)
    hidden, packed, probs, own = call(
        forward_kernel,
        (windows,),
        [
            pl.BlockSpec(chunk, lambda i, _: (2 * i + 1, 0, 0)),
            pl.BlockSpec(chunk, lambda i, _: (jnp.minimum(2 * i + 2, head_count - 1), 0, 0)),
            whole(far_input),
            whole(labels),
            whole(weights[0]),
            mine,
            mine,
        ],
        [
            ((windows, WIN, width), BF, window(width)),
            ((windows, WIN, 4 * columns), BF, window(4 * columns)),
            ((windows, WIN, WIN), F32, window(WIN)),
            (own_rows.shape, BF, whole(own_rows)),
        ],
        (chunks_in, chunks_in, far_input, labels, weights[0], chunks_mid, chunks_out),
        chosen=head_place,
        flops=53 * 10**8,
    )
    mid, own_grad_mid = call(
        middle_kernel,
        (1,),
        [whole(parts), whole(own)],
        [(row_part.shape, F32, whole(row_part)), (row_part.shape, BF, whole(row_part))],
        (parts, own),
        vmem=16,
    )
    far_grad = lax.ppermute(
        own_grad_mid,
        WIN_AXES + HEAD_AXES,
        [((i + 1) % count * head_count, i * head_count) for i in range(count)],
    )
    (given,) = call(
        give_kernel,
        (1,),
        [whole(own_grad_mid), whole(far_grad)],
        [(row_part.shape, BF, whole(row_part))],
        (own_grad_mid, far_grad),
        chosen=head_place,
        vmem=16,
    )
    grad_mid = lax.all_gather(given, HEAD_AXES, axis=0)
    piece = jax.ShapeDtypeStruct((24,) + BLOCK, BF)
    in_rows = jax.ShapeDtypeStruct((head_count, HALF, width), BF)
    in_grad, *pieces = call(
        backward_kernel,
        (windows,),
        [
            pl.BlockSpec(chunk, lambda i, _: (2 * i + 1, 0, 0)),
            pl.BlockSpec(chunk, lambda i, _: (lax.rem(2 * i + 2, head_count), 0, 0)),
            window(width),
            window(4 * columns),
            window(WIN),
            *[whole(weight) for weight in weights],
            whole(early),
            whole(late),
        ],
        [(in_rows.shape, BF, whole(in_rows))] + [(piece.shape, BF, whole(piece))] * 4,
        (grad_mid, grad_mid, hidden, packed, probs, *weights, early, late),
        scratch=[
            pltpu.VMEM((width, 3 * columns), F32),
            pltpu.VMEM((columns, width), F32),
            pltpu.VMEM((3, width, columns), F32),
            pltpu.VMEM((8 * 32, 128), F32),
            pltpu.VMEM((4, 24) + BLOCK, BF),
        ],
        chosen=x_place,
        vmem=24,
        flops=70 * 10**8,
    )
    in_parts = lax.all_to_all(in_grad, HEAD_AXES, 0, 0)
    moved = [
        lax.ppermute(pieces[k], "x", [(i, (i + k) % 4) for i in range(4)]) for k in range(1, 4)
    ]
    (partial_sum,) = call(
        join_kernel,
        (1,),
        [whole(piece)] * 4,
        [(piece.shape, BF, whole(piece))],
        (pieces[0], *moved),
        vmem=16,
    )
    summed, summed_b = call(
        sum_kernel,
        (1,),
        [whole(in_parts)],
        [(row_part.shape, F32, whole(row_part)), (row_part.shape, BF, whole(row_part))],
        (in_parts,),
        vmem=16,
    )
    arrived = lax.ppermute(
        summed_b,
        WIN_AXES + HEAD_AXES,
        [(i * head_count, (i + 1) % count * head_count) for i in range(count)],
    )
    received = lax.all_to_all(partial_sum, ("y", "zh"), 0, 0)
    grad_input, ready = call(
        final_kernel,
        (1,),
        [whole(summed), whole(arrived), whole(mid), mine],
        [(row_part.shape, BF, whole(row_part)), (token.shape, F32, whole(token))],
        (summed, arrived, mid, chunks_in),
        chosen=head_place,
        vmem=16,
    )
    owner_block = jax.ShapeDtypeStruct(BLOCK, F32)
    (owned,) = call(
        total_kernel,
        (1,),
        [whole(received), ANY],
        [(BLOCK, F32, whole(owner_block))],
        (received, ready),
        vmem=16,
    )
    return (grad_input, owned.reshape(1, -1))


def solution(mesh):
    fine = Mesh(mesh.devices.reshape(8, 4, 3, 4, 2), WIN_AXES + HEAD_AXES)
    return jax.shard_map(
        shards,
        mesh=fine,
        in_specs=(
            P(WIN_AXES, None),
            P(WIN_AXES, None),
            P(WIN_AXES, None),
            P(WIN_AXES),
            P(None, None, HEAD_AXES),
            P(HEAD_AXES, None),
            P(None, HEAD_AXES),
            P(HEAD_AXES, None),
        ),
        out_specs=(P(WIN_AXES + HEAD_AXES, None), P(HEAD_AXES, WIN_AXES)),
        check_vma=False,
    )
```

```python
import jax
import jax.numpy as jnp
from jax import lax
from jax.experimental import pallas as pl
from jax.experimental.pallas import tpu as pltpu
from jax.sharding import Mesh, PartitionSpec as P

HS = 64
WIN = 144
HALF = 72
WIN_AXES = ("y", "x", "zh")
HEAD_AXES = ("zl", "core")
BLOCK = (32, 128)
EPSILON = 1e-05
BF = jnp.bfloat16
F32 = jnp.float32


def normalize(values):
    data_f = values.astype(F32)
    centred = data_f - jnp.mean(data_f, axis=-1, keepdims=True)
    factor = lax.rsqrt(jnp.mean(centred * centred, axis=-1, keepdims=True) + EPSILON)
    return (centred * factor, factor)


def norm_back(normed, factor, upper):
    inner = upper - jnp.mean(upper, axis=-1, keepdims=True)
    return factor * (inner - normed * jnp.mean(upper * normed, axis=-1, keepdims=True))


def dot(left, right):
    return lax.dot_general(left, right, (((1,), (0,)), ((), ())), preferred_element_type=F32)


def contract_rows(left, right):
    return lax.dot_general(left, right, (((0,), (0,)), ((), ())), preferred_element_type=F32)


def contract_cols(left, right):
    return lax.dot_general(left, right, (((1,), (1,)), ((), ())), preferred_element_type=F32)


VMEM = pl.BlockSpec(memory_space=pltpu.VMEM)
SMEM = pl.BlockSpec(memory_space=pltpu.SMEM)
ANY = pl.BlockSpec(memory_space=pl.ANY)


def call(kernel, grid, ins, outs, args, scratch=(), chosen=None, flops=10**8, vmem=60, aliases=None):
    spec = pltpu.PrefetchScalarGridSpec(
        num_scalar_prefetch=0 if chosen is None else 1,
        grid=grid,
        in_specs=ins,
        out_specs=[out[2] for out in outs],
        scratch_shapes=list(scratch),
    )
    first = () if chosen is None else (chosen,)
    return pl.pallas_call(
        kernel,
        grid_spec=spec,
        out_shape=[jax.ShapeDtypeStruct(out[0], out[1]) for out in outs],
        input_output_aliases=aliases or {},
        compiler_params=pltpu.CompilerParams(vmem_limit_bytes=int(vmem * 2**20)),
        cost_estimate=pl.CostEstimate(flops=flops, bytes_accessed=2 * 2**20, transcendentals=0),
    )(*first, *args)


def whole(array):
    zeros = (0,) * len(array.shape)
    return pl.BlockSpec(array.shape, lambda *_: zeros)


def mlp_kernel(
    place, stream, grad_out, up_weight, down_weight, keep, give, late, early, up_sum, down_sum,
    rows_f32,
):
    step = pl.program_id(0)
    unit = normalize(stream[...])[0].astype(BF)
    pre = dot(unit, up_weight[...])
    upper = contract_cols(grad_out[...], down_weight[...])
    scale = 0.7978845608028654
    square = pre * pre
    bent = jnp.tanh(scale * (pre + 0.044715 * (square * pre)))
    slope = 0.5 * (1.0 + bent) + 0.5 * pre * (1.0 - bent * bent) * (
        scale * (1.0 + 3 * 0.044715 * square)
    )
    pre_grad = (upper * slope).astype(BF)
    act = (0.5 * pre * (1.0 + bent)).astype(BF)
    grad = contract_cols(pre_grad, up_weight[...])
    even = place[0] == 0
    keep[0] = jnp.where(even, grad[:HALF], grad[HALF:]).astype(BF)
    give[0] = jnp.where(even, grad[HALF:], grad[:HALF]).astype(BF)
    up_part = contract_rows(unit, pre_grad)
    down_part = contract_rows(act, grad_out[...])

    @pl.when(step == 0)
    def _():
        up_sum[...] = up_part
        down_sum[...] = down_part

    @pl.when(step > 0)
    def _():
        up_sum[...] += up_part
        down_sum[...] += down_part

    @pl.when(step == pl.num_programs(0) - 1)
    def _():
        base = 0
        for total in (up_sum, down_sum):
            rows, wide = total.shape[0], total.shape[1] // 128
            for column in range(wide):
                rows_f32[pl.ds(base + column, rows, stride=wide), :] = total[
                    :, 128 * column : 128 * column + 128
                ]
            base += rows * wide
        for owner in range(32, 96):
            block = rows_f32[32 * (owner - 32) : 32 * (owner - 31), :].astype(BF)
            if owner < 36:
                early[owner - 32] = block
            else:
                late[owner % 12 // 3 * 15 + owner // 12 * 3 + owner % 3 - 9] = block


def mlp(place, stream, grad_out, up_weight, down_weight):
    rows, width = stream.shape
    units = up_weight.shape[1]
    part = lambda columns: pl.BlockSpec((WIN, columns), lambda i, _: (i, 0))
    late = jax.ShapeDtypeStruct((60,) + BLOCK, BF)
    early = jax.ShapeDtypeStruct((4,) + BLOCK, BF)
    return call(
        mlp_kernel,
        (rows // WIN,),
        [part(width), part(width), whole(up_weight), whole(down_weight)],
        [((rows // WIN, HALF, width), BF, pl.BlockSpec((1, HALF, width), lambda i, _: (i, 0, 0)))] * 2
        + [(late.shape, BF, whole(late)), (early.shape, BF, whole(early))],
        (stream, grad_out, up_weight, down_weight),
        scratch=[
            pltpu.VMEM((width, units), F32),
            pltpu.VMEM((units, width), F32),
            pltpu.VMEM((64 * 32, 128), F32),
        ],
        chosen=place,
        flops=69 * 10**8,
    )


def window_forward(lead, tail, row, turned_qkv):
    piece = jnp.concatenate([normalize(lead)[0], normalize(tail)[0]], axis=0)
    inputs = piece.astype(BF)
    query, key, value = [
        contract_cols(inputs, turned_qkv[HS * i : HS * i + HS, :]).astype(BF) for i in range(3)
    ]
    row = row.astype(F32)
    column = jnp.broadcast_to(row, (8, WIN)).T[:, :1]
    scores = contract_cols(query, key) * HS**-0.5
    kept = jnp.where(column == row, scores, -jnp.inf)
    raised = jnp.exp(kept - jnp.max(kept, axis=-1, keepdims=True))
    probs = raised / jnp.sum(raised, axis=-1, keepdims=True)
    attended = dot(probs.astype(BF), value).astype(BF)
    return inputs, (query, key, value, attended), probs


def forward_kernel(
    place, lead, tail, labels, turned_qkv, stream, grad_out, hidden, packed, probs_out, own
):
    row = labels[pl.ds(pl.program_id(0), 1), :]
    hidden[0], parts, probs_out[0] = window_forward(lead[0], tail[0], row, turned_qkv)
    packed[0] = jnp.concatenate(parts, axis=1)
    own[0] = stream[0]
    own[1] = grad_out[0]


def last_forward_kernel(
    lead, tail, labels, turned_qkv, hidden, packed, probs_out, token
):
    row = labels[labels.shape[0] - 1 :, :]
    hidden[0], parts, probs_out[0] = window_forward(lead[0], tail[...], row, turned_qkv)
    packed[0] = jnp.concatenate(parts, axis=1)
    token[...] = jnp.zeros_like(token)


def give_kernel(place, own, far, _, given):
    given[...] = jnp.where(place[0] == 0, far[...].astype(F32), own[...].astype(F32)).astype(BF)


def pair_kernel(keep, taken, pair):
    pair[...] = (keep[...].astype(F32) + taken[...].astype(F32)).astype(BF)


def middle_kernel(parts, own, mid, grad_mid):
    summed = jnp.sum(parts[...].astype(F32), axis=0)
    normed, factor = normalize(own[0])
    middle = own[1].astype(F32) + norm_back(normed, factor, summed)
    mid[...] = middle
    grad_mid[...] = middle.astype(BF)


def window_back(upper, hidden, parts, probs, turned_qkv, out_weight):
    query, key, value, attended = parts
    attended_grad = contract_cols(upper, out_weight[...]).astype(BF)
    out_grad = contract_rows(attended, upper)
    prob_grad = contract_cols(attended_grad, value)
    inner = prob_grad - jnp.sum(prob_grad * probs, axis=-1, keepdims=True)
    score_grad = (probs * inner * HS**-0.5).astype(BF)
    grads = jnp.concatenate(
        [
            dot(score_grad, key),
            contract_rows(score_grad, query),
            contract_rows(probs.astype(BF), attended_grad),
        ],
        axis=1,
    ).astype(BF)
    return dot(grads, turned_qkv[...]), contract_rows(hidden, grads), out_grad


def backward_kernel(
    place, lead, trail, hidden, packed, probs, last_hidden, last_packed, last_probs, turned_qkv,
    out_weight, early, _, in_grad, first, second, third, fourth, qkv_sum, out_sum, grads, outs, pieces,
):
    step = pl.program_id(0)
    last = step == pl.num_programs(0) - 1
    saved = jnp.where(last, last_packed[0].astype(F32), packed[0].astype(F32)).astype(BF)
    parts = [saved[:, HS * i : HS * i + HS] for i in range(4)]
    inputs = jnp.where(last, last_hidden[0].astype(F32), hidden[0].astype(F32)).astype(BF)
    upper = jnp.concatenate([lead[0].astype(F32), trail[0].astype(F32)], axis=0).astype(BF)
    rows, qkv_part, out_part = window_back(
        upper, inputs, parts, jnp.where(last, last_probs[0], probs[0]), turned_qkv, out_weight
    )
    in_grad[2 * step + 1] = rows[:HALF].astype(BF)
    in_grad[lax.rem(2 * step + 2, in_grad.shape[0])] = rows[HALF:].astype(BF)

    @pl.when(step == 0)
    def _():
        qkv_sum[...] = qkv_part
        out_sum[...] = out_part

    @pl.when(step > 0)
    def _():
        qkv_sum[...] += qkv_part
        out_sum[...] += out_part

    @pl.when(step == pl.num_programs(0) - 1)
    def _():
        for i in range(3):
            grads[i] = qkv_sum[:, HS * i : HS * i + HS]
        for column in range(out_sum.shape[1] // 128):
            outs[pl.ds(column, HS, stride=4), :] = out_sum[:, 128 * column : 128 * column + 128]
        slots = [lax.rem(x - place[0] + 4, 4) for x in range(4)]
        for owner in range(36):
            if owner < 24:
                kind, start = owner // 8, owner % 8 * 64
                even = grads[kind, pl.ds(start, 32, stride=2), :]
                odd = grads[kind, pl.ds(start + 1, 32, stride=2), :]
                block = jnp.concatenate([even, odd], axis=1).astype(BF)
            elif owner < 32:
                block = outs[32 * (owner - 24) : 32 * (owner - 23), :].astype(BF)
            else:
                block = early[owner - 32]
            pieces[slots[owner % 12 // 3], owner // 12 * 3 + owner % 3] = block
        for slot, out in enumerate((first, second, third, fourth)):
            out[...] = pieces[slot]


def sum_kernel(parts, total, total_b):
    total[...] = jnp.sum(parts[...].astype(F32), axis=0)
    total_b[...] = total[...].astype(BF)


def final_kernel(place, summed, arrived, mid, block_input, grad_input, token):
    total = jnp.where(place[0] == 0, arrived[...].astype(F32), summed[...])
    normed, factor = normalize(block_input[0])
    grad_input[...] = (mid[...] + norm_back(normed, factor, total)).astype(BF)
    token[...] = jnp.zeros_like(token)


def join_kernel(first, second, third, fourth, late, joined):
    count = first.shape[0]
    near = (first[...].astype(F32) + second[...].astype(F32)) + (
        third[...].astype(F32) + fourth[...].astype(F32)
    )
    joined[:count] = near.astype(BF)
    joined[count:] = late[...]


def total_kernel(received, _, owned):
    owned[...] = jnp.sum(received[...].astype(F32), axis=0)


def shards(block_input, stream, grad_out, regions, qkv_weight, out_weight, up_weight, down_weight):
    rows, width = block_input.shape
    windows = rows // WIN
    head_count = lax.axis_size(HEAD_AXES)
    share_rows = rows // head_count
    head = lax.axis_index(HEAD_AXES)
    columns = qkv_weight.shape[2]
    count = lax.axis_size(WIN_AXES)
    head_place = head.astype(jnp.int32).reshape(1)
    x_place = lax.axis_index("x").astype(jnp.int32).reshape(1)
    chunk = (1, HALF, width)
    chunked = [array.reshape(-1, HALF, width) for array in (block_input, stream, grad_out)]
    chunks_in, chunks_mid, chunks_out = chunked
    turned_qkv = jnp.swapaxes(qkv_weight, 1, 2)

    def from_next(values):
        return lax.ppermute(values, WIN_AXES, [((i + 1) % count, i) for i in range(count)])

    far_input = from_next(block_input[:HALF])
    core_place = lax.axis_index("core").astype(jnp.int32).reshape(1)
    keep, give, late, early = mlp(core_place, stream, grad_out, up_weight, down_weight)
    late_sum = lax.psum_scatter(late, "x", scatter_dimension=0, tiled=True)
    taken = lax.ppermute(give, "core", [(0, 1), (1, 0)])
    (pair,) = call(
        pair_kernel,
        (1,),
        [whole(keep), whole(taken)],
        [(keep.shape, BF, whole(keep))],
        (keep, taken),
        vmem=16,
    )
    parts = lax.all_to_all(pair, "zl", 0, 0)
    labels = regions.reshape(windows, WIN)
    window = lambda columns: pl.BlockSpec((1, WIN, columns), lambda i, *_: (i, 0, 0))
    weights = (turned_qkv.reshape(-1, width), out_weight)
    token = jax.ShapeDtypeStruct((8, 128), F32)
    row_part = jax.ShapeDtypeStruct((share_rows, width), BF)
    mine = pl.BlockSpec(chunk, lambda i, place: (place[0], 0, 0))
    own_rows = jax.ShapeDtypeStruct((2, share_rows, width), BF)
    hidden, packed, probs, own = call(
        forward_kernel,
        (windows - 1,),
        [
            pl.BlockSpec(chunk, lambda i, _: (2 * i + 1, 0, 0)),
            pl.BlockSpec(chunk, lambda i, _: (2 * i + 2, 0, 0)),
            whole(labels),
            whole(weights[0]),
            mine,
            mine,
        ],
        [
            ((windows - 1, WIN, width), BF, window(width)),
            ((windows - 1, WIN, 4 * columns), BF, window(4 * columns)),
            ((windows - 1, WIN, WIN), F32, window(WIN)),
            (own_rows.shape, BF, whole(own_rows)),
        ],
        (chunks_in, chunks_in, labels, weights[0], chunks_mid, chunks_out),
        chosen=head_place,
        flops=53 * 10**8,
    )
    mid, own_grad_mid = call(
        middle_kernel,
        (1,),
        [whole(parts), whole(own)],
        [(row_part.shape, F32, whole(row_part)), (row_part.shape, BF, whole(row_part))],
        (parts, own),
        vmem=16,
    )
    far_grad = lax.ppermute(
        own_grad_mid,
        WIN_AXES + HEAD_AXES,
        [((i + 1) % count * head_count, i * head_count) for i in range(count)],
    )
    one = lambda columns: pl.BlockSpec((1, WIN, columns), lambda *_: (0, 0, 0))
    *last, done = call(
        last_forward_kernel,
        (1,),
        [
            pl.BlockSpec(chunk, lambda i: (head_count - 1, 0, 0)),
            whole(far_input),
            whole(labels),
            whole(weights[0]),
        ],
        [
            ((1, WIN, width), BF, one(width)),
            ((1, WIN, 4 * columns), BF, one(4 * columns)),
            ((1, WIN, WIN), F32, one(WIN)),
            (token.shape, F32, whole(token)),
        ],
        (chunks_in, far_input, labels, weights[0]),
        flops=20 * 10**8,
    )
    (given,) = call(
        give_kernel,
        (1,),
        [whole(own_grad_mid), whole(far_grad), ANY],
        [(row_part.shape, BF, whole(row_part))],
        (own_grad_mid, far_grad, done),
        chosen=head_place,
        vmem=16,
    )
    grad_mid = lax.all_gather(given, HEAD_AXES, axis=0)
    piece = jax.ShapeDtypeStruct((9,) + BLOCK, BF)
    in_rows = jax.ShapeDtypeStruct((head_count, HALF, width), BF)
    in_grad, *pieces = call(
        backward_kernel,
        (windows,),
        [
            pl.BlockSpec(chunk, lambda i, _: (2 * i + 1, 0, 0)),
            pl.BlockSpec(chunk, lambda i, _: (lax.rem(2 * i + 2, head_count), 0, 0)),
            *[
                pl.BlockSpec((1, WIN, size), lambda i, _: (jnp.minimum(i, windows - 2), 0, 0))
                for size in (width, 4 * columns, WIN)
            ],
            one(width),
            one(4 * columns),
            one(WIN),
            *[whole(weight) for weight in weights],
            whole(early),
            ANY,
        ],
        [(in_rows.shape, BF, whole(in_rows))] + [(piece.shape, BF, whole(piece))] * 4,
        (grad_mid, grad_mid, hidden, packed, probs, *last, *weights, early, late_sum),
        scratch=[
            pltpu.VMEM((width, 3 * columns), F32),
            pltpu.VMEM((columns, width), F32),
            pltpu.VMEM((3, width, columns), F32),
            pltpu.VMEM((8 * 32, 128), F32),
            pltpu.VMEM((4, 9) + BLOCK, BF),
        ],
        chosen=x_place,
        vmem=24,
        flops=70 * 10**8,
    )
    in_parts = lax.all_to_all(in_grad, HEAD_AXES, 0, 0)
    moved = [
        lax.ppermute(pieces[k], "x", [(i, (i + k) % 4) for i in range(4)]) for k in range(1, 4)
    ]
    joined = jax.ShapeDtypeStruct((24,) + BLOCK, BF)
    (partial_sum,) = call(
        join_kernel,
        (1,),
        [whole(piece)] * 4 + [whole(late_sum)],
        [(joined.shape, BF, whole(joined))],
        (pieces[0], *moved, late_sum),
        vmem=16,
    )
    summed, summed_b = call(
        sum_kernel,
        (1,),
        [whole(in_parts)],
        [(row_part.shape, F32, whole(row_part)), (row_part.shape, BF, whole(row_part))],
        (in_parts,),
        vmem=16,
    )
    arrived = lax.ppermute(
        summed_b,
        WIN_AXES + HEAD_AXES,
        [(i * head_count, (i + 1) % count * head_count) for i in range(count)],
    )
    received = lax.all_to_all(partial_sum, ("y", "zh"), 0, 0)
    grad_input, ready = call(
        final_kernel,
        (1,),
        [whole(summed), whole(arrived), whole(mid), mine],
        [(row_part.shape, BF, whole(row_part)), (token.shape, F32, whole(token))],
        (summed, arrived, mid, chunks_in),
        chosen=head_place,
        vmem=16,
    )
    owner_block = jax.ShapeDtypeStruct(BLOCK, F32)
    (owned,) = call(
        total_kernel,
        (1,),
        [whole(received), ANY],
        [(BLOCK, F32, whole(owner_block))],
        (received, ready),
        vmem=16,
    )
    return (grad_input, owned.reshape(1, -1))


def solution(mesh):
    fine = Mesh(mesh.devices.reshape(8, 4, 3, 4, 2), WIN_AXES + HEAD_AXES)
    return jax.shard_map(
        shards,
        mesh=fine,
        in_specs=(
            P(WIN_AXES, None),
            P(WIN_AXES, None),
            P(WIN_AXES, None),
            P(WIN_AXES),
            P(None, None, HEAD_AXES),
            P(HEAD_AXES, None),
            P(None, HEAD_AXES),
            P(HEAD_AXES, None),
        ),
        out_specs=(P(WIN_AXES + HEAD_AXES, None), P(HEAD_AXES, WIN_AXES)),
        check_vma=False,
    )
```

```python
import jax
import jax.numpy as jnp
from jax import lax
from jax.experimental import pallas as pl
from jax.experimental.pallas import tpu as pltpu
from jax.sharding import Mesh, PartitionSpec as P

HS = 64
WIN = 144
HALF = 72
WIN_AXES = ("y", "x", "zh")
HEAD_AXES = ("zl", "core")
BLOCK = (32, 128)
EPSILON = 1e-05
BF = jnp.bfloat16
F32 = jnp.float32


def normalize(values):
    data_f = values.astype(F32)
    centred = data_f - jnp.mean(data_f, axis=-1, keepdims=True)
    factor = lax.rsqrt(jnp.mean(centred * centred, axis=-1, keepdims=True) + EPSILON)
    return (centred * factor, factor)


def norm_back(normed, factor, upper):
    inner = upper - jnp.mean(upper, axis=-1, keepdims=True)
    return factor * (inner - normed * jnp.mean(upper * normed, axis=-1, keepdims=True))


def dot(left, right):
    return lax.dot_general(left, right, (((1,), (0,)), ((), ())), preferred_element_type=F32)


def contract_rows(left, right):
    return lax.dot_general(left, right, (((0,), (0,)), ((), ())), preferred_element_type=F32)


def contract_cols(left, right):
    return lax.dot_general(left, right, (((1,), (1,)), ((), ())), preferred_element_type=F32)


VMEM = pl.BlockSpec(memory_space=pltpu.VMEM)
SMEM = pl.BlockSpec(memory_space=pltpu.SMEM)
ANY = pl.BlockSpec(memory_space=pl.ANY)


def call(kernel, grid, ins, outs, args, scratch=(), chosen=None, flops=10**8, vmem=60, aliases=None):
    spec = pltpu.PrefetchScalarGridSpec(
        num_scalar_prefetch=0 if chosen is None else 1,
        grid=grid,
        in_specs=ins,
        out_specs=[out[2] for out in outs],
        scratch_shapes=list(scratch),
    )
    first = () if chosen is None else (chosen,)
    return pl.pallas_call(
        kernel,
        grid_spec=spec,
        out_shape=[jax.ShapeDtypeStruct(out[0], out[1]) for out in outs],
        input_output_aliases=aliases or {},
        compiler_params=pltpu.CompilerParams(vmem_limit_bytes=int(vmem * 2**20)),
        cost_estimate=pl.CostEstimate(flops=flops, bytes_accessed=2 * 2**20, transcendentals=0),
    )(*first, *args)


def whole(array):
    zeros = (0,) * len(array.shape)
    return pl.BlockSpec(array.shape, lambda *_: zeros)


def mlp_kernel(
    place, stream, grad_out, up_weight, down_weight, keep, give, late, early, up_sum, down_sum,
    rows_f32,
):
    step = pl.program_id(0)
    unit = normalize(stream[...])[0].astype(BF)
    pre = dot(unit, up_weight[...])
    upper = contract_cols(grad_out[...], down_weight[...])
    scale = 0.7978845608028654
    square = pre * pre
    bent = jnp.tanh(scale * (pre + 0.044715 * (square * pre)))
    slope = 0.5 * (1.0 + bent) + 0.5 * pre * (1.0 - bent * bent) * (
        scale * (1.0 + 3 * 0.044715 * square)
    )
    pre_grad = (upper * slope).astype(BF)
    act = (0.5 * pre * (1.0 + bent)).astype(BF)
    grad = contract_cols(pre_grad, up_weight[...])
    even = place[0] == 0
    keep[0] = jnp.where(even, grad[:HALF], grad[HALF:]).astype(BF)
    give[0] = jnp.where(even, grad[HALF:], grad[:HALF]).astype(BF)
    up_part = contract_rows(unit, pre_grad)
    down_part = contract_rows(act, grad_out[...])

    @pl.when(step == 0)
    def _():
        up_sum[...] = up_part
        down_sum[...] = down_part

    @pl.when(step > 0)
    def _():
        up_sum[...] += up_part
        down_sum[...] += down_part

    @pl.when(step == pl.num_programs(0) - 1)
    def _():
        base = 0
        for total in (up_sum, down_sum):
            rows, wide = total.shape[0], total.shape[1] // 128
            for column in range(wide):
                rows_f32[pl.ds(base + column, rows, stride=wide), :] = total[
                    :, 128 * column : 128 * column + 128
                ]
            base += rows * wide
        for owner in range(32, 96):
            block = rows_f32[32 * (owner - 32) : 32 * (owner - 31), :].astype(BF)
            if owner < 36:
                early[owner - 32] = block
            else:
                late[owner % 12 // 3, owner // 12 * 3 + owner % 3 - 9] = block


def mlp(place, stream, grad_out, up_weight, down_weight):
    rows, width = stream.shape
    units = up_weight.shape[1]
    part = lambda columns: pl.BlockSpec((WIN, columns), lambda i, _: (i, 0))
    late = jax.ShapeDtypeStruct((4, 15) + BLOCK, BF)
    early = jax.ShapeDtypeStruct((4,) + BLOCK, BF)
    return call(
        mlp_kernel,
        (rows // WIN,),
        [part(width), part(width), whole(up_weight), whole(down_weight)],
        [((rows // WIN, HALF, width), BF, pl.BlockSpec((1, HALF, width), lambda i, _: (i, 0, 0)))] * 2
        + [(late.shape, BF, whole(late)), (early.shape, BF, whole(early))],
        (stream, grad_out, up_weight, down_weight),
        scratch=[
            pltpu.VMEM((width, units), F32),
            pltpu.VMEM((units, width), F32),
            pltpu.VMEM((64 * 32, 128), F32),
        ],
        chosen=place,
        flops=69 * 10**8,
    )


def window_forward(lead, tail, row, turned_qkv):
    piece = jnp.concatenate([normalize(lead)[0], normalize(tail)[0]], axis=0)
    inputs = piece.astype(BF)
    query, key, value = [
        contract_cols(inputs, turned_qkv[HS * i : HS * i + HS, :]).astype(BF) for i in range(3)
    ]
    row = row.astype(F32)
    column = jnp.broadcast_to(row, (8, WIN)).T[:, :1]
    scores = contract_cols(query, key) * HS**-0.5
    kept = jnp.where(column == row, scores, -jnp.inf)
    raised = jnp.exp(kept - jnp.max(kept, axis=-1, keepdims=True))
    probs = raised / jnp.sum(raised, axis=-1, keepdims=True)
    attended = dot(probs.astype(BF), value).astype(BF)
    return inputs, (query, key, value, attended), probs


def forward_kernel(
    place, lead, tail, labels, turned_qkv, stream, grad_out, hidden, packed, probs_out, own
):
    row = labels[pl.ds(pl.program_id(0), 1), :]
    hidden[0], parts, probs_out[0] = window_forward(lead[0], tail[0], row, turned_qkv)
    packed[0] = jnp.concatenate(parts, axis=1)
    own[0] = stream[0]
    own[1] = grad_out[0]


def last_forward_kernel(
    lead, tail, labels, turned_qkv, hidden, packed, probs_out, token
):
    row = labels[labels.shape[0] - 1 :, :]
    hidden[0], parts, probs_out[0] = window_forward(lead[0], tail[...], row, turned_qkv)
    packed[0] = jnp.concatenate(parts, axis=1)
    token[...] = jnp.zeros_like(token)


def give_kernel(place, own, far, _, given):
    given[...] = jnp.where(place[0] == 0, far[...].astype(F32), own[...].astype(F32)).astype(BF)


def pair_kernel(keep, taken, _, __, pair, ___, ____):
    pair[...] = (keep[...].astype(F32) + taken[...].astype(F32)).astype(BF)


def middle_kernel(parts, own, _, mid, grad_mid, __):
    summed = jnp.sum(parts[...].astype(F32), axis=0)
    normed, factor = normalize(own[0])
    middle = own[1].astype(F32) + norm_back(normed, factor, summed)
    mid[...] = middle
    grad_mid[...] = middle.astype(BF)


def window_back(upper, hidden, parts, probs, turned_qkv, out_weight):
    query, key, value, attended = parts
    attended_grad = contract_cols(upper, out_weight[...]).astype(BF)
    out_grad = contract_rows(attended, upper)
    prob_grad = contract_cols(attended_grad, value)
    inner = prob_grad - jnp.sum(prob_grad * probs, axis=-1, keepdims=True)
    score_grad = (probs * inner * HS**-0.5).astype(BF)
    grads = jnp.concatenate(
        [
            dot(score_grad, key),
            contract_rows(score_grad, query),
            contract_rows(probs.astype(BF), attended_grad),
        ],
        axis=1,
    ).astype(BF)
    return dot(grads, turned_qkv[...]), contract_rows(hidden, grads), out_grad


def backward_kernel(
    place, lead, trail, hidden, packed, probs, last_hidden, last_packed, last_probs, turned_qkv,
    out_weight, early, in_grad, first, second, third, fourth, qkv_sum, out_sum, grads, outs, pieces,
):
    step = pl.program_id(0)
    last = step == pl.num_programs(0) - 1
    saved = jnp.where(last, last_packed[0].astype(F32), packed[0].astype(F32)).astype(BF)
    parts = [saved[:, HS * i : HS * i + HS] for i in range(4)]
    inputs = jnp.where(last, last_hidden[0].astype(F32), hidden[0].astype(F32)).astype(BF)
    upper = jnp.concatenate([lead[0].astype(F32), trail[0].astype(F32)], axis=0).astype(BF)
    rows, qkv_part, out_part = window_back(
        upper, inputs, parts, jnp.where(last, last_probs[0], probs[0]), turned_qkv, out_weight
    )
    in_grad[2 * step + 1] = rows[:HALF].astype(BF)
    in_grad[lax.rem(2 * step + 2, in_grad.shape[0])] = rows[HALF:].astype(BF)

    @pl.when(step == 0)
    def _():
        qkv_sum[...] = qkv_part
        out_sum[...] = out_part

    @pl.when(step > 0)
    def _():
        qkv_sum[...] += qkv_part
        out_sum[...] += out_part

    @pl.when(step == pl.num_programs(0) - 1)
    def _():
        for i in range(3):
            grads[i] = qkv_sum[:, HS * i : HS * i + HS]
        for column in range(out_sum.shape[1] // 128):
            outs[pl.ds(column, HS, stride=4), :] = out_sum[:, 128 * column : 128 * column + 128]
        slots = [lax.rem(x - place[0] + 4, 4) for x in range(4)]
        for owner in range(36):
            if owner < 24:
                kind, start = owner // 8, owner % 8 * 64
                even = grads[kind, pl.ds(start, 32, stride=2), :]
                odd = grads[kind, pl.ds(start + 1, 32, stride=2), :]
                block = jnp.concatenate([even, odd], axis=1).astype(BF)
            elif owner < 32:
                block = outs[32 * (owner - 24) : 32 * (owner - 23), :].astype(BF)
            else:
                block = early[owner - 32]
            pieces[slots[owner % 12 // 3], owner // 12 * 3 + owner % 3] = block
        for slot, out in enumerate((first, second, third, fourth)):
            out[...] = pieces[slot]


def sum_kernel(parts, total, total_b):
    total[...] = jnp.sum(parts[...].astype(F32), axis=0)
    total_b[...] = total[...].astype(BF)


def final_kernel(place, summed, arrived, mid, block_input, grad_input, token):
    total = jnp.where(place[0] == 0, arrived[...].astype(F32), summed[...])
    normed, factor = normalize(block_input[0])
    grad_input[...] = (mid[...] + norm_back(normed, factor, total)).astype(BF)
    token[...] = jnp.zeros_like(token)


def join_kernel(first, second, third, fourth, late, joined):
    count = first.shape[0]
    near = (first[...].astype(F32) + second[...].astype(F32)) + (
        third[...].astype(F32) + fourth[...].astype(F32)
    )
    joined[:count] = near.astype(BF)
    joined[count:] = jnp.sum(late[...].astype(F32), axis=0).astype(BF)


def total_kernel(received, _, owned):
    owned[...] = jnp.sum(received[...].astype(F32), axis=0)


def shards(block_input, stream, grad_out, regions, qkv_weight, out_weight, up_weight, down_weight):
    rows, width = block_input.shape
    windows = rows // WIN
    head_count = lax.axis_size(HEAD_AXES)
    share_rows = rows // head_count
    head = lax.axis_index(HEAD_AXES)
    columns = qkv_weight.shape[2]
    count = lax.axis_size(WIN_AXES)
    head_place = head.astype(jnp.int32).reshape(1)
    x_place = lax.axis_index("x").astype(jnp.int32).reshape(1)
    chunk = (1, HALF, width)
    chunked = [array.reshape(-1, HALF, width) for array in (block_input, stream, grad_out)]
    chunks_in, chunks_mid, chunks_out = chunked
    turned_qkv = jnp.swapaxes(qkv_weight, 1, 2)

    def from_next(values):
        return lax.ppermute(values, WIN_AXES, [((i + 1) % count, i) for i in range(count)])

    first_rows = chunks_in[0]
    labels = regions.reshape(windows, WIN)
    core_place = lax.axis_index("core").astype(jnp.int32).reshape(1)
    keep, give, late, early = mlp(core_place, stream, grad_out, up_weight, down_weight)
    taken = lax.ppermute(give, "core", [(0, 1), (1, 0)])
    pair, first_rows, labels = call(
        pair_kernel,
        (1,),
        [whole(keep), whole(taken), ANY, ANY],
        [
            (keep.shape, BF, whole(keep)),
            (first_rows.shape, BF, ANY),
            (labels.shape, labels.dtype, ANY),
        ],
        (keep, taken, first_rows, labels),
        aliases={2: 1, 3: 2},
        vmem=16,
    )
    far_input = from_next(first_rows)
    parts = lax.all_to_all(pair, "zl", 0, 0)
    window = lambda columns: pl.BlockSpec((1, WIN, columns), lambda i, *_: (i, 0, 0))
    weights = (turned_qkv.reshape(-1, width), out_weight)
    token = jax.ShapeDtypeStruct((8, 128), F32)
    row_part = jax.ShapeDtypeStruct((share_rows, width), BF)
    mine = pl.BlockSpec(chunk, lambda i, place: (place[0], 0, 0))
    own_rows = jax.ShapeDtypeStruct((2, share_rows, width), BF)
    hidden, packed, probs, own = call(
        forward_kernel,
        (windows - 1,),
        [
            pl.BlockSpec(chunk, lambda i, _: (2 * i + 1, 0, 0)),
            pl.BlockSpec(chunk, lambda i, _: (2 * i + 2, 0, 0)),
            whole(labels),
            whole(weights[0]),
            mine,
            mine,
        ],
        [
            ((windows - 1, WIN, width), BF, window(width)),
            ((windows - 1, WIN, 4 * columns), BF, window(4 * columns)),
            ((windows - 1, WIN, WIN), F32, window(WIN)),
            (own_rows.shape, BF, whole(own_rows)),
        ],
        (chunks_in, chunks_in, labels, weights[0], chunks_mid, chunks_out),
        chosen=head_place,
        flops=53 * 10**8,
    )
    mid, own_grad_mid, late = call(
        middle_kernel,
        (1,),
        [whole(parts), whole(own), ANY],
        [
            (row_part.shape, F32, whole(row_part)),
            (row_part.shape, BF, whole(row_part)),
            (late.shape, BF, ANY),
        ],
        (parts, own, late),
        aliases={2: 2},
        vmem=16,
    )
    far_grad = lax.ppermute(
        own_grad_mid,
        WIN_AXES + HEAD_AXES,
        [((i + 1) % count * head_count, i * head_count) for i in range(count)],
    )
    late_parts = lax.all_to_all(late, "x", 0, 0)
    one = lambda columns: pl.BlockSpec((1, WIN, columns), lambda *_: (0, 0, 0))
    *last, done = call(
        last_forward_kernel,
        (1,),
        [
            pl.BlockSpec(chunk, lambda i: (head_count - 1, 0, 0)),
            whole(far_input),
            whole(labels),
            whole(weights[0]),
        ],
        [
            ((1, WIN, width), BF, one(width)),
            ((1, WIN, 4 * columns), BF, one(4 * columns)),
            ((1, WIN, WIN), F32, one(WIN)),
            (token.shape, F32, whole(token)),
        ],
        (chunks_in, far_input, labels, weights[0]),
        flops=20 * 10**8,
    )
    (given,) = call(
        give_kernel,
        (1,),
        [whole(own_grad_mid), whole(far_grad), ANY],
        [(row_part.shape, BF, whole(row_part))],
        (own_grad_mid, far_grad, done),
        chosen=head_place,
        vmem=16,
    )
    grad_mid = lax.all_gather(given, HEAD_AXES, axis=0)
    piece = jax.ShapeDtypeStruct((9,) + BLOCK, BF)
    in_rows = jax.ShapeDtypeStruct((head_count, HALF, width), BF)
    in_grad, *pieces = call(
        backward_kernel,
        (windows,),
        [
            pl.BlockSpec(chunk, lambda i, _: (2 * i + 1, 0, 0)),
            pl.BlockSpec(chunk, lambda i, _: (lax.rem(2 * i + 2, head_count), 0, 0)),
            *[
                pl.BlockSpec((1, WIN, size), lambda i, _: (jnp.minimum(i, windows - 2), 0, 0))
                for size in (width, 4 * columns, WIN)
            ],
            one(width),
            one(4 * columns),
            one(WIN),
            *[whole(weight) for weight in weights],
            whole(early),
        ],
        [(in_rows.shape, BF, whole(in_rows))] + [(piece.shape, BF, whole(piece))] * 4,
        (grad_mid, grad_mid, hidden, packed, probs, *last, *weights, early),
        scratch=[
            pltpu.VMEM((width, 3 * columns), F32),
            pltpu.VMEM((columns, width), F32),
            pltpu.VMEM((3, width, columns), F32),
            pltpu.VMEM((8 * 32, 128), F32),
            pltpu.VMEM((4, 9) + BLOCK, BF),
        ],
        chosen=x_place,
        vmem=24,
        flops=70 * 10**8,
    )
    in_parts = lax.all_to_all(in_grad, HEAD_AXES, 0, 0)
    moved = [
        lax.ppermute(pieces[k], "x", [(i, (i + k) % 4) for i in range(4)]) for k in range(1, 4)
    ]
    joined = jax.ShapeDtypeStruct((24,) + BLOCK, BF)
    (partial_sum,) = call(
        join_kernel,
        (1,),
        [whole(piece)] * 4 + [whole(late_parts)],
        [(joined.shape, BF, whole(joined))],
        (pieces[0], *moved, late_parts),
        vmem=16,
    )
    summed, summed_b = call(
        sum_kernel,
        (1,),
        [whole(in_parts)],
        [(row_part.shape, F32, whole(row_part)), (row_part.shape, BF, whole(row_part))],
        (in_parts,),
        vmem=16,
    )
    arrived = lax.ppermute(
        summed_b,
        WIN_AXES + HEAD_AXES,
        [(i * head_count, (i + 1) % count * head_count) for i in range(count)],
    )
    received = lax.all_to_all(partial_sum, ("y", "zh"), 0, 0)
    grad_input, ready = call(
        final_kernel,
        (1,),
        [whole(summed), whole(arrived), whole(mid), mine],
        [(row_part.shape, BF, whole(row_part)), (token.shape, F32, whole(token))],
        (summed, arrived, mid, chunks_in),
        chosen=head_place,
        vmem=16,
    )
    owner_block = jax.ShapeDtypeStruct(BLOCK, F32)
    (owned,) = call(
        total_kernel,
        (1,),
        [whole(received), ANY],
        [(BLOCK, F32, whole(owner_block))],
        (received, ready),
        vmem=16,
    )
    return (grad_input, owned.reshape(1, -1))


def solution(mesh):
    fine = Mesh(mesh.devices.reshape(8, 4, 3, 4, 2), WIN_AXES + HEAD_AXES)
    return jax.shard_map(
        shards,
        mesh=fine,
        in_specs=(
            P(WIN_AXES, None),
            P(WIN_AXES, None),
            P(WIN_AXES, None),
            P(WIN_AXES),
            P(None, None, HEAD_AXES),
            P(HEAD_AXES, None),
            P(None, HEAD_AXES),
            P(HEAD_AXES, None),
        ),
        out_specs=(P(WIN_AXES + HEAD_AXES, None), P(HEAD_AXES, WIN_AXES)),
        check_vma=False,
    )
```

```python
import jax
import jax.numpy as jnp
from jax import lax
from jax.experimental import pallas as pl
from jax.experimental.pallas import tpu as pltpu
from jax.sharding import Mesh, PartitionSpec as P

HS = 64
WIN = 144
HALF = 72
WIN_AXES = ("y", "x", "zh")
HEAD_AXES = ("zl", "core")
BLOCK = (32, 128)
EPSILON = 1e-05
BF = jnp.bfloat16
F32 = jnp.float32


def normalize(values):
    data_f = values.astype(F32)
    centred = data_f - jnp.mean(data_f, axis=-1, keepdims=True)
    factor = lax.rsqrt(jnp.mean(centred * centred, axis=-1, keepdims=True) + EPSILON)
    return (centred * factor, factor)


def norm_back(normed, factor, upper):
    inner = upper - jnp.mean(upper, axis=-1, keepdims=True)
    return factor * (inner - normed * jnp.mean(upper * normed, axis=-1, keepdims=True))


def dot(left, right):
    return lax.dot_general(left, right, (((1,), (0,)), ((), ())), preferred_element_type=F32)


def contract_rows(left, right):
    return lax.dot_general(left, right, (((0,), (0,)), ((), ())), preferred_element_type=F32)


def contract_cols(left, right):
    return lax.dot_general(left, right, (((1,), (1,)), ((), ())), preferred_element_type=F32)


VMEM = pl.BlockSpec(memory_space=pltpu.VMEM)
SMEM = pl.BlockSpec(memory_space=pltpu.SMEM)
ANY = pl.BlockSpec(memory_space=pl.ANY)


def call(kernel, grid, ins, outs, args, scratch=(), chosen=None, flops=10**8, vmem=60, aliases=None):
    spec = pltpu.PrefetchScalarGridSpec(
        num_scalar_prefetch=0 if chosen is None else 1,
        grid=grid,
        in_specs=ins,
        out_specs=[out[2] for out in outs],
        scratch_shapes=list(scratch),
    )
    first = () if chosen is None else (chosen,)
    return pl.pallas_call(
        kernel,
        grid_spec=spec,
        out_shape=[jax.ShapeDtypeStruct(out[0], out[1]) for out in outs],
        input_output_aliases=aliases or {},
        compiler_params=pltpu.CompilerParams(vmem_limit_bytes=int(vmem * 2**20)),
        cost_estimate=pl.CostEstimate(flops=flops, bytes_accessed=2 * 2**20, transcendentals=0),
    )(*first, *args)


def whole(array):
    zeros = (0,) * len(array.shape)
    return pl.BlockSpec(array.shape, lambda *_: zeros)


def mlp_kernel(
    place, stream, grad_out, up_weight, down_weight, keep, give, late, early, up_sum, down_sum,
    rows_f32,
):
    step = pl.program_id(0)
    unit = normalize(stream[...])[0].astype(BF)
    pre = dot(unit, up_weight[...])
    upper = contract_cols(grad_out[...], down_weight[...])
    scale = 0.7978845608028654
    square = pre * pre
    bent = jnp.tanh(scale * (pre + 0.044715 * (square * pre)))
    slope = 0.5 * (1.0 + bent) + 0.5 * pre * (1.0 - bent * bent) * (
        scale * (1.0 + 3 * 0.044715 * square)
    )
    pre_grad = (upper * slope).astype(BF)
    act = (0.5 * pre * (1.0 + bent)).astype(BF)
    grad = contract_cols(pre_grad, up_weight[...])
    even = place[0] == 0
    keep[0] = jnp.where(even, grad[:HALF], grad[HALF:]).astype(BF)
    give[0] = jnp.where(even, grad[HALF:], grad[:HALF]).astype(BF)
    up_part = contract_rows(unit, pre_grad)
    down_part = contract_rows(act, grad_out[...])

    @pl.when(step == 0)
    def _():
        up_sum[...] = up_part
        down_sum[...] = down_part

    @pl.when(step > 0)
    def _():
        up_sum[...] += up_part
        down_sum[...] += down_part

    @pl.when(step == pl.num_programs(0) - 1)
    def _():
        base = 0
        for total in (up_sum, down_sum):
            rows, wide = total.shape[0], total.shape[1] // 128
            for column in range(wide):
                rows_f32[pl.ds(base + column, rows, stride=wide), :] = total[
                    :, 128 * column : 128 * column + 128
                ]
            base += rows * wide
        for owner in range(32, 96):
            block = rows_f32[32 * (owner - 32) : 32 * (owner - 31), :].astype(BF)
            if owner < 36:
                early[owner - 32] = block
            else:
                late[owner % 12 // 3, owner // 12 * 3 + owner % 3 - 9] = block


def mlp(place, stream, grad_out, up_weight, down_weight):
    rows, width = stream.shape
    units = up_weight.shape[1]
    part = lambda columns: pl.BlockSpec((WIN, columns), lambda i, _: (i, 0))
    late = jax.ShapeDtypeStruct((4, 15) + BLOCK, BF)
    early = jax.ShapeDtypeStruct((4,) + BLOCK, BF)
    return call(
        mlp_kernel,
        (rows // WIN,),
        [part(width), part(width), whole(up_weight), whole(down_weight)],
        [((rows // WIN, HALF, width), BF, pl.BlockSpec((1, HALF, width), lambda i, _: (i, 0, 0)))] * 2
        + [(late.shape, BF, whole(late)), (early.shape, BF, whole(early))],
        (stream, grad_out, up_weight, down_weight),
        scratch=[
            pltpu.VMEM((width, units), F32),
            pltpu.VMEM((units, width), F32),
            pltpu.VMEM((64 * 32, 128), F32),
        ],
        chosen=place,
        flops=69 * 10**8,
    )


def window_forward(lead, tail, row, turned_qkv):
    piece = jnp.concatenate([normalize(lead)[0], normalize(tail)[0]], axis=0)
    inputs = piece.astype(BF)
    query, key, value = [
        contract_cols(inputs, turned_qkv[HS * i : HS * i + HS, :]).astype(BF) for i in range(3)
    ]
    row = row.astype(F32)
    column = jnp.broadcast_to(row, (8, WIN)).T[:, :1]
    scores = contract_cols(query, key) * HS**-0.5
    kept = jnp.where(column == row, scores, -jnp.inf)
    raised = jnp.exp(kept - jnp.max(kept, axis=-1, keepdims=True))
    probs = raised / jnp.sum(raised, axis=-1, keepdims=True)
    attended = dot(probs.astype(BF), value).astype(BF)
    return inputs, (query, key, value, attended), probs


def forward_kernel(
    place, lead, tail, labels, turned_qkv, stream, grad_out, hidden, packed, probs_out, own
):
    row = labels[pl.ds(pl.program_id(0), 1), :]
    hidden[0], parts, probs_out[0] = window_forward(lead[0], tail[0], row, turned_qkv)
    packed[0] = jnp.concatenate(parts, axis=1)
    own[0] = stream[0]
    own[1] = grad_out[0]


def give_kernel(place, own, far, given):
    given[...] = jnp.where(place[0] == 0, far[...].astype(F32), own[...].astype(F32)).astype(BF)


def pair_kernel(keep, taken, _, pair, __):
    pair[...] = (keep[...].astype(F32) + taken[...].astype(F32)).astype(BF)


def middle_kernel(parts, own, _, __, mid, grad_mid, ___):
    summed = jnp.sum(parts[...].astype(F32), axis=0)
    normed, factor = normalize(own[0])
    middle = own[1].astype(F32) + norm_back(normed, factor, summed)
    mid[...] = middle
    grad_mid[...] = middle.astype(BF)


def window_back(upper, hidden, parts, probs, turned_qkv, out_weight):
    query, key, value, attended = parts
    attended_grad = contract_cols(upper, out_weight[...]).astype(BF)
    out_grad = contract_rows(attended, upper)
    prob_grad = contract_cols(attended_grad, value)
    inner = prob_grad - jnp.sum(prob_grad * probs, axis=-1, keepdims=True)
    score_grad = (probs * inner * HS**-0.5).astype(BF)
    grads = jnp.concatenate(
        [
            dot(score_grad, key),
            contract_rows(score_grad, query),
            contract_rows(probs.astype(BF), attended_grad),
        ],
        axis=1,
    ).astype(BF)
    return dot(grads, turned_qkv[...]), contract_rows(hidden, grads), out_grad


def backward_kernel(
    place, lead, trail, hidden, packed, probs, last_lead, last_tail, labels, turned_qkv, out_weight,
    early, in_grad, first, second, third, fourth, last_hidden, last_packed, last_probs, qkv_sum, out_sum, grads, outs, pieces,
):
    step = pl.program_id(0)
    last = step == pl.num_programs(0) - 1

    @pl.when(step == 0)
    def _():
        row = labels[labels.shape[0] - 1 :, :]
        last_hidden[...], kept, last_probs[...] = window_forward(
            last_lead[0], last_tail[...], row, turned_qkv
        )
        last_packed[...] = jnp.concatenate(kept, axis=1)

    saved = jnp.where(last, last_packed[...].astype(F32), packed[0].astype(F32)).astype(BF)
    parts = [saved[:, HS * i : HS * i + HS] for i in range(4)]
    inputs = jnp.where(last, last_hidden[...].astype(F32), hidden[0].astype(F32)).astype(BF)
    upper = jnp.concatenate([lead[0].astype(F32), trail[0].astype(F32)], axis=0).astype(BF)
    rows, qkv_part, out_part = window_back(
        upper, inputs, parts, jnp.where(last, last_probs[...], probs[0]), turned_qkv, out_weight
    )
    in_grad[2 * step + 1] = rows[:HALF].astype(BF)
    in_grad[lax.rem(2 * step + 2, in_grad.shape[0])] = rows[HALF:].astype(BF)

    @pl.when(step == 0)
    def _():
        qkv_sum[...] = qkv_part
        out_sum[...] = out_part

    @pl.when(step > 0)
    def _():
        qkv_sum[...] += qkv_part
        out_sum[...] += out_part

    @pl.when(step == pl.num_programs(0) - 1)
    def _():
        for i in range(3):
            grads[i] = qkv_sum[:, HS * i : HS * i + HS]
        for column in range(out_sum.shape[1] // 128):
            outs[pl.ds(column, HS, stride=4), :] = out_sum[:, 128 * column : 128 * column + 128]
        slots = [lax.rem(x - place[0] + 4, 4) for x in range(4)]
        for owner in range(36):
            if owner < 24:
                kind, start = owner // 8, owner % 8 * 64
                even = grads[kind, pl.ds(start, 32, stride=2), :]
                odd = grads[kind, pl.ds(start + 1, 32, stride=2), :]
                block = jnp.concatenate([even, odd], axis=1).astype(BF)
            elif owner < 32:
                block = outs[32 * (owner - 24) : 32 * (owner - 23), :].astype(BF)
            else:
                block = early[owner - 32]
            pieces[slots[owner % 12 // 3], owner // 12 * 3 + owner % 3] = block
        for slot, out in enumerate((first, second, third, fourth)):
            out[...] = pieces[slot]


def sum_kernel(parts, total, total_b):
    total[...] = jnp.sum(parts[...].astype(F32), axis=0)
    total_b[...] = total[...].astype(BF)


def final_kernel(place, summed, arrived, mid, block_input, grad_input):
    total = jnp.where(place[0] == 0, arrived[...].astype(F32), summed[...])
    normed, factor = normalize(block_input[0])
    grad_input[...] = (mid[...] + norm_back(normed, factor, total)).astype(BF)


def join_kernel(first, second, third, fourth, late, joined):
    count = first.shape[0]
    near = (first[...].astype(F32) + second[...].astype(F32)) + (
        third[...].astype(F32) + fourth[...].astype(F32)
    )
    joined[:count] = near.astype(BF)
    joined[count:] = jnp.sum(late[...].astype(F32), axis=0).astype(BF)


def total_kernel(received, owned):
    owned[...] = jnp.sum(received[...].astype(F32), axis=0)


def shards(block_input, stream, grad_out, regions, qkv_weight, out_weight, up_weight, down_weight):
    rows, width = block_input.shape
    windows = rows // WIN
    head_count = lax.axis_size(HEAD_AXES)
    share_rows = rows // head_count
    head = lax.axis_index(HEAD_AXES)
    columns = qkv_weight.shape[2]
    count = lax.axis_size(WIN_AXES)
    head_place = head.astype(jnp.int32).reshape(1)
    x_place = lax.axis_index("x").astype(jnp.int32).reshape(1)
    chunk = (1, HALF, width)
    chunked = [array.reshape(-1, HALF, width) for array in (block_input, stream, grad_out)]
    chunks_in, chunks_mid, chunks_out = chunked
    turned_qkv = jnp.swapaxes(qkv_weight, 1, 2)

    def from_next(values):
        return lax.ppermute(values, WIN_AXES, [((i + 1) % count, i) for i in range(count)])

    first_rows = chunks_in[0]
    labels = regions.reshape(windows, WIN)
    core_place = lax.axis_index("core").astype(jnp.int32).reshape(1)
    keep, give, late, early = mlp(core_place, stream, grad_out, up_weight, down_weight)
    taken = lax.ppermute(give, "core", [(0, 1), (1, 0)])
    pair, first_rows = call(
        pair_kernel,
        (1,),
        [whole(keep), whole(taken), ANY],
        [(keep.shape, BF, whole(keep)), (first_rows.shape, BF, ANY)],
        (keep, taken, first_rows),
        aliases={2: 1},
        vmem=16,
    )
    far_input = from_next(first_rows)
    parts = lax.all_to_all(pair, "zl", 0, 0)
    window = lambda columns: pl.BlockSpec((1, WIN, columns), lambda i, *_: (i, 0, 0))
    weights = (turned_qkv.reshape(-1, width), out_weight)
    row_part = jax.ShapeDtypeStruct((share_rows, width), BF)
    mine = pl.BlockSpec(chunk, lambda i, place: (place[0], 0, 0))
    own_rows = jax.ShapeDtypeStruct((2, share_rows, width), BF)
    hidden, packed, probs, own = call(
        forward_kernel,
        (windows - 1,),
        [
            pl.BlockSpec(chunk, lambda i, _: (2 * i + 1, 0, 0)),
            pl.BlockSpec(chunk, lambda i, _: (2 * i + 2, 0, 0)),
            whole(labels),
            whole(weights[0]),
            mine,
            mine,
        ],
        [
            ((windows - 1, WIN, width), BF, window(width)),
            ((windows - 1, WIN, 4 * columns), BF, window(4 * columns)),
            ((windows - 1, WIN, WIN), F32, window(WIN)),
            (own_rows.shape, BF, whole(own_rows)),
        ],
        (chunks_in, chunks_in, labels, weights[0], chunks_mid, chunks_out),
        chosen=head_place,
        flops=53 * 10**8,
    )
    mid, own_grad_mid, late = call(
        middle_kernel,
        (1,),
        [whole(parts), whole(own), ANY, ANY],
        [
            (row_part.shape, F32, whole(row_part)),
            (row_part.shape, BF, whole(row_part)),
            (late.shape, BF, ANY),
        ],
        (parts, own, late, far_input),
        aliases={2: 2},
        vmem=16,
    )
    far_grad = lax.ppermute(
        own_grad_mid,
        WIN_AXES + HEAD_AXES,
        [((i + 1) % count * head_count, i * head_count) for i in range(count)],
    )
    late_parts = lax.all_to_all(late, "x", 0, 0)
    (given,) = call(
        give_kernel,
        (1,),
        [whole(own_grad_mid), whole(far_grad)],
        [(row_part.shape, BF, whole(row_part))],
        (own_grad_mid, far_grad),
        chosen=head_place,
        vmem=16,
    )
    grad_mid = lax.all_gather(given, HEAD_AXES, axis=0)
    piece = jax.ShapeDtypeStruct((9,) + BLOCK, BF)
    in_rows = jax.ShapeDtypeStruct((head_count, HALF, width), BF)
    in_grad, *pieces = call(
        backward_kernel,
        (windows,),
        [
            pl.BlockSpec(chunk, lambda i, _: (2 * i + 1, 0, 0)),
            pl.BlockSpec(chunk, lambda i, _: (lax.rem(2 * i + 2, head_count), 0, 0)),
            *[
                pl.BlockSpec((1, WIN, size), lambda i, _: (jnp.minimum(i, windows - 2), 0, 0))
                for size in (width, 4 * columns, WIN)
            ],
            pl.BlockSpec(chunk, lambda i, _: (head_count - 1, 0, 0)),
            whole(far_input),
            whole(labels),
            *[whole(weight) for weight in weights],
            whole(early),
        ],
        [(in_rows.shape, BF, whole(in_rows))] + [(piece.shape, BF, whole(piece))] * 4,
        (grad_mid, grad_mid, hidden, packed, probs, chunks_in, far_input, labels, *weights, early),
        scratch=[
            pltpu.VMEM((WIN, width), BF),
            pltpu.VMEM((WIN, 4 * columns), BF),
            pltpu.VMEM((WIN, WIN), F32),
            pltpu.VMEM((width, 3 * columns), F32),
            pltpu.VMEM((columns, width), F32),
            pltpu.VMEM((3, width, columns), F32),
            pltpu.VMEM((8 * 32, 128), F32),
            pltpu.VMEM((4, 9) + BLOCK, BF),
        ],
        chosen=x_place,
        vmem=24,
        flops=70 * 10**8,
    )
    in_parts = lax.all_to_all(in_grad, HEAD_AXES, 0, 0)
    moved = [
        lax.ppermute(pieces[k], "x", [(i, (i + k) % 4) for i in range(4)]) for k in range(1, 4)
    ]
    joined = jax.ShapeDtypeStruct((24,) + BLOCK, BF)
    (partial_sum,) = call(
        join_kernel,
        (1,),
        [whole(piece)] * 4 + [whole(late_parts)],
        [(joined.shape, BF, whole(joined))],
        (pieces[0], *moved, late_parts),
        vmem=16,
    )
    summed, summed_b = call(
        sum_kernel,
        (1,),
        [whole(in_parts)],
        [(row_part.shape, F32, whole(row_part)), (row_part.shape, BF, whole(row_part))],
        (in_parts,),
        vmem=16,
    )
    arrived = lax.ppermute(
        summed_b,
        WIN_AXES + HEAD_AXES,
        [(i * head_count, (i + 1) % count * head_count) for i in range(count)],
    )
    received = lax.all_to_all(partial_sum, ("y", "zh"), 0, 0)
    (grad_input,) = call(
        final_kernel,
        (1,),
        [whole(summed), whole(arrived), whole(mid), mine],
        [(row_part.shape, BF, whole(row_part))],
        (summed, arrived, mid, chunks_in),
        chosen=head_place,
        vmem=16,
    )
    owner_block = jax.ShapeDtypeStruct(BLOCK, F32)
    (owned,) = call(
        total_kernel,
        (1,),
        [whole(received)],
        [(BLOCK, F32, whole(owner_block))],
        (received,),
        vmem=16,
    )
    return (grad_input, owned.reshape(1, -1))


def solution(mesh):
    fine = Mesh(mesh.devices.reshape(8, 4, 3, 4, 2), WIN_AXES + HEAD_AXES)
    return jax.shard_map(
        shards,
        mesh=fine,
        in_specs=(
            P(WIN_AXES, None),
            P(WIN_AXES, None),
            P(WIN_AXES, None),
            P(WIN_AXES),
            P(None, None, HEAD_AXES),
            P(HEAD_AXES, None),
            P(None, HEAD_AXES),
            P(HEAD_AXES, None),
        ),
        out_specs=(P(WIN_AXES + HEAD_AXES, None), P(HEAD_AXES, WIN_AXES)),
        check_vma=False,
    )
```

```python
import jax
import jax.numpy as jnp
from jax import lax
from jax.experimental import pallas as pl
from jax.experimental.pallas import tpu as pltpu
from jax.sharding import Mesh, PartitionSpec as P

HS = 64
WIN = 144
HALF = 72
WIN_AXES = ("y", "x", "zh")
HEAD_AXES = ("zl", "core")
BLOCK = (32, 128)
EPSILON = 1e-05
BF = jnp.bfloat16
F32 = jnp.float32


def normalize(values):
    data_f = values.astype(F32)
    centred = data_f - jnp.mean(data_f, axis=-1, keepdims=True)
    factor = lax.rsqrt(jnp.mean(centred * centred, axis=-1, keepdims=True) + EPSILON)
    return (centred * factor, factor)


def norm_back(normed, factor, upper):
    inner = upper - jnp.mean(upper, axis=-1, keepdims=True)
    return factor * (inner - normed * jnp.mean(upper * normed, axis=-1, keepdims=True))


def dot(left, right):
    return lax.dot_general(left, right, (((1,), (0,)), ((), ())), preferred_element_type=F32)


def contract_rows(left, right):
    return lax.dot_general(left, right, (((0,), (0,)), ((), ())), preferred_element_type=F32)


def contract_cols(left, right):
    return lax.dot_general(left, right, (((1,), (1,)), ((), ())), preferred_element_type=F32)


VMEM = pl.BlockSpec(memory_space=pltpu.VMEM)
SMEM = pl.BlockSpec(memory_space=pltpu.SMEM)
ANY = pl.BlockSpec(memory_space=pl.ANY)


def call(kernel, grid, ins, outs, args, scratch=(), chosen=None, flops=10**8, vmem=60, aliases=None):
    spec = pltpu.PrefetchScalarGridSpec(
        num_scalar_prefetch=0 if chosen is None else 1,
        grid=grid,
        in_specs=ins,
        out_specs=[out[2] for out in outs],
        scratch_shapes=list(scratch),
    )
    first = () if chosen is None else (chosen,)
    return pl.pallas_call(
        kernel,
        grid_spec=spec,
        out_shape=[jax.ShapeDtypeStruct(out[0], out[1]) for out in outs],
        input_output_aliases=aliases or {},
        compiler_params=pltpu.CompilerParams(vmem_limit_bytes=int(vmem * 2**20)),
        cost_estimate=pl.CostEstimate(flops=flops, bytes_accessed=2 * 2**20, transcendentals=0),
    )(*first, *args)


def whole(array):
    zeros = (0,) * len(array.shape)
    return pl.BlockSpec(array.shape, lambda *_: zeros)


def mlp_kernel(
    place, stream, grad_out, up_weight, down_weight, keep, give, late, early, up_sum, down_sum,
    rows_f32,
):
    step = pl.program_id(0)
    unit = normalize(stream[...])[0].astype(BF)
    pre = dot(unit, up_weight[...])
    upper = contract_cols(grad_out[...], down_weight[...])
    scale = 0.7978845608028654
    square = pre * pre
    bent = jnp.tanh(scale * (pre + 0.044715 * (square * pre)))
    slope = 0.5 * (1.0 + bent) + 0.5 * pre * (1.0 - bent * bent) * (
        scale * (1.0 + 3 * 0.044715 * square)
    )
    pre_grad = (upper * slope).astype(BF)
    act = (0.5 * pre * (1.0 + bent)).astype(BF)
    grad = contract_cols(pre_grad, up_weight[...])
    even = place[0] == 0
    keep[0] = jnp.where(even, grad[:HALF], grad[HALF:]).astype(BF)
    give[0] = jnp.where(even, grad[HALF:], grad[:HALF]).astype(BF)
    up_part = contract_rows(unit, pre_grad)
    down_part = contract_rows(act, grad_out[...])

    @pl.when(step == 0)
    def _():
        up_sum[...] = up_part
        down_sum[...] = down_part

    @pl.when(step > 0)
    def _():
        up_sum[...] += up_part
        down_sum[...] += down_part

    @pl.when(step == pl.num_programs(0) - 1)
    def _():
        base = 0
        for total in (up_sum, down_sum):
            rows, wide = total.shape[0], total.shape[1] // 128
            for column in range(wide):
                rows_f32[pl.ds(base + column, rows, stride=wide), :] = total[
                    :, 128 * column : 128 * column + 128
                ]
            base += rows * wide
        for owner in range(32, 96):
            block = rows_f32[32 * (owner - 32) : 32 * (owner - 31), :].astype(BF)
            if owner < 36:
                early[owner - 32] = block
            else:
                late[owner % 12 // 3, owner // 12 * 3 + owner % 3 - 9] = block


def mlp(place, stream, grad_out, up_weight, down_weight):
    rows, width = stream.shape
    units = up_weight.shape[1]
    part = lambda columns: pl.BlockSpec((WIN, columns), lambda i, _: (i, 0))
    late = jax.ShapeDtypeStruct((4, 15) + BLOCK, BF)
    early = jax.ShapeDtypeStruct((4,) + BLOCK, BF)
    return call(
        mlp_kernel,
        (rows // WIN,),
        [part(width), part(width), whole(up_weight), whole(down_weight)],
        [((rows // WIN, HALF, width), BF, pl.BlockSpec((1, HALF, width), lambda i, _: (i, 0, 0)))] * 2
        + [(late.shape, BF, whole(late)), (early.shape, BF, whole(early))],
        (stream, grad_out, up_weight, down_weight),
        scratch=[
            pltpu.VMEM((width, units), F32),
            pltpu.VMEM((units, width), F32),
            pltpu.VMEM((64 * 32, 128), F32),
        ],
        chosen=place,
        flops=69 * 10**8,
    )


def window_forward(lead, tail, row, turned_qkv):
    piece = jnp.concatenate([normalize(lead)[0], normalize(tail)[0]], axis=0)
    inputs = piece.astype(BF)
    query, key, value = [
        contract_cols(inputs, turned_qkv[HS * i : HS * i + HS, :]).astype(BF) for i in range(3)
    ]
    row = row.astype(F32)
    column = jnp.broadcast_to(row, (8, WIN)).T[:, :1]
    scores = contract_cols(query, key) * HS**-0.5
    kept = jnp.where(column == row, scores, -jnp.inf)
    raised = jnp.exp(kept - jnp.max(kept, axis=-1, keepdims=True))
    probs = raised / jnp.sum(raised, axis=-1, keepdims=True)
    attended = dot(probs.astype(BF), value).astype(BF)
    return inputs, (query, key, value, attended), probs


def forward_kernel(
    place, lead, tail, labels, turned_qkv, stream, grad_out, hidden, packed, probs_out, own
):
    row = labels[pl.ds(pl.program_id(0), 1), :]
    hidden[0], parts, probs_out[0] = window_forward(lead[0], tail[0], row, turned_qkv)
    packed[0] = jnp.concatenate(parts, axis=1)
    own[0] = stream[0]
    own[1] = grad_out[0]


def last_forward_kernel(
    lead, tail, labels, turned_qkv, hidden, packed, probs_out, token
):
    row = labels[labels.shape[0] - 1 :, :]
    hidden[0], parts, probs_out[0] = window_forward(lead[0], tail[...], row, turned_qkv)
    packed[0] = jnp.concatenate(parts, axis=1)
    token[...] = jnp.zeros_like(token)


def give_kernel(place, own, far, _, given):
    given[...] = jnp.where(place[0] == 0, far[...].astype(F32), own[...].astype(F32)).astype(BF)


def pair_kernel(keep, taken, _, pair, __):
    pair[...] = (keep[...].astype(F32) + taken[...].astype(F32)).astype(BF)


def middle_kernel(parts, own, _, mid, grad_mid, __):
    summed = jnp.sum(parts[...].astype(F32), axis=0)
    normed, factor = normalize(own[0])
    middle = own[1].astype(F32) + norm_back(normed, factor, summed)
    mid[...] = middle
    grad_mid[...] = middle.astype(BF)


def window_back(upper, hidden, parts, probs, turned_qkv, out_weight):
    query, key, value, attended = parts
    attended_grad = contract_cols(upper, out_weight[...]).astype(BF)
    out_grad = contract_rows(attended, upper)
    prob_grad = contract_cols(attended_grad, value)
    inner = prob_grad - jnp.sum(prob_grad * probs, axis=-1, keepdims=True)
    score_grad = (probs * inner * HS**-0.5).astype(BF)
    grads = jnp.concatenate(
        [
            dot(score_grad, key),
            contract_rows(score_grad, query),
            contract_rows(probs.astype(BF), attended_grad),
        ],
        axis=1,
    ).astype(BF)
    return dot(grads, turned_qkv[...]), contract_rows(hidden, grads), out_grad


def backward_kernel(
    place, lead, trail, hidden, packed, probs, last_hidden, last_packed, last_probs, turned_qkv,
    out_weight, early, in_grad, first, second, third, fourth, qkv_sum, out_sum, grads, outs, pieces,
):
    step = pl.program_id(0)
    last = step == pl.num_programs(0) - 1
    saved = jnp.where(last, last_packed[0].astype(F32), packed[0].astype(F32)).astype(BF)
    parts = [saved[:, HS * i : HS * i + HS] for i in range(4)]
    inputs = jnp.where(last, last_hidden[0].astype(F32), hidden[0].astype(F32)).astype(BF)
    upper = jnp.concatenate([lead[0].astype(F32), trail[0].astype(F32)], axis=0).astype(BF)
    rows, qkv_part, out_part = window_back(
        upper, inputs, parts, jnp.where(last, last_probs[0], probs[0]), turned_qkv, out_weight
    )
    in_grad[2 * step + 1] = rows[:HALF].astype(BF)
    in_grad[lax.rem(2 * step + 2, in_grad.shape[0])] = rows[HALF:].astype(BF)

    @pl.when(step == 0)
    def _():
        qkv_sum[...] = qkv_part
        out_sum[...] = out_part

    @pl.when(step > 0)
    def _():
        qkv_sum[...] += qkv_part
        out_sum[...] += out_part

    @pl.when(step == pl.num_programs(0) - 1)
    def _():
        for i in range(3):
            grads[i] = qkv_sum[:, HS * i : HS * i + HS]
        for column in range(out_sum.shape[1] // 128):
            outs[pl.ds(column, HS, stride=4), :] = out_sum[:, 128 * column : 128 * column + 128]
        slots = [lax.rem(x - place[0] + 4, 4) for x in range(4)]
        for owner in range(36):
            if owner < 24:
                kind, start = owner // 8, owner % 8 * 64
                even = grads[kind, pl.ds(start, 32, stride=2), :]
                odd = grads[kind, pl.ds(start + 1, 32, stride=2), :]
                block = jnp.concatenate([even, odd], axis=1).astype(BF)
            elif owner < 32:
                block = outs[32 * (owner - 24) : 32 * (owner - 23), :].astype(BF)
            else:
                block = early[owner - 32]
            pieces[slots[owner % 12 // 3], owner // 12 * 3 + owner % 3] = block
        for slot, out in enumerate((first, second, third, fourth)):
            out[...] = pieces[slot]


def sum_kernel(parts, total, total_b):
    total[...] = jnp.sum(parts[...].astype(F32), axis=0)
    total_b[...] = total[...].astype(BF)


def final_kernel(place, summed, arrived, mid, block_input, grad_input):
    total = jnp.where(place[0] == 0, arrived[...].astype(F32), summed[...])
    normed, factor = normalize(block_input[0])
    grad_input[...] = (mid[...] + norm_back(normed, factor, total)).astype(BF)


def join_kernel(first, second, third, fourth, late, joined):
    count = first.shape[0]
    near = (first[...].astype(F32) + second[...].astype(F32)) + (
        third[...].astype(F32) + fourth[...].astype(F32)
    )
    joined[:count] = near.astype(BF)
    joined[count:] = jnp.sum(late[...].astype(F32), axis=0).astype(BF)


def total_kernel(received, owned):
    owned[...] = jnp.sum(received[...].astype(F32), axis=0)


def shards(block_input, stream, grad_out, regions, qkv_weight, out_weight, up_weight, down_weight):
    rows, width = block_input.shape
    windows = rows // WIN
    head_count = lax.axis_size(HEAD_AXES)
    share_rows = rows // head_count
    head = lax.axis_index(HEAD_AXES)
    columns = qkv_weight.shape[2]
    count = lax.axis_size(WIN_AXES)
    head_place = head.astype(jnp.int32).reshape(1)
    x_place = lax.axis_index("x").astype(jnp.int32).reshape(1)
    chunk = (1, HALF, width)
    chunked = [array.reshape(-1, HALF, width) for array in (block_input, stream, grad_out)]
    chunks_in, chunks_mid, chunks_out = chunked
    turned_qkv = jnp.swapaxes(qkv_weight, 1, 2)

    def from_next(values):
        return lax.ppermute(values, WIN_AXES, [((i + 1) % count, i) for i in range(count)])

    first_rows = chunks_in[0]
    labels = regions.reshape(windows, WIN)
    core_place = lax.axis_index("core").astype(jnp.int32).reshape(1)
    keep, give, late, early = mlp(core_place, stream, grad_out, up_weight, down_weight)
    taken = lax.ppermute(give, "core", [(0, 1), (1, 0)])
    pair, first_rows = call(
        pair_kernel,
        (1,),
        [whole(keep), whole(taken), ANY],
        [(keep.shape, BF, whole(keep)), (first_rows.shape, BF, ANY)],
        (keep, taken, first_rows),
        aliases={2: 1},
        vmem=16,
    )
    far_input = from_next(first_rows)
    parts = lax.all_to_all(pair, "zl", 0, 0)
    window = lambda columns: pl.BlockSpec((1, WIN, columns), lambda i, *_: (i, 0, 0))
    weights = (turned_qkv.reshape(-1, width), out_weight)
    token = jax.ShapeDtypeStruct((8, 128), F32)
    row_part = jax.ShapeDtypeStruct((share_rows, width), BF)
    mine = pl.BlockSpec(chunk, lambda i, place: (place[0], 0, 0))
    own_rows = jax.ShapeDtypeStruct((2, share_rows, width), BF)
    hidden, packed, probs, own = call(
        forward_kernel,
        (windows - 1,),
        [
            pl.BlockSpec(chunk, lambda i, _: (2 * i + 1, 0, 0)),
            pl.BlockSpec(chunk, lambda i, _: (2 * i + 2, 0, 0)),
            whole(labels),
            whole(weights[0]),
            mine,
            mine,
        ],
        [
            ((windows - 1, WIN, width), BF, window(width)),
            ((windows - 1, WIN, 4 * columns), BF, window(4 * columns)),
            ((windows - 1, WIN, WIN), F32, window(WIN)),
            (own_rows.shape, BF, whole(own_rows)),
        ],
        (chunks_in, chunks_in, labels, weights[0], chunks_mid, chunks_out),
        chosen=head_place,
        flops=53 * 10**8,
    )
    mid, own_grad_mid, late = call(
        middle_kernel,
        (1,),
        [whole(parts), whole(own), ANY],
        [
            (row_part.shape, F32, whole(row_part)),
            (row_part.shape, BF, whole(row_part)),
            (late.shape, BF, ANY),
        ],
        (parts, own, late),
        aliases={2: 2},
        vmem=16,
    )
    far_grad = lax.ppermute(
        own_grad_mid,
        WIN_AXES + HEAD_AXES,
        [((i + 1) % count * head_count, i * head_count) for i in range(count)],
    )
    late_parts = lax.all_to_all(late, "x", 0, 0)
    one = lambda columns: pl.BlockSpec((1, WIN, columns), lambda *_: (0, 0, 0))
    *last, done = call(
        last_forward_kernel,
        (1,),
        [
            pl.BlockSpec(chunk, lambda i: (head_count - 1, 0, 0)),
            whole(far_input),
            whole(labels),
            whole(weights[0]),
        ],
        [
            ((1, WIN, width), BF, one(width)),
            ((1, WIN, 4 * columns), BF, one(4 * columns)),
            ((1, WIN, WIN), F32, one(WIN)),
            (token.shape, F32, whole(token)),
        ],
        (chunks_in, far_input, labels, weights[0]),
        flops=20 * 10**8,
    )
    (given,) = call(
        give_kernel,
        (1,),
        [whole(own_grad_mid), whole(far_grad), ANY],
        [(row_part.shape, BF, whole(row_part))],
        (own_grad_mid, far_grad, done),
        chosen=head_place,
        vmem=16,
    )
    grad_mid = lax.all_gather(given, HEAD_AXES, axis=0)
    piece = jax.ShapeDtypeStruct((9,) + BLOCK, BF)
    in_rows = jax.ShapeDtypeStruct((head_count, HALF, width), BF)
    in_grad, *pieces = call(
        backward_kernel,
        (windows,),
        [
            pl.BlockSpec(chunk, lambda i, _: (2 * i + 1, 0, 0)),
            pl.BlockSpec(chunk, lambda i, _: (lax.rem(2 * i + 2, head_count), 0, 0)),
            *[
                pl.BlockSpec((1, WIN, size), lambda i, _: (jnp.minimum(i, windows - 2), 0, 0))
                for size in (width, 4 * columns, WIN)
            ],
            one(width),
            one(4 * columns),
            one(WIN),
            *[whole(weight) for weight in weights],
            whole(early),
        ],
        [(in_rows.shape, BF, whole(in_rows))] + [(piece.shape, BF, whole(piece))] * 4,
        (grad_mid, grad_mid, hidden, packed, probs, *last, *weights, early),
        scratch=[
            pltpu.VMEM((width, 3 * columns), F32),
            pltpu.VMEM((columns, width), F32),
            pltpu.VMEM((3, width, columns), F32),
            pltpu.VMEM((8 * 32, 128), F32),
            pltpu.VMEM((4, 9) + BLOCK, BF),
        ],
        chosen=x_place,
        vmem=24,
        flops=70 * 10**8,
    )
    in_parts = lax.all_to_all(in_grad, HEAD_AXES, 0, 0)
    moved = [
        lax.ppermute(pieces[k], "x", [(i, (i + k) % 4) for i in range(4)]) for k in range(1, 4)
    ]
    joined = jax.ShapeDtypeStruct((24,) + BLOCK, BF)
    (partial_sum,) = call(
        join_kernel,
        (1,),
        [whole(piece)] * 4 + [whole(late_parts)],
        [(joined.shape, BF, whole(joined))],
        (pieces[0], *moved, late_parts),
        vmem=16,
    )
    summed, summed_b = call(
        sum_kernel,
        (1,),
        [whole(in_parts)],
        [(row_part.shape, F32, whole(row_part)), (row_part.shape, BF, whole(row_part))],
        (in_parts,),
        vmem=16,
    )
    arrived = lax.ppermute(
        summed_b,
        WIN_AXES + HEAD_AXES,
        [(i * head_count, (i + 1) % count * head_count) for i in range(count)],
    )
    received = lax.all_to_all(partial_sum, ("y", "zh"), 0, 0)
    (grad_input,) = call(
        final_kernel,
        (1,),
        [whole(summed), whole(arrived), whole(mid), mine],
        [(row_part.shape, BF, whole(row_part))],
        (summed, arrived, mid, chunks_in),
        chosen=head_place,
        vmem=16,
    )
    owner_block = jax.ShapeDtypeStruct(BLOCK, F32)
    (owned,) = call(
        total_kernel,
        (1,),
        [whole(received)],
        [(BLOCK, F32, whole(owner_block))],
        (received,),
        vmem=16,
    )
    return (grad_input, owned.reshape(1, -1))


def solution(mesh):
    fine = Mesh(mesh.devices.reshape(8, 4, 3, 4, 2), WIN_AXES + HEAD_AXES)
    return jax.shard_map(
        shards,
        mesh=fine,
        in_specs=(
            P(WIN_AXES, None),
            P(WIN_AXES, None),
            P(WIN_AXES, None),
            P(WIN_AXES),
            P(None, None, HEAD_AXES),
            P(HEAD_AXES, None),
            P(None, HEAD_AXES),
            P(HEAD_AXES, None),
        ),
        out_specs=(P(WIN_AXES + HEAD_AXES, None), P(HEAD_AXES, WIN_AXES)),
        check_vma=False,
    )
```
